128 devices in a mesh: seq: 2 (over x_lo), shard: 64 (over z, y, x_hi, core).
Axes of the slice: x: 4 (x_hi: 2, x_lo: 2; x = x_hi * 2 + x_lo), y: 4, z: 4, core: 2. Of those that a mesh axis runs over, the one named last changes fastest.
Arguments:
- tokens: bfloat16 [64, 2, 128, 768], P('shard', 'seq'), may hold values from -16 to 16
- cotangent: bfloat16 [64, 2, 128, 768], P('shard', 'seq'), may hold values from -6 to 6
- first_gain: bfloat16 [768], P('shard'), may hold values from 0.25 to 1.75
- first_offset: bfloat16 [768], P('shard'), may hold values from -1.75 to 1.75
- in_weight: bfloat16 [768, 2304], P('shard'), may hold values from -0.21875 to 0.21875
- query_bias: bfloat16 [768], P('shard'), may hold values from -1.75 to 1.75
- value_bias: bfloat16 [768], P('shard'), may hold values from -1.75 to 1.75
- out_weight: bfloat16 [768, 768], P('shard'), may hold values from -1.75 to 1.75
- out_bias: bfloat16 [768], P('shard'), may hold values from -1.75 to 1.75
- second_gain: bfloat16 [768], P('shard'), may hold values from 0.25 to 1.75
- second_offset: bfloat16 [768], P('shard'), may hold values from -1.75 to 1.75
- up_weight: bfloat16 [768, 3072], P('shard'), may hold values from -0.21875 to 0.21875
- up_bias: bfloat16 [3072], P('shard'), may hold values from -1.75 to 1.75
- down_weight: bfloat16 [3072, 768], P('shard'), may hold values from -0.109375 to 0.109375
- down_bias: bfloat16 [768], P('shard'), may hold values from -1.75 to 1.75
Outputs:
- layer_out: bfloat16 [64, 2, 128, 768], P('shard', 'seq')
- grad_tokens: bfloat16 [64, 2, 128, 768], P('shard', 'seq')
- grad_first_gain: float32 [768], P('shard')
- grad_first_offset: float32 [768], P('shard')
- grad_in_weight: float32 [768, 2304], P('shard')
- grad_query_bias: float32 [768], P('shard')
- grad_value_bias: float32 [768], P('shard')
- grad_out_weight: float32 [768, 768], P('shard')
- grad_out_bias: float32 [768], P('shard')
- grad_second_gain: float32 [768], P('shard')
- grad_second_offset: float32 [768], P('shard')
- grad_up_weight: float32 [768, 3072], P('shard')
- grad_up_bias: float32 [3072], P('shard')
- grad_down_weight: float32 [3072, 768], P('shard')
- grad_down_bias: float32 [768], P('shard')
The draws below stay inside these ranges and needn't reach their ends.
All inputs are finite; a program needn't handle non-finite values.
Results may differ from the reference program's by a relative error of at most 0.025.
Values may be sent and summed in bfloat16 or wider, within the bound.
No kernel may reach another device: no remote copies, remote signals or barrier semaphores. Data moves between devices by JAX's collectives and lax.ppermute only.
A program may use at most 128 MiB of HBM per device.

```python
import jax
import jax.numpy as jnp
from jax import lax

D = 768
H = 12
HEAD_DIM = 64
FF = 3072
TOK_DEV = 128
SEQ_LEN = 1024
SEQS = 16
BLOCKS = 64
N_SEQ = 2


def raised(values, stream_key, source, target, blocks, factor):
    def block_of(position):
        return (jnp.arange(values.shape[position]) // (values.shape[position] // blocks)).reshape((-1,) + (1,) * (values.ndim - 1 - position))

    first = jax.random.permutation(stream_key, blocks)[block_of(target)]
    second = (block_of(target) + blocks // 2) % blocks
    return jnp.where((block_of(source) == first) | (block_of(source) == second), factor * values, values)


def block_levels(stream_key, extent, shards, least, high):
    def one(axis_at, parts):
        steps = jax.random.uniform(jax.random.fold_in(jax.random.fold_in(stream_key, 6), axis_at), (parts,), jnp.float32, least / len(shards), high / len(shards))
        return jnp.repeat(jnp.exp(steps), extent[axis_at] // parts).reshape((-1,) + (1,) * (len(extent) - axis_at - 1))

    gain = one(*shards[0])
    for cut in shards[1:]:
        gain = gain * one(*cut)
    return gain


def centred(stream_key, dims, deviation, most, shards=(), kind=jnp.bfloat16):
    level = block_levels(stream_key, dims, shards, -0.22, 0.18) if shards else 1.0
    values = jax.random.normal(stream_key, dims, jnp.float32) * deviation * level
    return jnp.minimum(jnp.maximum(values, -most), most).astype(kind)


def bell_draw_with(rng, extent, scale, most, pieces, heavy, held_as=jnp.bfloat16):
    array = scale * jax.random.normal(rng, extent, jnp.float32)
    if pieces:
        array = array * block_levels(rng, extent, pieces, -0.22, 0.18)
    return jnp.clip(raised(array, jax.random.fold_in(rng, 3), *heavy), -most, most).astype(held_as)


def setup_inputs(seed: int = 0) -> dict:
    key_list = jax.random.split(jax.random.key(seed), 16)
    return {
        "tokens": bell_draw_with(key_list[0], (BLOCKS, N_SEQ, TOK_DEV, D), 1.0, 16.0, ((0, 64), (1, 2)), (0, 3, 64, 4.0)),
        "cotangent": centred(key_list[1], (BLOCKS, N_SEQ, TOK_DEV, D), 1.0, 6.0, ((0, 64), (1, 2))),
        "first_gain": jnp.clip(1.0 + 0.15 * jax.random.normal(key_list[2], (D,), jnp.float32), 0.25, 1.75).astype(jnp.bfloat16),
        "first_offset": centred(key_list[3], (D,), 0.3, 1.75, ((0, 64),)),
        "in_weight": centred(key_list[4], (D, 3 * D), D ** -0.5, 0.21875, ((0, 64),)),
        "query_bias": centred(key_list[5], (D,), 0.3, 1.75, ((0, 64),)),
        "value_bias": centred(key_list[6], (D,), 0.3, 1.75, ((0, 64),)),
        "out_weight": centred(key_list[7], (D, D), (D // 64) ** -0.5, 1.75, ((0, 64),)),
        "out_bias": centred(key_list[8], (D,), 0.3, 1.75, ((0, 64),)),
        "second_gain": jnp.clip(1.0 + 0.15 * jax.random.normal(key_list[9], (D,), jnp.float32), 0.25, 1.75).astype(jnp.bfloat16),
        "second_offset": centred(key_list[10], (D,), 0.3, 1.75, ((0, 64),)),
        "up_weight": centred(key_list[11], (D, FF), D ** -0.5, 0.21875, ((0, 64),)),
        "up_bias": centred(key_list[12], (FF,), 0.3, 1.75, ((0, 64),)),
        "down_weight": centred(key_list[13], (FF, D), FF ** -0.5, 0.109375, ((0, 64),)),
        "down_bias": centred(key_list[14], (D,), 0.3, 1.75, ((0, 64),)),
    }


@jax.custom_vjp
def low(v):
    return lax.optimization_barrier(v.astype(jnp.bfloat16)).astype(jnp.float32)

@jax.custom_vjp
def low_back(v):
    return v

def low_keep(v):
    return (low(v), None)

def low_pass(kept, grad):
    return (grad,)

def back_keep(v):
    return (v, None)

def back_low(kept, grad):
    return (low(grad),)
low.defvjp(low_keep, low_pass)
low_back.defvjp(back_keep, back_low)

def matmul(operand, matrix):
    return jnp.dot(operand, matrix, precision=lax.Precision.HIGHEST)

def gelu_tanh(inputs):
    return 0.5 * inputs * (1.0 + jnp.tanh(0.7978845608028654 * (inputs + 0.044715 * inputs * inputs * inputs)))

def layer_norm(values, norm_gain, offset):
    average = lax.optimization_barrier(jnp.mean(values, axis=-1, keepdims=True))
    centered = values - average
    variance = lax.optimization_barrier(jnp.mean(centered * centered, axis=-1, keepdims=True))
    return centered * lax.rsqrt(variance + 1e-05) * norm_gain + offset

def attend_sequence(queries, key_heads, value_heads):
    factor = HEAD_DIM ** (-0.5)
    scores = jnp.einsum('qhd,khd->hqk', queries, key_heads, precision=lax.Precision.HIGHEST) * factor
    length = queries.shape[0]
    causal = jnp.arange(length)[:, None] >= jnp.arange(length)[None, :]
    scores = low_back(jnp.where(causal[None], scores, -1e+30))
    highest = lax.optimization_barrier(jnp.max(scores, axis=-1, keepdims=True))
    exponent = jnp.exp(scores - highest)
    attention = low(exponent / lax.optimization_barrier(jnp.sum(exponent, axis=-1, keepdims=True)))
    return jnp.einsum('hqk,khd->qhd', attention, value_heads, precision=lax.Precision.HIGHEST)

def forward(hidden_in, params):
    gain_one, offset_one, weight_in, bias_query, bias_value, weight_out, bias_out, gain_two, offset_two, weight_up, bias_up, weight_down, bias_down = params
    normed = low(layer_norm(hidden_in, gain_one, offset_one))
    projected = matmul(normed, weight_in)
    queries = low(low_back(projected[:, :D] + bias_query))
    key_rows = low(low_back(projected[:, D:2 * D]))
    value_rows = low(low_back(projected[:, 2 * D:] + bias_value))
    head_shape = (SEQS, SEQ_LEN, H, HEAD_DIM)
    checked = jax.checkpoint(attend_sequence)
    attended = lax.map(lambda triple: checked(triple[0], triple[1], triple[2]), (queries.reshape(head_shape), key_rows.reshape(head_shape), value_rows.reshape(head_shape)))
    attended = low(low_back(attended.reshape(SEQS * SEQ_LEN, D)))
    branch = low_back(matmul(attended, weight_out) + bias_out)
    middle = hidden_in + branch
    normed_two = low(layer_norm(middle, gain_two, offset_two))
    pre_act = low_back(matmul(normed_two, weight_up) + bias_up)
    activated = low(gelu_tanh(pre_act))
    return middle + matmul(activated, weight_down) + bias_down

def reference(tokens, cotangent, first_gain, first_offset, in_weight, query_bias, value_bias, out_weight, out_bias, second_gain, second_offset, up_weight, up_bias, down_weight, down_bias):
    arrays = tuple((item.astype(jnp.float32) for item in (first_gain, first_offset, in_weight, query_bias, value_bias, out_weight, out_bias, second_gain, second_offset, up_weight, up_bias, down_weight, down_bias)))
    inputs = tokens.astype(jnp.float32).reshape(SEQS * SEQ_LEN, D)
    upstream = cotangent.astype(jnp.float32).reshape(SEQS * SEQ_LEN, D)
    result, pullback = jax.vjp(forward, inputs, arrays)
    grad_input, grads = pullback(upstream)
    return (result.astype(jnp.bfloat16).reshape(tokens.shape), grad_input.astype(jnp.bfloat16).reshape(tokens.shape), grads[0], grads[1], grads[2], grads[3], grads[4], grads[5], grads[6], grads[7], grads[8], grads[9], grads[10], grads[11], grads[12])
```

```python
import jax
import jax.numpy as jnp
from jax import lax
from jax.sharding import Mesh, PartitionSpec as P

HEAD_DIM = 64
HEADS = 12
WIDTH = 768
HIDDEN = 3072
TOK = 128
RING = ("xl", "xh")
CHIPS = ("xl", "z", "y", "xh")
SHARD = ("z", "y", "xh", "c")
SWAP = [(0, 1), (1, 0)]
F32 = jnp.float32
BF16 = jnp.bfloat16


def ring_index(place):
    return (place % 2) * 2 + place // 2


def ring_shift(value, steps):
    pairs = [(ring_index(i), ring_index((i + steps) % 4)) for i in range(4)]
    return lax.ppermute(value, RING, pairs)


def mirror(value):
    pairs = [(ring_index(i), ring_index(3 - i)) for i in range(4)]
    return lax.ppermute(value, RING, pairs)


def core_swap(value):
    return lax.ppermute(value, "c", SWAP)


def ordered(flag, own, other, axis):
    return jnp.where(
        flag == 0,
        jnp.concatenate([own, other], axis=axis),
        jnp.concatenate([other, own], axis=axis),
    )


def half_of(value, which, axis):
    size = value.shape[axis] // 2
    return lax.dynamic_slice_in_dim(value, which * size, size, axis)


def gelu_tanh(inputs):
    return (
        0.5
        * inputs
        * (1.0 + jnp.tanh(0.7978845608028654 * (inputs + 0.044715 * inputs * inputs * inputs)))
    )


def normed_of(values):
    average = jnp.mean(values, axis=-1, keepdims=True)
    centered = values - average
    inverse = lax.rsqrt(jnp.mean(centered * centered, axis=-1, keepdims=True) + 1e-05)
    return centered * inverse, inverse


def norm_backward(upstream, normed, inverse, norm_gain):
    scaled = upstream * norm_gain
    return inverse * (
        scaled
        - jnp.mean(scaled, axis=-1, keepdims=True)
        - normed * jnp.mean(scaled * normed, axis=-1, keepdims=True)
    )


def gather_tokens(own):
    ring = jnp.stack([own] + [ring_shift(own, steps) for steps in (1, 2, 3)])
    return jnp.concatenate([ring, core_swap(ring)])


def gather_weights(core, xh, pieces):
    in_weight, out_weight, up_weight, down_weight, vectors, up_bias = pieces
    wide = jnp.concatenate([in_weight, out_weight, up_weight], axis=1)
    small = jnp.concatenate(
        [jnp.stack(vectors, axis=1), up_bias.reshape(12, 4), jnp.zeros((12, 116), BF16)], axis=1
    )
    own = jnp.concatenate([half_of(wide, core, 1), small], axis=1)
    far = jnp.concatenate([half_of(wide, 1 - core, 1), small], axis=1)
    rows = ordered(core, own, core_swap(far), 0)
    rows = ordered(xh, rows, mirror(rows), 0)
    down = ordered(core, half_of(down_weight, core, 1), core_swap(half_of(down_weight, 1 - core, 1)), 0)
    down = ordered(xh, down, mirror(down), 0)
    packed = jnp.concatenate([rows] + [down[48 * k : 48 * k + 48] for k in range(4)], axis=1)
    full = lax.all_gather(packed, ("z", "y"), axis=0, tiled=True)
    wide_own = full[:, :3072]
    small = full[:, 3072:3084].astype(F32)
    down_own = full[:, 3200:]
    wide_other = core_swap(wide_own)
    down_other = core_swap(down_own)
    in_out = jnp.where(core == 0, wide_own, wide_other)
    up = jnp.where(core == 0, wide_other, wide_own)

    def rows_of(value):
        return value.reshape(16, 48, 4, 384).transpose(0, 2, 1, 3).reshape(HIDDEN, 384)

    down = ordered(core, rows_of(down_own), rows_of(down_other), 1)
    return in_out, up, down, small


def pair_halves(grad, core, axis):
    low = grad.astype(BF16)
    mine = half_of(grad, core, axis)
    return mine + core_swap(half_of(low, 1 - core, axis)).astype(F32)


def spread(blocks):
    got = lax.all_to_all(blocks.astype(BF16), CHIPS, 0, 0, tiled=True)
    return jnp.sum(got.astype(F32), axis=0)


def wide_blocks(grad):
    return grad.reshape(32, 24, 2, 2, 384).transpose(2, 0, 3, 1, 4).reshape(64, 48, 384)


def local(
    tokens,
    cotangent,
    first_gain,
    first_offset,
    in_weight,
    query_bias,
    value_bias,
    out_weight,
    out_bias,
    second_gain,
    second_offset,
    up_weight,
    up_bias,
    down_weight,
    down_bias,
):
    core = lax.axis_index("c")
    xh = lax.axis_index("xh")
    xl = lax.axis_index("xl")
    place = 2 * xh + xl
    own_tokens = tokens.reshape(TOK, WIDTH)
    group = gather_tokens(own_tokens).astype(F32).reshape(8 * TOK, WIDTH)
    vectors = (
        first_gain,
        first_offset,
        query_bias,
        value_bias,
        out_bias,
        second_gain,
        second_offset,
        down_bias,
    )
    in_out, weight_up, weight_down, small = gather_weights(
        core, xh, (in_weight, out_weight, up_weight, down_weight, vectors, up_bias)
    )
    gain_one, offset_one, bias_query, bias_value, bias_out, gain_two, offset_two, bias_down = (
        small[:, k] for k in range(8)
    )
    bias_up = small[:, 8:12].reshape(HIDDEN)
    weight_in = in_out[:, : 3 * WIDTH]
    weight_out = in_out[:, 3 * WIDTH :]

    blocks = []
    for other in (0, 1):
        for steps in range(4):
            there = (place + 4 - steps) % 4
            blocks.append(((there // 2) * 2 + (core + other) % 2) * 2 + there % 2)
    starts = jnp.stack(blocks) * TOK
    key_pos = (starts[:, None] + jnp.arange(TOK)[None]).reshape(-1)
    query_pos = starts[0] + jnp.arange(TOK)
    visible = key_pos[None, :] <= query_pos[:, None]

    unit_one, inverse_one = normed_of(group)
    normed_one = (unit_one * gain_one + offset_one).astype(BF16)
    own_normed = normed_one[:TOK]
    query = (
        jnp.dot(own_normed, weight_in[:, :WIDTH], preferred_element_type=F32) + bias_query
    ).astype(BF16)
    key_value = jnp.dot(normed_one, weight_in[:, WIDTH:], preferred_element_type=F32)
    key = key_value[:, :WIDTH].astype(BF16)
    value = (key_value[:, WIDTH:] + bias_value).astype(BF16)
    query_h = query.reshape(TOK, HEADS, HEAD_DIM)
    key_h = key.reshape(8 * TOK, HEADS, HEAD_DIM)
    value_h = value.reshape(8 * TOK, HEADS, HEAD_DIM)
    scores = jnp.einsum("qhd,khd->hqk", query_h, key_h, preferred_element_type=F32) * 0.125
    scores = jnp.where(visible[None], scores, -1e30)
    highest = jnp.max(scores, axis=-1, keepdims=True)
    exponent = jnp.exp(scores - highest)
    probs = exponent / jnp.sum(exponent, axis=-1, keepdims=True)
    probs_low = probs.astype(BF16)
    attended = jnp.einsum("hqk,khd->qhd", probs_low, value_h, preferred_element_type=F32)
    attended = attended.reshape(TOK, WIDTH).astype(BF16)
    own_float = own_tokens.astype(F32)
    middle = own_float + jnp.dot(attended, weight_out, preferred_element_type=F32) + bias_out
    unit_two, inverse_two = normed_of(middle)
    normed_two = (unit_two * gain_two + offset_two).astype(BF16)
    pre_act = jnp.dot(normed_two, weight_up, preferred_element_type=F32) + bias_up
    activated, gelu_pull = jax.vjp(gelu_tanh, pre_act)
    activated = activated.astype(BF16)
    result = middle + jnp.dot(activated, weight_down, preferred_element_type=F32) + bias_down

    upstream_low = cotangent.reshape(TOK, WIDTH)
    upstream = upstream_low.astype(F32)
    grad_down_bias = jnp.sum(upstream, axis=0)
    grad_down = jnp.einsum("tf,td->fd", activated, upstream_low, preferred_element_type=F32)
    grad_act = jnp.einsum("td,fd->tf", upstream_low, weight_down, preferred_element_type=F32)
    grad_pre_float = gelu_pull(grad_act)[0]
    grad_pre = grad_pre_float.astype(BF16)
    grad_up_bias = jnp.sum(grad_pre.astype(F32), axis=0)
    grad_up = jnp.einsum("td,tf->df", normed_two, grad_pre, preferred_element_type=F32)
    down_half = pair_halves(grad_down, core, 1)
    up_half = pair_halves(grad_up, core, 1)
    first_blocks = jnp.concatenate(
        [
            wide_blocks(up_half),
            down_half.reshape(32, 2, 2, 24, 384).transpose(2, 0, 1, 3, 4).reshape(64, 48, 384),
        ],
        axis=1,
    )
    first_sum = spread(first_blocks)

    grad_mid_norm = jnp.einsum("tf,df->td", grad_pre, weight_up, preferred_element_type=F32)
    grad_gain_two = jnp.sum(grad_mid_norm * unit_two, axis=0)
    grad_offset_two = jnp.sum(grad_mid_norm, axis=0)
    grad_middle = upstream + norm_backward(grad_mid_norm, unit_two, inverse_two, gain_two)
    grad_branch = grad_middle.astype(BF16)
    grad_out_bias = jnp.sum(grad_branch.astype(F32), axis=0)
    grad_out = jnp.einsum("td,te->de", attended, grad_branch, preferred_element_type=F32)
    grad_attended = jnp.einsum("te,de->td", grad_branch, weight_out, preferred_element_type=F32)
    grad_attended = grad_attended.astype(BF16).reshape(TOK, HEADS, HEAD_DIM)

    grad_probs = jnp.einsum("qhd,khd->hqk", grad_attended, value_h, preferred_element_type=F32)
    inner = jnp.sum(probs * grad_probs, axis=-1, keepdims=True)
    grad_scores = (probs * (grad_probs - inner)).astype(BF16)
    grad_query = (
        jnp.einsum("hqk,khd->qhd", grad_scores, key_h, preferred_element_type=F32) * 0.125
    )
    grad_query = grad_query.reshape(TOK, WIDTH).astype(BF16)
    grad_key = jnp.einsum("hqk,qhd->khd", grad_scores, query_h, preferred_element_type=F32) * 0.125
    grad_value = jnp.einsum("hqk,qhd->khd", probs_low, grad_attended, preferred_element_type=F32)
    grad_value = grad_value.reshape(8 * TOK, WIDTH)
    grad_kv = jnp.concatenate([grad_key.reshape(8 * TOK, WIDTH), grad_value], axis=1).astype(BF16)
    grad_query_bias = jnp.sum(grad_query.astype(F32), axis=0)
    grad_value_bias = jnp.sum(grad_value, axis=0)

    partial = jnp.einsum("tf,df->td", grad_kv, weight_in[:, WIDTH:], preferred_element_type=F32)
    partial = partial.reshape(8, TOK, WIDTH)
    ring = partial[:4] + core_swap(partial[4:].astype(BF16)).astype(F32)
    grad_normed = ring[0] + jnp.einsum(
        "tf,df->td", grad_query, weight_in[:, :WIDTH], preferred_element_type=F32
    )
    for steps in (1, 2, 3):
        grad_normed = grad_normed + ring_shift(ring[steps].astype(BF16), -steps).astype(F32)
    own_unit = unit_one[:TOK]
    grad_gain_one = jnp.sum(grad_normed * own_unit, axis=0)
    grad_offset_one = jnp.sum(grad_normed, axis=0)
    grad_input = grad_middle + norm_backward(grad_normed, own_unit, inverse_one[:TOK], gain_one)

    grad_in_q = jnp.einsum("td,tf->df", own_normed, grad_query, preferred_element_type=F32)
    grad_in_kv = jnp.einsum("td,tf->df", normed_one, grad_kv, preferred_element_type=F32)
    in_half = pair_halves(jnp.concatenate([grad_in_q, grad_in_kv, grad_out], axis=1), core, 1)
    second_sum = spread(wide_blocks(in_half))

    small_grads = jnp.stack(
        [
            grad_gain_one,
            grad_offset_one,
            grad_query_bias,
            grad_value_bias,
            grad_out_bias,
            grad_gain_two,
            grad_offset_two,
            grad_down_bias,
        ],
        axis=1,
    )
    small_grads = jnp.concatenate([small_grads, grad_up_bias.reshape(WIDTH, 4)], axis=1)
    small_grads = jnp.pad(small_grads.reshape(32, 2, 144), ((0, 0), (0, 6), (0, 112)))
    small_got = lax.all_to_all(jnp.concatenate([small_grads, small_grads]), CHIPS, 0, 0, tiled=True)
    small_sum = jnp.sum(small_got, axis=0)
    small_sum = small_sum + core_swap(small_sum)
    small_own = lax.dynamic_slice_in_dim(small_sum, core, 1, 0)[0, :144].reshape(12, 12)

    everything = jnp.concatenate([first_sum, second_sum])
    wide = jnp.concatenate([first_sum[:48], second_sum]).reshape(4, 2, 12, 384)
    down = first_sum[48:].reshape(2, 24, 384)
    wide_keep = half_of(wide, core, 1).reshape(48, 384)
    wide_send = half_of(wide, 1 - core, 1).reshape(48, 384)
    down_keep = half_of(down, core, 0).reshape(24, 384)
    down_send = half_of(down, 1 - core, 0).reshape(24, 384)
    keep = jnp.concatenate([wide_keep, down_keep]).astype(BF16)
    send = jnp.concatenate([wide_send, down_send]).astype(BF16)
    both = ordered(core, keep[None], core_swap(send)[None], 0)
    quad = ordered(xl, both[None], lax.ppermute(both[None], "xl", SWAP), 0).astype(F32)
    wide_own = quad[:, :, :48].reshape(2, 2, 2, 2, 12, 384)
    wide_own = wide_own.transpose(2, 4, 1, 0, 3, 5).reshape(2, 12, 3072)
    down_own = quad[:, :, 48:].transpose(0, 2, 1, 3).reshape(48, WIDTH)
    return (
        result.astype(BF16).reshape(tokens.shape),
        grad_input.astype(BF16).reshape(tokens.shape),
        small_own[:, 0],
        small_own[:, 1],
        wide_own[1][:, : 3 * WIDTH],
        small_own[:, 2],
        small_own[:, 3],
        wide_own[1][:, 3 * WIDTH :],
        small_own[:, 4],
        small_own[:, 5],
        small_own[:, 6],
        wide_own[0],
        small_own[:, 8:].reshape(48),
        down_own,
        small_own[:, 7],
    )


def solution(mesh):
    fine = Mesh(mesh.devices.reshape(2, 4, 4, 2, 2), ("xl", "z", "y", "xh", "c"))
    tok = P(SHARD, "xl", None, None)
    vec = P(SHARD)
    mat = P(SHARD, None)
    return jax.shard_map(
        local,
        mesh=fine,
        in_specs=(tok, tok, vec, vec, mat, vec, vec, mat, vec, vec, vec, mat, vec, mat, vec),
        out_specs=(tok, tok, vec, vec, mat, vec, vec, mat, vec, vec, vec, mat, vec, mat, vec),
        check_vma=False,
    )
```

```python
import jax
import jax.numpy as jnp
from jax import lax
from jax.experimental import pallas as pl
from jax.experimental.pallas import tpu as pltpu
from jax.sharding import Mesh, PartitionSpec as P

HEAD_DIM = 64
HEADS = 12
WIDTH = 768
HIDDEN = 3072
TOK = 128
RING = ("xl", "xh")
CHIPS = ("xl", "z", "y", "xh")
SHARD = ("z", "y", "xh", "c")
SWAP = [(0, 1), (1, 0)]
F32 = jnp.float32
BF16 = jnp.bfloat16


def ring_index(place):
    return (place % 2) * 2 + place // 2


def ring_shift(value, steps):
    pairs = [(ring_index(i), ring_index((i + steps) % 4)) for i in range(4)]
    return lax.ppermute(value, RING, pairs)


def mirror(value):
    pairs = [(ring_index(i), ring_index(3 - i)) for i in range(4)]
    return lax.ppermute(value, RING, pairs)


def core_swap(value):
    return lax.ppermute(value, "c", SWAP)


def ordered(flag, own, other, axis):
    return jnp.where(
        flag == 0,
        jnp.concatenate([own, other], axis=axis),
        jnp.concatenate([other, own], axis=axis),
    )


def half_of(value, which, axis):
    size = value.shape[axis] // 2
    return lax.dynamic_slice_in_dim(value, which * size, size, axis)


def normed_of(values):
    average = jnp.mean(values, axis=-1, keepdims=True)
    centered = values - average
    inverse = lax.rsqrt(jnp.mean(centered * centered, axis=-1, keepdims=True) + 1e-05)
    return centered * inverse, inverse


def norm_backward(upstream, normed, inverse, norm_gain):
    scaled = upstream * norm_gain
    return inverse * (
        scaled
        - jnp.mean(scaled, axis=-1, keepdims=True)
        - normed * jnp.mean(scaled * normed, axis=-1, keepdims=True)
    )


def gather_tokens(own):
    ring = jnp.stack([own] + [ring_shift(own, steps) for steps in (1, 2, 3)])
    return jnp.concatenate([ring, core_swap(ring)])


VMEM_LIMIT = 56 * 1024 * 1024


def dot(a, b, dims=((1,), (0,))):
    return lax.dot_general(a, b, (dims, ((), ())), preferred_element_type=F32)


ROWS = ((1,), (1,))


def call(kernel, outs, scratch, specs, args, flops, size):
    return pl.pallas_call(
        kernel,
        out_shape=[jax.ShapeDtypeStruct(shape, kind) for shape, kind in outs],
        in_specs=specs,
        scratch_shapes=scratch,
        compiler_params=pltpu.CompilerParams(vmem_limit_bytes=VMEM_LIMIT),
        cost_estimate=pl.CostEstimate(flops=flops, bytes_accessed=size, transcendentals=0),
    )(*args)


IN_VMEM = pl.BlockSpec(memory_space=pltpu.VMEM)
IN_SMEM = pl.BlockSpec(memory_space=pltpu.SMEM)
ANYWHERE = pl.BlockSpec(memory_space=pl.ANY)


def stacked_heads(pair):
    lane = lax.broadcasted_iota(jnp.int32, pair.shape, 1)
    zero = jnp.zeros_like(pair)
    return jnp.concatenate([jnp.where(lane < 64, pair, zero), jnp.where(lane < 64, zero, pair)])


def merged_heads(rows):
    lane = lax.broadcasted_iota(jnp.int32, (128, 128), 1)
    return jnp.where(lane < 64, rows[:128], rows[128:])


def front_kernel(
    meta, tok, vec, mine, other, h1, q, k, v, p, o, mid, weights, bias, sems
):
    core = meta[0]
    copies = []
    for b in range(2):
        cols = pl.ds(b * WIDTH, WIDTH)
        copies.append(pltpu.make_async_copy(mine.at[:, :, cols], weights.at[2 * core + b], sems.at[b]))
        copies.append(
            pltpu.make_async_copy(other.at[:, :, cols], weights.at[2 * (1 - core) + b], sems.at[2 + b])
        )
    for copy in copies:
        copy.start()
    for j in range(8):
        unit, _ = normed_of(tok[j].astype(F32))
        h1[j * TOK : (j + 1) * TOK, :] = (unit * vec[0:1, :] + vec[1:2, :]).astype(BF16)
    key_row = lax.broadcasted_iota(jnp.int32, (TOK, 2 * TOK), 0)
    query_col = lax.broadcasted_iota(jnp.int32, (TOK, 2 * TOK), 1) % TOK
    bias[0:TOK, :] = jnp.where(key_row <= query_col, 0.0, -1e30)
    for j in range(1, 8):
        shown = meta[j] > 0
        bias[j * TOK : (j + 1) * TOK, :] = jnp.full((TOK, 2 * TOK), jnp.where(shown, 0.0, -1e30), F32)
    for copy in copies:
        copy.wait()
    q[...] = (dot(h1[0:TOK, :], weights[0].reshape(WIDTH, WIDTH)) + vec[2:3, :]).astype(BF16)
    weight_key = weights[1].reshape(WIDTH, WIDTH)
    weight_value = weights[2].reshape(WIDTH, WIDTH)
    for j in range(4):
        rows = slice(j * 256, (j + 1) * 256)
        k[rows, :] = dot(h1[rows, :], weight_key).astype(BF16)
        v[rows, :] = (dot(h1[rows, :], weight_value) + vec[3:4, :]).astype(BF16)
    for pair in range(6):
        lanes = slice(pair * 128, (pair + 1) * 128)
        scores = dot(k[:, lanes], stacked_heads(q[:, lanes]), ROWS) * 0.125 + bias[...]
        exponent = jnp.exp(scores - jnp.max(scores, axis=0, keepdims=True))
        probs = exponent * (1.0 / jnp.sum(exponent, axis=0, keepdims=True))
        low = probs.astype(BF16)
        p[pair] = low
        attended = dot(v[:, lanes].T, low)
        o[:, lanes] = merged_heads(attended.T).astype(BF16)
    mid[...] = (
        tok[0].astype(F32) + dot(o[...], weights[3].reshape(WIDTH, WIDTH)) + vec[4:5, :]
    )


def middle_kernel(
    meta, mid, dy, vec, bias_up, mine, other_first, other_rest,
    result, act, du_keep, du_send, h2, dmid, da, dattended, small, up_bias_grad,
    up, down, weight_out, sems,
):
    core = meta[0]
    far = 1 - core
    copies = [
        pltpu.make_async_copy(mine.at[:, :, pl.ds(1536, 1536)], up.at[core], sems.at[0]),
        pltpu.make_async_copy(other_rest.at[:, :, pl.ds(0, 1536)], up.at[far], sems.at[1]),
    ]
    for g in range(4):
        copies.append(
            pltpu.make_async_copy(
                mine.at[:, :, pl.ds(3072 + 384 * g, 384)], down.at[core, :, g], sems.at[2 + g]
            )
        )
        copies.append(
            pltpu.make_async_copy(
                other_rest.at[:, :, pl.ds(1536 + 384 * g, 384)], down.at[far, :, g], sems.at[6 + g]
            )
        )
    for copy in copies:
        copy.start()

    @pl.when(core == 0)
    def _():
        copy = pltpu.make_async_copy(other_first.at[:, :, pl.ds(768, 768)], weight_out, sems.at[10])
        copy.start()
        copy.wait()

    @pl.when(core == 1)
    def _():
        copy = pltpu.make_async_copy(mine.at[:, :, pl.ds(768, 768)], weight_out, sems.at[10])
        copy.start()
        copy.wait()

    unit, inverse = normed_of(mid[...])
    h2[...] = (unit * vec[5:6, :] + vec[6:7, :]).astype(BF16)
    for copy in copies:
        copy.wait()
    low = dy[...]
    outcome = [mid[:, 384 * n : 384 * n + 384] + vec[7:8, 384 * n : 384 * n + 384] for n in range(2)]
    dh2 = None
    for half in range(2):
        cols = slice(half * 1536, (half + 1) * 1536)
        wide = up[half].reshape(WIDTH, 1536)
        u = dot(h2[...], wide) + bias_up[:, cols]
        cube = 0.7978845608028654 * (u + 0.044715 * u * u * u)
        tanh = jnp.tanh(cube)
        low_act = (0.5 * u * (1.0 + tanh)).astype(BF16)
        act[:, cols] = low_act
        slope_half = 0.5 * (1.0 + tanh) + 0.5 * u * (1.0 - tanh * tanh) * 0.7978845608028654 * (
            1.0 + 3.0 * 0.044715 * u * u
        )
        grad_act = None
        for n in range(2):
            rows = down[n, half * 8 : half * 8 + 8].reshape(1536, 384)
            outcome[n] = outcome[n] + dot(low_act, rows)
            term = dot(low[:, 384 * n : 384 * n + 384], rows, ROWS)
            grad_act = term if grad_act is None else grad_act + term
        du = (grad_act * slope_half).astype(BF16)
        up_bias_grad[:, cols] = jnp.sum(du.astype(F32), axis=0, keepdims=True)

        @pl.when(core == half)
        def _():
            du_keep[...] = du

        @pl.when(core != half)
        def _():
            du_send[...] = du

        term = dot(du, wide, ROWS)
        dh2 = term if dh2 is None else dh2 + term
    for n in range(2):
        result[:, 384 * n : 384 * n + 384] = outcome[n].astype(BF16)
    upstream = low.astype(F32)
    dm = upstream + norm_backward(dh2, unit, inverse, vec[5:6, :])
    dmid[...] = dm
    branch = dm.astype(BF16)
    da[...] = branch
    small[0:1, :] = jnp.sum(branch.astype(F32), axis=0, keepdims=True)
    small[1:2, :] = jnp.sum(dh2 * unit, axis=0, keepdims=True)
    small[2:3, :] = jnp.sum(dh2, axis=0, keepdims=True)
    small[3:4, :] = jnp.sum(upstream, axis=0, keepdims=True)
    dattended[...] = dot(branch, weight_out[...].reshape(WIDTH, WIDTH), ROWS).astype(BF16)


def attention_back_kernel(meta, q, k, v, p, do, dq, keep, send, value_bias):
    first = meta[0] == 0
    for pair in range(6):
        lanes = slice(pair * 128, (pair + 1) * 128)
        upstream = stacked_heads(do[:, lanes])
        keys = k[:, lanes]
        low = p[pair]
        probs = low.astype(F32)
        dprobs = dot(v[:, lanes], upstream, ROWS)
        inner = jnp.sum(probs * dprobs, axis=0, keepdims=True)
        dscores = (probs * (dprobs - inner)).astype(BF16)
        dk = dot(dscores, stacked_heads(q[:, lanes])) * 0.125
        dv = dot(low, upstream)
        dq[:, lanes] = (merged_heads(dot(keys.T, dscores).T) * 0.125).astype(BF16)
        value_bias[:, lanes] = jnp.sum(dv, axis=0, keepdims=True)
        keep[:, lanes] = jnp.where(first, dk, dv).astype(BF16)
        send[:, lanes] = jnp.where(first, dv, dk).astype(BF16)


def feed_grads_kernel(h2, h2_far, du, du_far, act, act_far, dy, dy_far, out):
    lhs = jnp.concatenate([h2[...], h2_far[...]]).T
    for x in range(4):
        cols = slice(x * 384, (x + 1) * 384)
        grad = dot(lhs, jnp.concatenate([du[:, cols], du_far[:, cols]])).astype(BF16)
        for zy in range(16):
            out[((x % 2) * 16 + zy) * 2 + x // 2, 0:48, :] = grad[zy * 48 : zy * 48 + 48]
    rhs = jnp.concatenate([dy[...], dy_far[...]])
    for part in range(4):
        cols = slice(part * 768, (part + 1) * 768)
        lhs = jnp.concatenate([act[:, cols], act_far[:, cols]]).T
        grad = dot(lhs, rhs).astype(BF16)
        for n in range(16):
            zy, x = part * 4 + n // 4, n % 4
            out[((x % 2) * 16 + zy) * 2 + x // 2, 48:96, :] = grad[n * 48 : n * 48 + 48]


def in_grads_kernel(
    meta, h1, keep, got, o, o_far, da, da_far, dq, dq_far, mine, other,
    out, ring, send, total, weight, weight_query, sems,
):
    core = meta[0]

    def load(source_q, source_kv):
        copies = [
            pltpu.make_async_copy(source_q.at[:, :, pl.ds(0, 768)], weight_query, sems.at[0]),
            source_kv,
        ]
        for copy in copies:
            copy.start()
        for copy in copies:
            copy.wait()

    @pl.when(core == 0)
    def _():
        load(mine, pltpu.make_async_copy(mine.at[:, :, pl.ds(768, 768)], weight, sems.at[1]))

    @pl.when(core == 1)
    def _():
        load(other, pltpu.make_async_copy(mine.at[:, :, pl.ds(0, 768)], weight, sems.at[1]))

    for j in range(8):
        there = (j + 4) % 8
        total[j * TOK : (j + 1) * TOK, :] = (
            keep[j * TOK : (j + 1) * TOK, :].astype(F32)
            + got[there * TOK : (there + 1) * TOK, :].astype(F32)
        ).astype(BF16)
    whole = weight[...].reshape(WIDTH, WIDTH)
    for j in range(8):
        grad = dot(total[j * TOK : (j + 1) * TOK, :], whole, ROWS)
        if j == 0:
            grad = grad + dot(dq[...], weight_query[...].reshape(WIDTH, WIDTH), ROWS)
        if j < 4:
            ring[j] = grad
        else:
            send[j - 4] = grad.astype(BF16)
    first = core == 0
    lhs = h1[...].T
    lhs_own = jnp.where(
        first,
        jnp.concatenate([h1[0:TOK, :], h1[4 * TOK : 5 * TOK, :]]).astype(F32),
        jnp.concatenate([o[...], o_far[...]]).astype(F32),
    ).astype(BF16).T
    rhs_own = jnp.where(
        first,
        jnp.concatenate([dq[...], dq_far[...]]).astype(F32),
        jnp.concatenate([da[...], da_far[...]]).astype(F32),
    ).astype(BF16)
    for b in range(2):
        cols = slice(b * 384, (b + 1) * 384)
        grad = dot(lhs, total[:, cols]).astype(BF16)
        grad_own = dot(lhs_own, rhs_own[:, cols]).astype(BF16)
        for zy in range(16):
            rows = slice(zy * 48, zy * 48 + 48)
            out[(b * 16 + zy) * 2 + 1 - core] = grad[rows]
            out[(b * 16 + zy) * 2 + core] = grad_own[rows]


def gather_weights(core, xh, pieces):
    in_weight, out_weight, up_weight, down_weight, vectors, up_bias = pieces
    first = jnp.concatenate([in_weight, out_weight], axis=1)
    small = jnp.concatenate(
        [jnp.stack(vectors, axis=1), up_bias.reshape(12, 4), jnp.zeros((12, 116), BF16)], axis=1
    )

    def part(which):
        return jnp.concatenate([half_of(first, which, 1), half_of(up_weight, which, 1), small], axis=1)

    rows = ordered(core, part(core), core_swap(part(1 - core)), 0)
    rows = ordered(xh, rows, mirror(rows), 0)
    down = ordered(core, half_of(down_weight, core, 1), core_swap(half_of(down_weight, 1 - core, 1)), 0)
    down = ordered(xh, down, mirror(down), 0)
    packed = jnp.concatenate(
        [rows[:, :3072]] + [down[48 * k : 48 * k + 48] for k in range(4)] + [rows[:, 3072:]], axis=1
    )
    return lax.all_gather(packed, ("z", "y"), axis=0)


def spread(blocks):
    got = lax.all_to_all(blocks, CHIPS, 0, 0, tiled=True)
    return jnp.sum(got.astype(F32), axis=0)


def local(
    tokens,
    cotangent,
    first_gain,
    first_offset,
    in_weight,
    query_bias,
    value_bias,
    out_weight,
    out_bias,
    second_gain,
    second_offset,
    up_weight,
    up_bias,
    down_weight,
    down_bias,
):
    core = lax.axis_index("c")
    xh = lax.axis_index("xh")
    xl = lax.axis_index("xl")
    place = 2 * xh + xl
    own_tokens = tokens.reshape(TOK, WIDTH)
    group = gather_tokens(own_tokens)
    upstream = cotangent.reshape(TOK, WIDTH)
    upstream_half = half_of(upstream, core, 1)
    upstream_far = core_swap(half_of(upstream, 1 - core, 1))
    vectors = (
        first_gain,
        first_offset,
        query_bias,
        value_bias,
        out_bias,
        second_gain,
        second_offset,
        down_bias,
    )
    mine = gather_weights(core, xh, (in_weight, out_weight, up_weight, down_weight, vectors, up_bias))
    other_first = core_swap(mine[:, :, :1536])
    other_rest = core_swap(mine[:, :, 1536:4608])
    small = mine[:, :, 4608:4620].reshape(WIDTH, 12).astype(F32)
    vec = small[:, :8].T
    bias_up = small[:, 8:].reshape(1, HIDDEN)

    blocks = []
    for other in (0, 1):
        for steps in range(4):
            there = (place + 4 - steps) % 4
            blocks.append(((there // 2) * 2 + (core + other) % 2) * 2 + there % 2)
    meta = jnp.stack([core] + [(b < blocks[0]).astype(jnp.int32) for b in blocks[1:]])

    wide = (16, 48, WIDTH)
    h1, query, key, value, probs, attended, middle = call(
        front_kernel,
        [
            ((8 * TOK, WIDTH), BF16),
            ((TOK, WIDTH), BF16),
            ((8 * TOK, WIDTH), BF16),
            ((8 * TOK, WIDTH), BF16),
            ((6, 8 * TOK, 2 * TOK), BF16),
            ((TOK, WIDTH), BF16),
            ((TOK, WIDTH), F32),
        ],
        [
            pltpu.VMEM((4,) + wide, BF16),
            pltpu.VMEM((8 * TOK, 2 * TOK), F32),
            pltpu.SemaphoreType.DMA((4,)),
        ],
        [IN_SMEM, IN_VMEM, IN_VMEM, ANYWHERE, ANYWHERE],
        (meta, group, vec, mine, other_first),
        4_000_000_000,
        20_000_000,
    )
    (
        result,
        act,
        du_keep,
        du_send,
        h2,
        grad_middle,
        da,
        grad_attended,
        small_middle,
        grad_up_bias,
    ) = call(
        middle_kernel,
        [
            ((TOK, WIDTH), BF16),
            ((TOK, HIDDEN), BF16),
            ((TOK, HIDDEN // 2), BF16),
            ((TOK, HIDDEN // 2), BF16),
            ((TOK, WIDTH), BF16),
            ((TOK, WIDTH), F32),
            ((TOK, WIDTH), BF16),
            ((TOK, WIDTH), BF16),
            ((8, WIDTH), F32),
            ((1, HIDDEN), F32),
        ],
        [
            pltpu.VMEM((2, 16, 48, 1536), BF16),
            pltpu.VMEM((2, 16, 4, 48, 384), BF16),
            pltpu.VMEM(wide, BF16),
            pltpu.SemaphoreType.DMA((11,)),
        ],
        [IN_SMEM] + [IN_VMEM] * 4 + [ANYWHERE] * 3,
        (meta, middle, upstream, vec, bias_up, mine, other_first, other_rest),
        3_000_000_000,
        20_000_000,
    )
    act_far = core_swap(act)
    du_far = core_swap(du_send)
    rows_far = core_swap(jnp.concatenate([h2, attended, da]))
    (first_blocks,) = call(
        feed_grads_kernel,
        [((64, 96, 384), BF16)],
        [],
        [IN_VMEM] * 8,
        (h2, rows_far[:TOK], du_keep, du_far, act, act_far, upstream_half, upstream_far),
        2_000_000_000,
        10_000_000,
    )
    first_sum = spread(first_blocks)

    grad_query, keep, send, grad_value_bias = call(
        attention_back_kernel,
        [
            ((TOK, WIDTH), BF16),
            ((8 * TOK, WIDTH), BF16),
            ((8 * TOK, WIDTH), BF16),
            ((1, WIDTH), F32),
        ],
        [],
        [IN_SMEM] + [IN_VMEM] * 5,
        (meta, query, key, value, probs, grad_attended),
        3_000_000_000,
        20_000_000,
    )
    got = core_swap(send)
    query_far = core_swap(grad_query)
    second_blocks, ring, ring_send = call(
        in_grads_kernel,
        [
            ((64, 48, 384), BF16),
            ((4, TOK, WIDTH), F32),
            ((4, TOK, WIDTH), BF16),
        ],
        [
            pltpu.VMEM((8 * TOK, WIDTH), BF16),
            pltpu.VMEM(wide, BF16),
            pltpu.VMEM(wide, BF16),
            pltpu.SemaphoreType.DMA((2,)),
        ],
        [IN_SMEM] + [IN_VMEM] * 9 + [ANYWHERE] * 2,
        (
            meta,
            h1,
            keep,
            got,
            attended,
            rows_far[TOK : 2 * TOK],
            da,
            rows_far[2 * TOK :],
            grad_query,
            query_far,
            mine,
            other_first,
        ),
        3_000_000_000,
        20_000_000,
    )
    second_sum = spread(second_blocks)

    ring = ring + core_swap(ring_send).astype(F32)
    grad_normed = ring[0]
    for steps in (1, 2, 3):
        grad_normed = grad_normed + ring_shift(ring[steps].astype(BF16), -steps).astype(F32)
    unit_one, inverse_one = normed_of(own_tokens.astype(F32))
    grad_input = grad_middle + norm_backward(grad_normed, unit_one, inverse_one, vec[0])

    small_grads = jnp.stack(
        [
            jnp.sum(grad_normed * unit_one, axis=0),
            jnp.sum(grad_normed, axis=0),
            jnp.sum(grad_query.astype(F32), axis=0),
            grad_value_bias[0],
            small_middle[0],
            small_middle[1],
            small_middle[2],
            small_middle[3],
        ],
        axis=1,
    )
    small_grads = jnp.concatenate([small_grads, grad_up_bias.reshape(WIDTH, 4)], axis=1)
    small_grads = jnp.pad(small_grads.reshape(32, 2, 144), ((0, 0), (0, 6), (0, 112)))
    small_got = lax.all_to_all(jnp.concatenate([small_grads, small_grads]), CHIPS, 0, 0, tiled=True)
    small_sum = jnp.sum(small_got, axis=0)
    small_sum = small_sum + core_swap(small_sum)
    small_own = lax.dynamic_slice_in_dim(small_sum, core, 1, 0)[0, :144].reshape(12, 12)

    down_sum = first_sum[48:].astype(BF16)
    down_own = ordered(core, down_sum, core_swap(down_sum), 1)
    down_own = jnp.where(xl == core, down_own, lax.ppermute(down_own, "xl", SWAP)).astype(F32)
    sums = jnp.stack([first_sum[:48], second_sum]).astype(BF16)

    def rows_for(steps):
        there = ((place + steps) % 4) // 2
        return lax.dynamic_slice_in_dim(sums, there * 24, 24, 1)

    parts = jnp.stack([rows_for(0)] + [ring_shift(rows_for(steps), steps) for steps in (1, 2, 3)])
    parts = jnp.stack([parts[(place + 4 - source) % 4] for source in range(4)])
    parts = parts.reshape(4, 2, 2, 12, 384)
    keep_rows = lax.dynamic_index_in_dim(parts, core, 2, keepdims=False)
    send_rows = lax.dynamic_index_in_dim(parts, 1 - core, 2, keepdims=False)
    both = ordered(core, keep_rows[None], core_swap(send_rows)[None], 0)
    wide_own = both.transpose(2, 3, 0, 1, 4).reshape(2, 12, 3072).astype(F32)
    return (
        result.reshape(tokens.shape),
        grad_input.astype(BF16).reshape(tokens.shape),
        small_own[:, 0],
        small_own[:, 1],
        wide_own[1][:, : 3 * WIDTH],
        small_own[:, 2],
        small_own[:, 3],
        wide_own[1][:, 3 * WIDTH :],
        small_own[:, 4],
        small_own[:, 5],
        small_own[:, 6],
        wide_own[0],
        small_own[:, 8:].reshape(48),
        down_own,
        small_own[:, 7],
    )


def solution(mesh):
    fine = Mesh(mesh.devices.reshape(2, 4, 4, 2, 2), ("xl", "z", "y", "xh", "c"))
    tok = P(SHARD, "xl", None, None)
    vec = P(SHARD)
    mat = P(SHARD, None)
    return jax.shard_map(
        local,
        mesh=fine,
        in_specs=(tok, tok, vec, vec, mat, vec, vec, mat, vec, vec, vec, mat, vec, mat, vec),
        out_specs=(tok, tok, vec, vec, mat, vec, vec, mat, vec, vec, vec, mat, vec, mat, vec),
        check_vma=False,
    )
```

```python
import jax
import jax.numpy as jnp
from jax import lax
from jax.experimental import pallas as pl
from jax.experimental.pallas import tpu as pltpu
from jax.sharding import Mesh, PartitionSpec as P

HEAD_DIM = 64
HEADS = 12
WIDTH = 768
HIDDEN = 3072
TOK = 128
RING = ("xl", "xh")
CHIPS = ("xl", "z", "y", "xh")
SHARD = ("z", "y", "xh", "c")
SWAP = [(0, 1), (1, 0)]
F32 = jnp.float32
BF16 = jnp.bfloat16


def ring_index(place):
    return (place % 2) * 2 + place // 2


def ring_shift(value, steps):
    pairs = [(ring_index(i), ring_index((i + steps) % 4)) for i in range(4)]
    return lax.ppermute(value, RING, pairs)


def mirror(value):
    pairs = [(ring_index(i), ring_index(3 - i)) for i in range(4)]
    return lax.ppermute(value, RING, pairs)


def core_swap(value):
    return lax.ppermute(value, "c", SWAP)


def ordered(flag, own, other, axis):
    return jnp.where(
        flag == 0,
        jnp.concatenate([own, other], axis=axis),
        jnp.concatenate([other, own], axis=axis),
    )


def half_of(value, which, axis):
    size = value.shape[axis] // 2
    return lax.dynamic_slice_in_dim(value, which * size, size, axis)


def normed_of(values):
    average = jnp.mean(values, axis=-1, keepdims=True)
    centered = values - average
    inverse = lax.rsqrt(jnp.mean(centered * centered, axis=-1, keepdims=True) + 1e-05)
    return centered * inverse, inverse


def norm_backward(upstream, normed, inverse, norm_gain):
    scaled = upstream * norm_gain
    return inverse * (
        scaled
        - jnp.mean(scaled, axis=-1, keepdims=True)
        - normed * jnp.mean(scaled * normed, axis=-1, keepdims=True)
    )


def gather_tokens(own):
    ring = jnp.stack([own] + [ring_shift(own, steps) for steps in (1, 2, 3)])
    return jnp.concatenate([ring, core_swap(ring)])


VMEM_LIMIT = 56 * 1024 * 1024


def dot(a, b, dims=((1,), (0,))):
    return lax.dot_general(a, b, (dims, ((), ())), preferred_element_type=F32)


ROWS = ((1,), (1,))


def call(kernel, outs, scratch, specs, args, flops, size):
    return pl.pallas_call(
        kernel,
        out_shape=[jax.ShapeDtypeStruct(shape, kind) for shape, kind in outs],
        in_specs=specs,
        scratch_shapes=scratch,
        compiler_params=pltpu.CompilerParams(vmem_limit_bytes=VMEM_LIMIT),
        cost_estimate=pl.CostEstimate(flops=flops, bytes_accessed=size, transcendentals=0),
    )(*args)


IN_VMEM = pl.BlockSpec(memory_space=pltpu.VMEM)
IN_SMEM = pl.BlockSpec(memory_space=pltpu.SMEM)
ANYWHERE = pl.BlockSpec(memory_space=pl.ANY)


def stacked_heads(pair):
    lane = lax.broadcasted_iota(jnp.int32, pair.shape, 1)
    zero = jnp.zeros_like(pair)
    return jnp.concatenate([jnp.where(lane < 64, pair, zero), jnp.where(lane < 64, zero, pair)])


def merged_heads(rows):
    lane = lax.broadcasted_iota(jnp.int32, (128, 128), 1)
    return jnp.where(lane < 64, rows[:128], rows[128:])


def unpacked_small(meta, packed):
    core, place, row_y, row_z = meta[0], meta[8], meta[9], meta[10]
    shard = lax.broadcasted_iota(jnp.int32, (64, 64), 0)
    row = lax.broadcasted_iota(jnp.int32, (64, 64), 1)
    far_z = (row_z - shard // 16) & 3
    far_y = (row_y - shard // 4) & 3
    far_x = ((shard // 2) & 1) ^ (place // 2)
    far_c = (shard & 1) ^ core
    ours = (row == ((far_z * 4 + far_y) * 2 + far_x) * 2 + far_c).astype(BF16)
    values = dot(ours, packed).astype(BF16)

    def spread_out(part, size, first):
        count = 64 * size
        lane = lax.broadcasted_iota(jnp.int32, (128, count), 0)
        col = lax.broadcasted_iota(jnp.int32, (128, count), 1)
        wide = dot(part, (lane == first + lax.rem(col, size)).astype(BF16))
        row = lax.broadcasted_iota(jnp.int32, (64, count), 0)
        behind = lax.broadcasted_iota(jnp.int32, (64, count), 1) - size * row
        inside = jnp.logical_and(behind >= 0, behind < size)
        return jnp.sum(jnp.where(inside, wide, 0.0), axis=0, keepdims=True)

    vectors = [spread_out(values[:, :128], 12, 12 * k) for k in range(8)]
    return vectors, spread_out(values[:, 128:], 48, 0)


def front_kernel(
    meta, tok, small, p0, p1, p2, p3, f0, f1, f2, f3,
    h1, q, k, v, p, o, mid, weights, vec, bias_up, bias,
):
    core, place, row_y, row_z = meta[0], meta[8], meta[9], meta[10]
    for far, pieces in enumerate(((p0, p1, p2, p3), (f0, f1, f2, f3))):
        for s, piece in enumerate(pieces):
            block = lax.rem(core + far, 2) * 4 + lax.rem(place + 4 - s, 4)
            for sz in range(4):
                for sy in range(4):
                    zy = lax.rem(row_z + 4 - sz, 4) * 4 + lax.rem(row_y + 4 - sy, 4)
                    weights[block, zy] = piece[sz, sy]
    rows, up_row = unpacked_small(meta, small[...])
    for index, row in enumerate(rows):
        vec[index : index + 1, :] = row
    bias_up[...] = up_row
    for j in range(8):
        unit, _ = normed_of(tok[j].astype(F32))
        h1[j * TOK : (j + 1) * TOK, :] = (unit * vec[0:1, :] + vec[1:2, :]).astype(BF16)
    key_row = lax.broadcasted_iota(jnp.int32, (TOK, 2 * TOK), 0)
    query_col = lax.rem(lax.broadcasted_iota(jnp.int32, (TOK, 2 * TOK), 1), TOK)
    bias[0:TOK, :] = jnp.where(key_row <= query_col, 0.0, -1e30)
    for j in range(1, 8):
        shown = meta[j] > 0
        bias[j * TOK : (j + 1) * TOK, :] = jnp.full((TOK, 2 * TOK), jnp.where(shown, 0.0, -1e30), F32)
    for n in range(2):
        cols = slice(n * 384, (n + 1) * 384)
        q[:, cols] = (
            dot(h1[0:TOK, :], weights[n].reshape(WIDTH, 384)) + vec[2:3, cols]
        ).astype(BF16)
        weight_key = weights[2 + n].reshape(WIDTH, 384)
        weight_value = weights[4 + n].reshape(WIDTH, 384)
        for j in range(4):
            rows = slice(j * 256, (j + 1) * 256)
            k[rows, cols] = dot(h1[rows, :], weight_key).astype(BF16)
            v[rows, cols] = (dot(h1[rows, :], weight_value) + vec[3:4, cols]).astype(BF16)
    for pair in range(6):
        lanes = slice(pair * 128, (pair + 1) * 128)
        scores = dot(k[:, lanes], stacked_heads(q[:, lanes]), ROWS) * 0.125 + bias[...]
        exponent = jnp.exp(scores - jnp.max(scores, axis=0, keepdims=True))
        probs = exponent * (1.0 / jnp.sum(exponent, axis=0, keepdims=True))
        low = probs.astype(BF16)
        p[pair] = low
        attended = dot(v[:, lanes].T, low)
        o[:, lanes] = merged_heads(attended.T).astype(BF16)
    for n in range(2):
        cols = slice(n * 384, (n + 1) * 384)
        mid[:, cols] = (
            tok[0, :, cols].astype(F32)
            + dot(o[...], weights[6 + n].reshape(WIDTH, 384))
            + vec[4:5, cols]
        )


def middle_kernel(
    meta, mid, dy, vec, bias_up, mine, other, weights,
    result, act, du_keep, du_send, h2, dmid, da, dattended, small, up_bias_grad,
    up, down, weight_out, sems,
):
    core = meta[0]
    far = 1 - core
    copies = [
        pltpu.make_async_copy(mine.at[:, :, pl.ds(0, 1536)], up.at[core], sems.at[0]),
        pltpu.make_async_copy(other.at[:, :, pl.ds(0, 1536)], up.at[far], sems.at[1]),
        pltpu.make_async_copy(weights.at[pl.ds(6, 2)], weight_out, sems.at[10]),
    ]
    for g in range(4):
        cols = pl.ds(1536 + 384 * g, 384)
        copies.append(
            pltpu.make_async_copy(mine.at[:, :, cols], down.at[core, :, g], sems.at[2 + g])
        )
        copies.append(
            pltpu.make_async_copy(other.at[:, :, cols], down.at[far, :, g], sems.at[6 + g])
        )
    for copy in copies:
        copy.start()
    unit, inverse = normed_of(mid[...])
    h2[...] = (unit * vec[5:6, :] + vec[6:7, :]).astype(BF16)
    for copy in copies:
        copy.wait()
    low = dy[...]
    outcome = [mid[:, 384 * n : 384 * n + 384] + vec[7:8, 384 * n : 384 * n + 384] for n in range(2)]
    dh2 = None
    for half in range(2):
        cols = slice(half * 1536, (half + 1) * 1536)
        wide = up[half].reshape(WIDTH, 1536)
        u = dot(h2[...], wide) + bias_up[:, cols]
        cube = 0.7978845608028654 * (u + 0.044715 * u * u * u)
        tanh = jnp.tanh(cube)
        low_act = (0.5 * u * (1.0 + tanh)).astype(BF16)
        act[:, cols] = low_act
        slope_half = 0.5 * (1.0 + tanh) + 0.5 * u * (1.0 - tanh * tanh) * 0.7978845608028654 * (
            1.0 + 3.0 * 0.044715 * u * u
        )
        grad_act = None
        for n in range(2):
            rows = down[n, half * 8 : half * 8 + 8].reshape(1536, 384)
            outcome[n] = outcome[n] + dot(low_act, rows)
            term = dot(low[:, 384 * n : 384 * n + 384], rows, ROWS)
            grad_act = term if grad_act is None else grad_act + term
        du = (grad_act * slope_half).astype(BF16)
        up_bias_grad[:, cols] = jnp.sum(du.astype(F32), axis=0, keepdims=True)

        @pl.when(core == half)
        def _():
            du_keep[...] = du

        @pl.when(core != half)
        def _():
            du_send[...] = du

        term = dot(du, wide, ROWS)
        dh2 = term if dh2 is None else dh2 + term
    for n in range(2):
        result[:, 384 * n : 384 * n + 384] = outcome[n].astype(BF16)
    upstream = low.astype(F32)
    dm = upstream + norm_backward(dh2, unit, inverse, vec[5:6, :])
    dmid[...] = dm
    branch = dm.astype(BF16)
    da[...] = branch
    small[0:1, :] = jnp.sum(branch.astype(F32), axis=0, keepdims=True)
    small[1:2, :] = jnp.sum(dh2 * unit, axis=0, keepdims=True)
    small[2:3, :] = jnp.sum(dh2, axis=0, keepdims=True)
    small[3:4, :] = jnp.sum(upstream, axis=0, keepdims=True)
    grad = dot(branch[:, :384], weight_out[0].reshape(WIDTH, 384), ROWS)
    grad = grad + dot(branch[:, 384:], weight_out[1].reshape(WIDTH, 384), ROWS)
    dattended[...] = grad.astype(BF16)


def attention_back_kernel(meta, q, k, v, p, do, later, dq, keep, send, biases):
    first = meta[0] == 0
    for pair in range(6):
        lanes = slice(pair * 128, (pair + 1) * 128)
        upstream = stacked_heads(do[:, lanes])
        keys = k[:, lanes]
        low = p[pair]
        probs = low.astype(F32)
        dprobs = dot(v[:, lanes], upstream, ROWS)
        inner = jnp.sum(probs * dprobs, axis=0, keepdims=True)
        dscores = (probs * (dprobs - inner)).astype(BF16)
        dk = dot(dscores, stacked_heads(q[:, lanes])) * 0.125
        dv = dot(low, upstream)
        low_dq = (merged_heads(dot(keys.T, dscores).T) * 0.125).astype(BF16)
        dq[:, lanes] = low_dq
        biases[0:1, lanes] = jnp.sum(low_dq.astype(F32), axis=0, keepdims=True)
        biases[1:2, lanes] = jnp.sum(dv, axis=0, keepdims=True)
        keep[:, lanes] = jnp.where(first, dk, dv).astype(BF16)
        send[:, lanes] = jnp.where(first, dv, dk).astype(BF16)


def feed_grads_kernel(h2, h2_far, du, du_far, act, act_far, dy, dy_far, out):
    lhs = jnp.concatenate([h2[...], h2_far[...]]).T
    for x in range(4):
        cols = slice(x * 384, (x + 1) * 384)
        grad = dot(lhs, jnp.concatenate([du[:, cols], du_far[:, cols]])).astype(BF16)
        for zy in range(16):
            out[((x % 2) * 16 + zy) * 2 + x // 2, 0:48, :] = grad[zy * 48 : zy * 48 + 48]
    rhs = jnp.concatenate([dy[...], dy_far[...]])
    for part in range(4):
        cols = slice(part * 768, (part + 1) * 768)
        lhs = jnp.concatenate([act[:, cols], act_far[:, cols]]).T
        grad = dot(lhs, rhs).astype(BF16)
        for n in range(16):
            zy, x = part * 4 + n // 4, n % 4
            out[((x % 2) * 16 + zy) * 2 + x // 2, 48:96, :] = grad[n * 48 : n * 48 + 48]


def in_grads_kernel(
    meta, h1, keep, got, o, o_far, da, da_far, dq, dq_far, weights, tok,
    out, ring, send, sums, total, weight, weight_query, sems,
):
    core = meta[0]
    copies = [
        pltpu.make_async_copy(weights.at[pl.ds(0, 2)], weight_query, sems.at[0]),
        pltpu.make_async_copy(weights.at[pl.ds(2 + 2 * core, 2)], weight, sems.at[1]),
    ]
    for copy in copies:
        copy.start()
    for j in range(8):
        there = (j + 4) % 8
        total[j * TOK : (j + 1) * TOK, :] = (
            keep[j * TOK : (j + 1) * TOK, :].astype(F32)
            + got[there * TOK : (there + 1) * TOK, :].astype(F32)
        ).astype(BF16)
    for copy in copies:
        copy.wait()
    for j in range(8):
        rows = total[j * TOK : (j + 1) * TOK, :]
        grad = dot(rows[:, :384], weight[0].reshape(WIDTH, 384), ROWS)
        grad = grad + dot(rows[:, 384:], weight[1].reshape(WIDTH, 384), ROWS)
        if j == 0:
            grad = grad + dot(dq[:, :384], weight_query[0].reshape(WIDTH, 384), ROWS)
            grad = grad + dot(dq[:, 384:], weight_query[1].reshape(WIDTH, 384), ROWS)
        unit, _ = normed_of(tok[j].astype(F32))
        gain = jnp.sum(grad * unit, axis=0, keepdims=True)
        offset = jnp.sum(grad, axis=0, keepdims=True)
        sums[0:1, :] = gain if j == 0 else sums[0:1, :] + gain
        sums[1:2, :] = offset if j == 0 else sums[1:2, :] + offset
        if j < 4:
            ring[j] = grad
        else:
            send[j - 4] = grad.astype(BF16)
    first = core == 0
    lhs = h1[...].T
    lhs_own = jnp.where(
        first,
        jnp.concatenate([h1[0:TOK, :], h1[4 * TOK : 5 * TOK, :]]).astype(F32),
        jnp.concatenate([o[...], o_far[...]]).astype(F32),
    ).astype(BF16).T
    rhs_own = jnp.where(
        first,
        jnp.concatenate([dq[...], dq_far[...]]).astype(F32),
        jnp.concatenate([da[...], da_far[...]]).astype(F32),
    ).astype(BF16)
    for b in range(2):
        cols = slice(b * 384, (b + 1) * 384)
        grad = dot(lhs, total[:, cols]).astype(BF16)
        grad_own = dot(lhs_own, rhs_own[:, cols]).astype(BF16)
        for zy in range(16):
            rows = slice(zy * 48, zy * 48 + 48)
            out[(b * 16 + zy) * 2 + 1 - core] = grad[rows]
            out[(b * 16 + zy) * 2 + core] = grad_own[rows]


def pass_kernel(value, *others):
    pass


def after(value, *earlier):
    return pl.pallas_call(
        pass_kernel,
        out_shape=jax.ShapeDtypeStruct(value.shape, value.dtype),
        in_specs=[ANYWHERE] * (1 + len(earlier)),
        out_specs=ANYWHERE,
        input_output_aliases={0: 0},
    )(value, *earlier)


def shifted(value, axis, steps):
    return lax.ppermute(value, axis, [(i, (i + steps) % 4) for i in range(4)])


def along(value, axis):
    return jnp.stack([value] + [shifted(value, axis, steps) for steps in (1, 2, 3)])


def gather_small(vectors, up_bias):
    own = jnp.concatenate(list(vectors) + [jnp.zeros((32,), BF16), up_bias, jnp.zeros((80,), BF16)])
    own = own.reshape(1, 256)
    pair = jnp.concatenate([own, core_swap(own)])
    quad = jnp.concatenate([pair, mirror(pair)])
    return along(along(quad, "y"), "z").reshape(64, 256)


def gather_weights(core, xh, place, pieces):
    in_weight, out_weight, up_weight, down_weight = pieces
    first = jnp.concatenate([in_weight, out_weight], axis=1)

    def part(which):
        return jnp.concatenate([half_of(first, which, 1), half_of(up_weight, which, 1)], axis=1)

    rows = ordered(core, part(core), core_swap(part(1 - core)), 0)

    def block(which):
        return lax.dynamic_slice_in_dim(rows[:, :1536], which * 384, 384, 1)

    got = mirror(jnp.concatenate([block(3 - place), rows[:, 1536:]], axis=1))
    chunk = ordered(xh, block(place), got[:, :384], 0)
    rest = ordered(xh, rows[:, 1536:], got[:, 384:], 0)
    down = ordered(core, half_of(down_weight, core, 1), core_swap(half_of(down_weight, 1 - core, 1)), 0)
    down = ordered(xh, down, mirror(down), 0)
    packed = jnp.concatenate([rest] + [down[48 * k : 48 * k + 48] for k in range(4)], axis=1)
    mine = lax.all_gather(packed, ("z", "y"), axis=0)
    chunk = along(along(chunk, "y"), "z")
    ring = [chunk] + [ring_shift(chunk, steps) for steps in (1, 2, 3)]
    return mine, ring + [core_swap(piece) for piece in ring]


def spread(blocks):
    got = lax.all_to_all(blocks, CHIPS, 0, 0, tiled=True)
    return jnp.sum(got.astype(F32), axis=0)


def local(
    tokens,
    cotangent,
    first_gain,
    first_offset,
    in_weight,
    query_bias,
    value_bias,
    out_weight,
    out_bias,
    second_gain,
    second_offset,
    up_weight,
    up_bias,
    down_weight,
    down_bias,
):
    core = lax.axis_index("c")
    xh = lax.axis_index("xh")
    xl = lax.axis_index("xl")
    place = 2 * xh + xl
    own_tokens = tokens.reshape(TOK, WIDTH)
    group = gather_tokens(own_tokens)
    upstream = cotangent.reshape(TOK, WIDTH)
    upstream_half = half_of(upstream, core, 1)
    upstream_far = core_swap(half_of(upstream, 1 - core, 1))
    vectors = (
        first_gain,
        first_offset,
        query_bias,
        value_bias,
        out_bias,
        second_gain,
        second_offset,
        down_bias,
    )
    mine, pieces = gather_weights(core, xh, place, (in_weight, out_weight, up_weight, down_weight))
    small = gather_small(vectors, up_bias)
    mine = after(mine, small, group, *pieces)
    other = core_swap(mine)

    blocks = []
    for apart in (0, 1):
        for steps in range(4):
            there = (place + 4 - steps) % 4
            blocks.append(((there // 2) * 2 + (core + apart) % 2) * 2 + there % 2)
    meta = jnp.stack(
        [core]
        + [(b < blocks[0]).astype(jnp.int32) for b in blocks[1:]]
        + [place, lax.axis_index("y"), lax.axis_index("z")]
    )

    h1, query, key, value, probs, attended, middle, weights, vec, bias_up = call(
        front_kernel,
        [
            ((8 * TOK, WIDTH), BF16),
            ((TOK, WIDTH), BF16),
            ((8 * TOK, WIDTH), BF16),
            ((8 * TOK, WIDTH), BF16),
            ((6, 8 * TOK, 2 * TOK), BF16),
            ((TOK, WIDTH), BF16),
            ((TOK, WIDTH), F32),
            ((8, 16, 48, 384), BF16),
            ((8, WIDTH), F32),
            ((1, HIDDEN), F32),
        ],
        [
            pltpu.VMEM((8 * TOK, 2 * TOK), F32),
        ],
        [IN_SMEM] + [IN_VMEM] * 10,
        (meta, group, small) + tuple(pieces),
        4_000_000_000,
        20_000_000,
    )
    (
        result,
        act,
        du_keep,
        du_send,
        h2,
        grad_middle,
        da,
        grad_attended,
        small_middle,
        grad_up_bias,
    ) = call(
        middle_kernel,
        [
            ((TOK, WIDTH), BF16),
            ((TOK, HIDDEN), BF16),
            ((TOK, HIDDEN // 2), BF16),
            ((TOK, HIDDEN // 2), BF16),
            ((TOK, WIDTH), BF16),
            ((TOK, WIDTH), F32),
            ((TOK, WIDTH), BF16),
            ((TOK, WIDTH), BF16),
            ((4, WIDTH), F32),
            ((1, HIDDEN), F32),
        ],
        [
            pltpu.VMEM((2, 16, 48, 1536), BF16),
            pltpu.VMEM((2, 16, 4, 48, 384), BF16),
            pltpu.VMEM((2, 16, 48, 384), BF16),
            pltpu.SemaphoreType.DMA((11,)),
        ],
        [IN_SMEM] + [IN_VMEM] * 4 + [ANYWHERE] * 3,
        (meta, middle, upstream, vec, bias_up, mine, other, weights),
        3_000_000_000,
        20_000_000,
    )
    act_far = core_swap(act)
    du_far = core_swap(du_send)
    rows_far = core_swap(jnp.concatenate([h2, attended, da]))
    (first_blocks,) = call(
        feed_grads_kernel,
        [((64, 96, 384), BF16)],
        [],
        [IN_VMEM] * 8,
        (h2, rows_far[:TOK], du_keep, du_far, act, act_far, upstream_half, upstream_far),
        2_000_000_000,
        10_000_000,
    )
    first_sum = spread(first_blocks)

    grad_query, keep, send, small_attention = call(
        attention_back_kernel,
        [
            ((TOK, WIDTH), BF16),
            ((8 * TOK, WIDTH), BF16),
            ((8 * TOK, WIDTH), BF16),
            ((2, WIDTH), F32),
        ],
        [],
        [IN_SMEM] + [IN_VMEM] * 5 + [ANYWHERE],
        (meta, query, key, value, probs, grad_attended, first_blocks),
        3_000_000_000,
        20_000_000,
    )
    got = core_swap(send)
    query_far = core_swap(grad_query)
    second_blocks, ring, ring_send, small_first = call(
        in_grads_kernel,
        [
            ((64, 48, 384), BF16),
            ((4, TOK, WIDTH), F32),
            ((4, TOK, WIDTH), BF16),
            ((2, WIDTH), F32),
        ],
        [
            pltpu.VMEM((8 * TOK, WIDTH), BF16),
            pltpu.VMEM((2, 16, 48, 384), BF16),
            pltpu.VMEM((2, 16, 48, 384), BF16),
            pltpu.SemaphoreType.DMA((2,)),
        ],
        [IN_SMEM] + [IN_VMEM] * 9 + [ANYWHERE, IN_VMEM],
        (
            meta,
            h1,
            keep,
            got,
            attended,
            rows_far[TOK : 2 * TOK],
            da,
            rows_far[2 * TOK :],
            grad_query,
            query_far,
            weights,
            group,
        ),
        3_000_000_000,
        20_000_000,
    )
    second_blocks = after(second_blocks, first_sum)
    second_sum = spread(second_blocks)
    small_first = after(small_first, second_blocks)
    ring_send = after(ring_send, second_blocks)

    ring = ring + core_swap(ring_send).astype(F32)
    grad_normed = ring[0]
    for steps in (1, 2, 3):
        grad_normed = grad_normed + ring_shift(ring[steps].astype(BF16), -steps).astype(F32)
    unit_one, inverse_one = normed_of(own_tokens.astype(F32))
    grad_input = grad_middle + norm_backward(grad_normed, unit_one, inverse_one, vec[0])

    small_sum = jnp.concatenate(
        [small_first, small_attention, small_middle, grad_up_bias.reshape(4, WIDTH)]
    )
    for axis in ("y", "z"):
        small_sum = jnp.sum(along(small_sum, axis), axis=0)
    small_sum = small_sum + sum(ring_shift(small_sum, steps) for steps in (1, 2, 3))
    small_sum = small_sum + core_swap(small_sum)
    shard = ((lax.axis_index("z") * 4 + lax.axis_index("y")) * 2 + xh) * 2 + core
    small_own = lax.dynamic_slice_in_dim(small_sum[:8], 12 * shard, 12, 1)
    up_bias_own = lax.dynamic_slice_in_dim(small_sum[8:].reshape(HIDDEN), 48 * shard, 48, 0)

    down_sum = first_sum[48:].astype(BF16)
    down_own = ordered(core, down_sum, core_swap(down_sum), 1)
    down_own = jnp.where(xl == core, down_own, lax.ppermute(down_own, "xl", SWAP)).astype(F32)
    sums = jnp.stack([first_sum[:48], second_sum]).astype(BF16)

    def rows_for(steps):
        there = ((place + steps) % 4) // 2
        return lax.dynamic_slice_in_dim(sums, there * 24, 24, 1)

    parts = jnp.stack([rows_for(0)] + [ring_shift(rows_for(steps), steps) for steps in (1, 2, 3)])
    parts = jnp.stack([parts[(place + 4 - source) % 4] for source in range(4)])
    parts = parts.reshape(4, 2, 2, 12, 384)
    keep_rows = lax.dynamic_index_in_dim(parts, core, 2, keepdims=False)
    send_rows = lax.dynamic_index_in_dim(parts, 1 - core, 2, keepdims=False)
    both = ordered(core, keep_rows[None], core_swap(send_rows)[None], 0)
    wide_own = both.transpose(2, 3, 0, 1, 4).reshape(2, 12, 3072).astype(F32)
    return (
        result.reshape(tokens.shape),
        grad_input.astype(BF16).reshape(tokens.shape),
        small_own[0],
        small_own[1],
        wide_own[1][:, : 3 * WIDTH],
        small_own[2],
        small_own[3],
        wide_own[1][:, 3 * WIDTH :],
        small_own[4],
        small_own[5],
        small_own[6],
        wide_own[0],
        up_bias_own,
        down_own,
        small_own[7],
    )


def solution(mesh):
    fine = Mesh(mesh.devices.reshape(2, 4, 4, 2, 2), ("xl", "z", "y", "xh", "c"))
    tok = P(SHARD, "xl", None, None)
    vec = P(SHARD)
    mat = P(SHARD, None)
    return jax.shard_map(
        local,
        mesh=fine,
        in_specs=(tok, tok, vec, vec, mat, vec, vec, mat, vec, vec, vec, mat, vec, mat, vec),
        out_specs=(tok, tok, vec, vec, mat, vec, vec, mat, vec, vec, vec, mat, vec, mat, vec),
        check_vma=False,
    )
```

```python
import jax
import jax.numpy as jnp
from jax import lax
from jax.experimental import pallas as pl
from jax.experimental.pallas import tpu as pltpu
from jax.sharding import Mesh, PartitionSpec as P

HEAD_DIM = 64
HEADS = 12
WIDTH = 768
HIDDEN = 3072
TOK = 128
RING = ("xl", "xh")
CHIPS = ("xl", "z", "y", "xh")
SHARD = ("z", "y", "xh", "c")
SWAP = [(0, 1), (1, 0)]
F32 = jnp.float32
BF16 = jnp.bfloat16


def ring_index(place):
    return (place % 2) * 2 + place // 2


def ring_shift(value, steps):
    pairs = [(ring_index(i), ring_index((i + steps) % 4)) for i in range(4)]
    return lax.ppermute(value, RING, pairs)


def mirror(value):
    pairs = [(ring_index(i), ring_index(3 - i)) for i in range(4)]
    return lax.ppermute(value, RING, pairs)


def core_swap(value):
    return lax.ppermute(value, "c", SWAP)


def ordered(flag, own, other, axis):
    return jnp.where(
        flag == 0,
        jnp.concatenate([own, other], axis=axis),
        jnp.concatenate([other, own], axis=axis),
    )


def half_of(value, which, axis):
    size = value.shape[axis] // 2
    return lax.dynamic_slice_in_dim(value, which * size, size, axis)


def normed_of(values):
    average = jnp.mean(values, axis=-1, keepdims=True)
    centered = values - average
    inverse = lax.rsqrt(jnp.mean(centered * centered, axis=-1, keepdims=True) + 1e-05)
    return centered * inverse, inverse


def norm_backward(upstream, normed, inverse, norm_gain):
    scaled = upstream * norm_gain
    return inverse * (
        scaled
        - jnp.mean(scaled, axis=-1, keepdims=True)
        - normed * jnp.mean(scaled * normed, axis=-1, keepdims=True)
    )


def gather_tokens(own):
    return [own] + [ring_shift(own, steps) for steps in (1, 2, 3)]


VMEM_LIMIT = 56 * 1024 * 1024


def dot(a, b, dims=((1,), (0,))):
    return lax.dot_general(a, b, (dims, ((), ())), preferred_element_type=F32)


ROWS = ((1,), (1,))


def call(kernel, outs, scratch, specs, args, flops, size):
    return pl.pallas_call(
        kernel,
        out_shape=[jax.ShapeDtypeStruct(shape, kind) for shape, kind in outs],
        in_specs=specs,
        scratch_shapes=scratch,
        compiler_params=pltpu.CompilerParams(vmem_limit_bytes=VMEM_LIMIT),
        cost_estimate=pl.CostEstimate(flops=flops, bytes_accessed=size, transcendentals=0),
    )(*args)


IN_VMEM = pl.BlockSpec(memory_space=pltpu.VMEM)
IN_SMEM = pl.BlockSpec(memory_space=pltpu.SMEM)
ANYWHERE = pl.BlockSpec(memory_space=pl.ANY)


def stacked_heads(pair):
    lane = lax.broadcasted_iota(jnp.int32, pair.shape, 1)
    zero = jnp.zeros_like(pair)
    return jnp.concatenate([jnp.where(lane < 64, pair, zero), jnp.where(lane < 64, zero, pair)])


def merged_heads(rows):
    lane = lax.broadcasted_iota(jnp.int32, (128, 128), 1)
    return jnp.where(lane < 64, rows[:128], rows[128:])


def unpacked_small(meta, packed):
    row_y, row_z = meta[9], meta[10]
    shard = lax.broadcasted_iota(jnp.int32, (64, WIDTH), 0)
    row = lax.broadcasted_iota(jnp.int32, (64, WIDTH), 1)
    far_z = (row_z - shard // 16) & 3
    far_y = (row_y - shard // 4) & 3
    start = (far_z * 4 + far_y) * 48 + 12 * (shard & 3)

    def picked(offset):
        return dot((row == start + offset).astype(BF16), packed).astype(BF16)

    def spread_out(part, size, first):
        count = 64 * size
        lane = lax.broadcasted_iota(jnp.int32, (128, count), 0)
        col = lax.broadcasted_iota(jnp.int32, (128, count), 1)
        wide = dot(part, (lane == first + lax.rem(col, size)).astype(BF16))
        row = lax.broadcasted_iota(jnp.int32, (64, count), 0)
        behind = lax.broadcasted_iota(jnp.int32, (64, count), 1) - size * row
        inside = jnp.logical_and(behind >= 0, behind < size)
        return jnp.sum(jnp.where(inside, wide, 0.0), axis=0, keepdims=True)

    values = picked(0)
    return [spread_out(values, 12, 12 * k) for k in range(8)], spread_out(picked(1), 48, 0)


def front_kernel(
    meta, tok, small, p0, p1, p2, p3, f0, f1, f2, f3,
    h1, q, k, v, p, o, mid, weights, vec, bias_up, bias,
):
    core, place, row_y, row_z = meta[0], meta[8], meta[9], meta[10]
    for far, pieces in enumerate(((p0, p1, p2, p3), (f0, f1, f2, f3))):
        for s, piece in enumerate(pieces):
            block = lax.rem(core + far, 2) * 4 + lax.rem(place + 4 - s, 4)
            for sz in range(4):
                for sy in range(4):
                    zy = lax.rem(row_z + 4 - sz, 4) * 4 + lax.rem(row_y + 4 - sy, 4)
                    weights[block, zy] = piece[sz, sy]
    rows, up_row = unpacked_small(meta, small[...])
    for index, row in enumerate(rows):
        vec[index : index + 1, :] = row
    bias_up[...] = up_row
    for j in range(8):
        unit, _ = normed_of(tok[j].astype(F32))
        h1[j * TOK : (j + 1) * TOK, :] = (unit * vec[0:1, :] + vec[1:2, :]).astype(BF16)
    key_row = lax.broadcasted_iota(jnp.int32, (TOK, 2 * TOK), 0)
    query_col = lax.rem(lax.broadcasted_iota(jnp.int32, (TOK, 2 * TOK), 1), TOK)
    bias[0:TOK, :] = jnp.where(key_row <= query_col, 0.0, -1e30)
    for j in range(1, 8):
        shown = meta[j] > 0
        bias[j * TOK : (j + 1) * TOK, :] = jnp.full((TOK, 2 * TOK), jnp.where(shown, 0.0, -1e30), F32)
    for n in range(2):
        cols = slice(n * 384, (n + 1) * 384)
        q[:, cols] = (
            dot(h1[0:TOK, :], weights[n].reshape(WIDTH, 384)) + vec[2:3, cols]
        ).astype(BF16)
        weight_key = weights[2 + n].reshape(WIDTH, 384)
        weight_value = weights[4 + n].reshape(WIDTH, 384)
        for j in range(4):
            rows = slice(j * 256, (j + 1) * 256)
            k[rows, cols] = dot(h1[rows, :], weight_key).astype(BF16)
            v[rows, cols] = (dot(h1[rows, :], weight_value) + vec[3:4, cols]).astype(BF16)
    for pair in range(6):
        lanes = slice(pair * 128, (pair + 1) * 128)
        scores = dot(k[:, lanes], stacked_heads(q[:, lanes]), ROWS) * 0.125 + bias[...]
        exponent = jnp.exp(scores - jnp.max(scores, axis=0, keepdims=True))
        probs = exponent * (1.0 / jnp.sum(exponent, axis=0, keepdims=True))
        low = probs.astype(BF16)
        p[pair] = low
        attended = dot(v[:, lanes].T, low)
        o[:, lanes] = merged_heads(attended.T).astype(BF16)
    for n in range(2):
        cols = slice(n * 384, (n + 1) * 384)
        mid[:, cols] = (
            tok[0, :, cols].astype(F32)
            + dot(o[...], weights[6 + n].reshape(WIDTH, 384))
            + vec[4:5, cols]
        )


def middle_kernel(
    meta, mid, dy, vec, bias_up, mine, other, weights,
    result, act, du_keep, du_send, h2, dmid, da, dattended, small, up_bias_grad,
    up, down, weight_out, sems,
):
    core = meta[0]
    far = 1 - core
    copies = [
        pltpu.make_async_copy(mine.at[:, :, pl.ds(0, 1536)], up.at[core], sems.at[0]),
        pltpu.make_async_copy(other.at[:, :, pl.ds(0, 1536)], up.at[far], sems.at[1]),
        pltpu.make_async_copy(weights.at[pl.ds(6, 2)], weight_out, sems.at[10]),
    ]
    for g in range(4):
        cols = pl.ds(1536 + 384 * g, 384)
        copies.append(
            pltpu.make_async_copy(mine.at[:, :, cols], down.at[core, :, g], sems.at[2 + g])
        )
        copies.append(
            pltpu.make_async_copy(other.at[:, :, cols], down.at[far, :, g], sems.at[6 + g])
        )
    for copy in copies:
        copy.start()
    unit, inverse = normed_of(mid[...])
    h2[...] = (unit * vec[5:6, :] + vec[6:7, :]).astype(BF16)
    for copy in copies:
        copy.wait()
    low = dy[...]
    outcome = [mid[:, 384 * n : 384 * n + 384] + vec[7:8, 384 * n : 384 * n + 384] for n in range(2)]
    dh2 = None
    for half in range(2):
        cols = slice(half * 1536, (half + 1) * 1536)
        wide = up[half].reshape(WIDTH, 1536)
        u = dot(h2[...], wide) + bias_up[:, cols]
        cube = 0.7978845608028654 * (u + 0.044715 * u * u * u)
        tanh = jnp.tanh(cube)
        low_act = (0.5 * u * (1.0 + tanh)).astype(BF16)
        act[:, cols] = low_act
        slope_half = 0.5 * (1.0 + tanh) + 0.5 * u * (1.0 - tanh * tanh) * 0.7978845608028654 * (
            1.0 + 3.0 * 0.044715 * u * u
        )
        grad_act = None
        for n in range(2):
            rows = down[n, half * 8 : half * 8 + 8].reshape(1536, 384)
            outcome[n] = outcome[n] + dot(low_act, rows)
            term = dot(low[:, 384 * n : 384 * n + 384], rows, ROWS)
            grad_act = term if grad_act is None else grad_act + term
        du = (grad_act * slope_half).astype(BF16)
        up_bias_grad[:, cols] = jnp.sum(du.astype(F32), axis=0, keepdims=True)

        @pl.when(core == half)
        def _():
            du_keep[...] = du

        @pl.when(core != half)
        def _():
            du_send[...] = du

        term = dot(du, wide, ROWS)
        dh2 = term if dh2 is None else dh2 + term
    for n in range(2):
        result[:, 384 * n : 384 * n + 384] = outcome[n].astype(BF16)
    upstream = low.astype(F32)
    dm = upstream + norm_backward(dh2, unit, inverse, vec[5:6, :])
    dmid[...] = dm
    branch = dm.astype(BF16)
    da[...] = branch
    small[0:1, :] = jnp.sum(branch.astype(F32), axis=0, keepdims=True)
    small[1:2, :] = jnp.sum(dh2 * unit, axis=0, keepdims=True)
    small[2:3, :] = jnp.sum(dh2, axis=0, keepdims=True)
    small[3:4, :] = jnp.sum(upstream, axis=0, keepdims=True)
    grad = dot(branch[:, :384], weight_out[0].reshape(WIDTH, 384), ROWS)
    grad = grad + dot(branch[:, 384:], weight_out[1].reshape(WIDTH, 384), ROWS)
    dattended[...] = grad.astype(BF16)


def attention_back_kernel(meta, q, k, v, p, do, dq, keep, send, biases):
    first = meta[0] == 0
    for pair in range(6):
        lanes = slice(pair * 128, (pair + 1) * 128)
        upstream = stacked_heads(do[:, lanes])
        keys = k[:, lanes]
        low = p[pair]
        probs = low.astype(F32)
        dprobs = dot(v[:, lanes], upstream, ROWS)
        inner = jnp.sum(probs * dprobs, axis=0, keepdims=True)
        dscores = (probs * (dprobs - inner)).astype(BF16)
        dk = dot(dscores, stacked_heads(q[:, lanes])) * 0.125
        dv = dot(low, upstream)
        low_dq = (merged_heads(dot(keys.T, dscores).T) * 0.125).astype(BF16)
        dq[:, lanes] = low_dq
        biases[0:1, lanes] = jnp.sum(low_dq.astype(F32), axis=0, keepdims=True)
        biases[1:2, lanes] = jnp.sum(dv, axis=0, keepdims=True)
        keep[:, lanes] = jnp.where(first, dk, dv).astype(BF16)
        send[:, lanes] = jnp.where(first, dv, dk).astype(BF16)


def relative(base, steps):
    return lax.rem(base + steps, 4)


def write_parts(meta, rows_y, rows_z, by_y, by_z):
    row_y, row_z = meta[9], meta[10]
    for y in range(4):
        for t in range(4):
            by_y[y, t] = rows_y[relative(row_z, t) * 4 + y]
            by_z[y][t] = rows_z[relative(row_z, y) * 4 + relative(row_y, t)]


def feed_grads_kernel(meta, h2, h2_far, du, du_far, act, act_far, dy, dy_far, earlier, *refs):
    by_y, by_z, (up_grad, down_grad) = refs[0], refs[1:5], refs[5:]
    lhs = jnp.concatenate([h2[...], h2_far[...]]).T
    for n in range(4):
        cols = slice(n * 384, (n + 1) * 384)
        grad = dot(lhs, jnp.concatenate([du[:, cols], du_far[:, cols]])).astype(BF16)
        up_grad[:, :, cols] = grad.reshape(16, 48, 384)
    rhs = jnp.concatenate([dy[...], dy_far[...]])
    for n in range(4):
        cols = slice(n * 768, (n + 1) * 768)
        lhs = jnp.concatenate([act[:, cols], act_far[:, cols]]).T
        down_grad[4 * n : 4 * n + 4] = dot(lhs, rhs).astype(BF16).reshape(4, 192, 384)
    write_parts(meta, up_grad, down_grad, by_y, by_z)


def summed(pieces, index):
    total = pieces[0][index].astype(F32)
    for piece in pieces[1:]:
        total = total + piece[index].astype(F32)
    return total


def fold_kernel(meta, up, down0, down1, down2, down3, first, second0, second1, second2, second3, *outs):
    down, second = (down0, down1, down2, down3), (second0, second1, second2, second3)
    for s in range(4):
        sources = range(4)
        outs[s][:, 0:1536] = sum(up[n, s].astype(F32) for n in sources).astype(BF16)
        outs[s][:, 1536:2432] = sum(first[n, s].astype(F32) for n in sources).astype(BF16)
        y = relative(meta[9], s)
        outs[4][y, 0:192, :] = summed(down, s).astype(BF16)
        outs[4][y, 192:288, :] = summed(second, s).astype(BF16)


def second_fold_kernel(w0, w1, w2, w3, tall, out, wide_sum, tall_sum):
    wide_sum[...] = summed((w0, w1, w2, w3), ...)
    tall_sum[...] = sum(tall[n].astype(F32) for n in range(4))
    for place in range(4):
        half, index = place // 2, ring_index(place)
        rows = slice(24 * half, 24 * half + 24)
        out[index, :, 0:2304] = wide_sum[rows, 0:2304].astype(BF16)
        out[index, :, 4608:4736] = wide_sum[rows, 2304:2432].astype(BF16)
        for n in range(2):
            start = 192 + 48 * n + 24 * half
            out[index, :, 2304 + 384 * n : 2688 + 384 * n] = tall_sum[start : start + 24, :].astype(BF16)
        for n in range(4):
            start = 96 * half + 24 * n
            out[index, :, 3072 + 384 * n : 3456 + 384 * n] = tall_sum[start : start + 24, :].astype(BF16)


def third_fold_kernel(meta, parts, keep_wide, send_wide, keep_down, send_down):
    total = sum(parts[n].astype(F32) for n in range(4))

    def part(which):
        down = total[:, 3072 + 768 * which : 3840 + 768 * which]
        return (
            jnp.concatenate([total[12 * which : 12 * which + 12, 0:3072], total[12 * which : 12 * which + 12, 4608:4736]], axis=1),
            jnp.concatenate([down[:, :384], down[:, 384:]]),
        )

    for core in range(2):

        @pl.when(meta[0] == core)
        def _():
            keep_wide[...], keep_down[...] = part(core)
            wide, down = part(1 - core)
            send_wide[...] = wide.astype(BF16)
            send_down[...] = down.astype(BF16)


def finish_kernel(meta, keep_wide, got_wide, keep_down, got_down, up, in_grad, out_grad, down, small):
    small[...] = keep_wide[:, 3072:3200] + got_wide[:, 3072:3200].astype(F32)
    for core in range(2):

        @pl.when(meta[0] == core)
        def _():
            wide = [keep_wide[...], got_wide[...].astype(F32)]
            tall = [keep_down[...], got_down[...].astype(F32)]
            if core == 1:
                wide, tall = wide[::-1], tall[::-1]
            up[:, 0:1536] = wide[0][:, 0:1536]
            up[:, 1536:3072] = wide[1][:, 0:1536]
            in_grad[:, 0:1536] = wide[0][:, 1536:3072]
            in_grad[:, 1536:2304] = wide[1][:, 1536:2304]
            out_grad[...] = wide[1][:, 2304:3072]
            down[:, 0:384] = tall[0]
            down[:, 384:768] = tall[1]


def in_grads_kernel(
    meta, h1, keep, got, o, o_far, da, da_far, dq, dq_far, small, weights, tok, earlier, earlier_too,
    *refs,
):
    by_y, by_z = refs[0], refs[1:5]
    ring, send, sums, total, weight, weight_query, grads_y, grads_z, sems = refs[5:]
    sums[...] = jnp.zeros_like(sums)
    sums[2:12, :] = small[...]
    core = meta[0]
    copies = [
        pltpu.make_async_copy(weights.at[pl.ds(0, 2)], weight_query, sems.at[0]),
        pltpu.make_async_copy(weights.at[pl.ds(2 + 2 * core, 2)], weight, sems.at[1]),
    ]
    for copy in copies:
        copy.start()
    for j in range(8):
        there = (j + 4) % 8
        total[j * TOK : (j + 1) * TOK, :] = (
            keep[j * TOK : (j + 1) * TOK, :].astype(F32)
            + got[there * TOK : (there + 1) * TOK, :].astype(F32)
        ).astype(BF16)
    for copy in copies:
        copy.wait()
    for j in range(8):
        rows = total[j * TOK : (j + 1) * TOK, :]
        grad = dot(rows[:, :384], weight[0].reshape(WIDTH, 384), ROWS)
        grad = grad + dot(rows[:, 384:], weight[1].reshape(WIDTH, 384), ROWS)
        if j == 0:
            grad = grad + dot(dq[:, :384], weight_query[0].reshape(WIDTH, 384), ROWS)
            grad = grad + dot(dq[:, 384:], weight_query[1].reshape(WIDTH, 384), ROWS)
        unit, _ = normed_of(tok[j].astype(F32))
        gain = jnp.sum(grad * unit, axis=0, keepdims=True)
        offset = jnp.sum(grad, axis=0, keepdims=True)
        sums[0:1, :] = gain if j == 0 else sums[0:1, :] + gain
        sums[1:2, :] = offset if j == 0 else sums[1:2, :] + offset
        if j < 4:
            ring[j] = grad
        else:
            send[j - 4] = grad.astype(BF16)
    first = core == 0
    lhs = h1[...].T
    lhs_own = jnp.where(
        first,
        jnp.concatenate([h1[0:TOK, :], h1[4 * TOK : 5 * TOK, :]]).astype(F32),
        jnp.concatenate([o[...], o_far[...]]).astype(F32),
    ).astype(BF16).T
    rhs_own = jnp.where(
        first,
        jnp.concatenate([dq[...], dq_far[...]]).astype(F32),
        jnp.concatenate([da[...], da_far[...]]).astype(F32),
    ).astype(BF16)
    for b in range(2):
        cols = slice(b * 384, (b + 1) * 384)
        grad = dot(lhs, total[:, cols])
        grad_own = dot(lhs_own, rhs_own[:, cols])
        low = jnp.where(first, grad_own, grad).astype(BF16)
        grads_y[:, :, cols] = low.reshape(16, 48, 384)
        low = jnp.where(first, grad, grad_own).astype(BF16)
        grads_z[:, 48 * b : 48 * b + 48, :] = low.reshape(16, 48, 384)
    grads_y[:, :, 768:896] = sums[...].T.astype(BF16).reshape(16, 48, 128)
    write_parts(meta, grads_y, grads_z, by_y, by_z)


def pass_kernel(value, *others):
    pass


def after(value, *earlier):
    return pl.pallas_call(
        pass_kernel,
        out_shape=jax.ShapeDtypeStruct(value.shape, value.dtype),
        in_specs=[ANYWHERE] * (1 + len(earlier)),
        out_specs=ANYWHERE,
        input_output_aliases={0: 0},
    )(value, *earlier)


def shifted(value, axis, steps):
    return lax.ppermute(value, axis, [(i, (i + steps) % 4) for i in range(4)])


def along(value, axis):
    return jnp.stack([value] + [shifted(value, axis, steps) for steps in (1, 2, 3)])


def quad_small(core, xh, vectors, up_bias):
    own = jnp.concatenate(list(vectors) + [jnp.zeros((32,), BF16), up_bias, jnp.zeros((1360,), BF16)])
    own = own.reshape(12, 128)
    pair = ordered(core, own, core_swap(own), 0)
    return ordered(xh, pair, mirror(pair), 0)


def gather_weights(core, xh, place, pieces, small):
    in_weight, out_weight, up_weight, down_weight = pieces
    first = jnp.concatenate([in_weight, out_weight], axis=1)

    def part(which):
        return jnp.concatenate([half_of(first, which, 1), half_of(up_weight, which, 1)], axis=1)

    rows = ordered(core, part(core), core_swap(part(1 - core)), 0)

    def block(which):
        return lax.dynamic_slice_in_dim(rows[:, :1536], which * 384, 384, 1)

    got = mirror(jnp.concatenate([block(3 - place), rows[:, 1536:]], axis=1))
    chunk = ordered(xh, block(place), got[:, :384], 0)
    rest = ordered(xh, rows[:, 1536:], got[:, 384:], 0)
    down = ordered(core, half_of(down_weight, core, 1), core_swap(half_of(down_weight, 1 - core, 1)), 0)
    down = ordered(xh, down, mirror(down), 0)
    packed = jnp.concatenate([rest] + [down[48 * k : 48 * k + 48] for k in range(4)], axis=1)
    mine = lax.all_gather(packed, ("z", "y"), axis=0)
    chunk = along(along(jnp.concatenate([chunk, small], axis=1), "y"), "z")
    small = chunk[:, :, :, 384:].reshape(WIDTH, 128)
    chunk = chunk[:, :, :, :384]
    ring = [chunk] + [ring_shift(chunk, steps) for steps in (1, 2, 3)]
    return mine, small, ring + [core_swap(piece) for piece in ring]


def travel_z(parts):
    return [parts[0]] + [shifted(parts[steps], "z", steps) for steps in (1, 2, 3)]


def exchanged(value, axis):
    return lax.all_to_all(value, axis, 0, 0, tiled=True)


def local(
    tokens,
    cotangent,
    first_gain,
    first_offset,
    in_weight,
    query_bias,
    value_bias,
    out_weight,
    out_bias,
    second_gain,
    second_offset,
    up_weight,
    up_bias,
    down_weight,
    down_bias,
):
    core = lax.axis_index("c")
    xh = lax.axis_index("xh")
    xl = lax.axis_index("xl")
    place = 2 * xh + xl
    own_tokens = tokens.reshape(TOK, WIDTH)
    token_ring = gather_tokens(own_tokens)
    upstream = cotangent.reshape(TOK, WIDTH)
    upstream_half = half_of(upstream, core, 1)
    upstream_far = core_swap(half_of(upstream, 1 - core, 1))
    vectors = (
        first_gain,
        first_offset,
        query_bias,
        value_bias,
        out_bias,
        second_gain,
        second_offset,
        down_bias,
    )
    mine, small, pieces = gather_weights(
        core,
        xh,
        place,
        (in_weight, out_weight, up_weight, down_weight),
        quad_small(core, xh, vectors, up_bias),
    )
    group = jnp.stack(token_ring)
    group = jnp.concatenate([group, core_swap(group)])
    mine = after(mine, small, group, *pieces)
    other = core_swap(mine)

    blocks = []
    for apart in (0, 1):
        for steps in range(4):
            there = (place + 4 - steps) % 4
            blocks.append(((there // 2) * 2 + (core + apart) % 2) * 2 + there % 2)
    meta = jnp.stack(
        [core]
        + [(b < blocks[0]).astype(jnp.int32) for b in blocks[1:]]
        + [place, lax.axis_index("y"), lax.axis_index("z")]
    )

    h1, query, key, value, probs, attended, middle, weights, vec, bias_up = call(
        front_kernel,
        [
            ((8 * TOK, WIDTH), BF16),
            ((TOK, WIDTH), BF16),
            ((8 * TOK, WIDTH), BF16),
            ((8 * TOK, WIDTH), BF16),
            ((6, 8 * TOK, 2 * TOK), BF16),
            ((TOK, WIDTH), BF16),
            ((TOK, WIDTH), F32),
            ((8, 16, 48, 384), BF16),
            ((8, WIDTH), F32),
            ((1, HIDDEN), F32),
        ],
        [
            pltpu.VMEM((8 * TOK, 2 * TOK), F32),
        ],
        [IN_SMEM] + [IN_VMEM] * 10,
        (meta, group, small) + tuple(pieces),
        1000,
        1000,
    )
    (
        result,
        act,
        du_keep,
        du_send,
        h2,
        grad_middle,
        da,
        grad_attended,
        small_middle,
        grad_up_bias,
    ) = call(
        middle_kernel,
        [
            ((TOK, WIDTH), BF16),
            ((TOK, HIDDEN), BF16),
            ((TOK, HIDDEN // 2), BF16),
            ((TOK, HIDDEN // 2), BF16),
            ((TOK, WIDTH), BF16),
            ((TOK, WIDTH), F32),
            ((TOK, WIDTH), BF16),
            ((TOK, WIDTH), BF16),
            ((4, WIDTH), F32),
            ((1, HIDDEN), F32),
        ],
        [
            pltpu.VMEM((2, 16, 48, 1536), BF16),
            pltpu.VMEM((2, 16, 4, 48, 384), BF16),
            pltpu.VMEM((2, 16, 48, 384), BF16),
            pltpu.SemaphoreType.DMA((11,)),
        ],
        [IN_SMEM] + [IN_VMEM] * 4 + [ANYWHERE] * 3,
        (meta, middle, upstream, vec, bias_up, mine, other, weights),
        1000,
        1000,
    )
    act_far = core_swap(act)
    du_far = core_swap(du_send)
    rows_far = core_swap(jnp.concatenate([h2, attended, da]))
    grad_query, keep, send, small_attention = call(
        attention_back_kernel,
        [
            ((TOK, WIDTH), BF16),
            ((8 * TOK, WIDTH), BF16),
            ((8 * TOK, WIDTH), BF16),
            ((2, WIDTH), F32),
        ],
        [],
        [IN_SMEM] + [IN_VMEM] * 5,
        (meta, query, key, value, probs, grad_attended),
        10_000_000_000,
        20_000_000,
    )
    first_parts = call(
        feed_grads_kernel,
        [((4, 4, 48, 1536), BF16)] + [((4, 192, 384), BF16)] * 4,
        [pltpu.VMEM((16, 48, 1536), BF16), pltpu.VMEM((16, 192, 384), BF16)],
        [IN_SMEM] + [IN_VMEM] * 8 + [ANYWHERE],
        (
            meta,
            h2,
            rows_far[:TOK],
            du_keep,
            du_far,
            act,
            act_far,
            upstream_half,
            upstream_far,
            grad_query,
        ),
        1000,
        1000,
    )
    first_got = [exchanged(first_parts[0], "y")] + travel_z(first_parts[1:])

    small_rows = jnp.concatenate(
        [
            small_attention,
            small_middle,
            grad_up_bias.reshape(64, 4, 12).transpose(1, 0, 2).reshape(4, WIDTH),
        ]
    )
    got = core_swap(send)
    query_far = core_swap(grad_query)
    *second_parts, ring, ring_send = call(
        in_grads_kernel,
        [
            ((4, 4, 48, 896), BF16),
            *([((4, 96, 384), BF16)] * 4),
            ((4, TOK, WIDTH), F32),
            ((4, TOK, WIDTH), BF16),
        ],
        [
            pltpu.VMEM((TOK, WIDTH), F32),
            pltpu.VMEM((8 * TOK, WIDTH), BF16),
            pltpu.VMEM((2, 16, 48, 384), BF16),
            pltpu.VMEM((2, 16, 48, 384), BF16),
            pltpu.VMEM((16, 48, 896), BF16),
            pltpu.VMEM((16, 96, 384), BF16),
            pltpu.SemaphoreType.DMA((2,)),
        ],
        [IN_SMEM] + [IN_VMEM] * 10 + [ANYWHERE, IN_VMEM, ANYWHERE, ANYWHERE],
        (
            meta,
            h1,
            keep,
            got,
            attended,
            rows_far[TOK : 2 * TOK],
            da,
            rows_far[2 * TOK :],
            grad_query,
            query_far,
            small_rows,
            weights,
            group,
            first_got[2],
            first_got[4],
        ),
        10_000_000_000,
        20_000_000,
    )
    second_got = [exchanged(second_parts[0], "y")] + travel_z(second_parts[1:])
    parts = call(
        fold_kernel,
        [((48, 2432), BF16)] * 4 + [((4, 288, 384), BF16)],
        [],
        [IN_SMEM] + [IN_VMEM] * 10,
        [meta] + first_got + second_got,
        1000,
        1000,
    )
    ring = ring + core_swap(ring_send).astype(F32)
    returned = [ring_shift(ring[steps].astype(BF16), -steps) for steps in (1, 2, 3)]
    grad_normed = ring[0] + sum(value.astype(F32) for value in returned)
    parts = [after(parts[0], *returned)] + list(parts[1:])
    (parts,) = call(
        second_fold_kernel,
        [((4, 24, 4736), BF16)],
        [pltpu.VMEM((48, 2432), F32), pltpu.VMEM((288, 384), F32)],
        [IN_VMEM] * 5,
        travel_z(parts) + [exchanged(parts[4], "y")],
        1000,
        1000,
    )
    keep_wide, send_wide, keep_down, send_down = call(
        third_fold_kernel,
        [((12, 3200), F32), ((12, 3200), BF16), ((48, 384), F32), ((48, 384), BF16)],
        [],
        [IN_SMEM, IN_VMEM],
        [meta, exchanged(parts, RING)],
        1000,
        1000,
    )
    up_own, in_own, out_own, down_own, small_own = call(
        finish_kernel,
        [((12, 3072), F32), ((12, 2304), F32), ((12, 768), F32), ((48, 768), F32), ((12, 128), F32)],
        [],
        [IN_SMEM] + [IN_VMEM] * 4,
        (meta, keep_wide, core_swap(send_wide), keep_down, core_swap(send_down)),
        1000,
        1000,
    )
    unit_one, inverse_one = normed_of(own_tokens.astype(F32))
    grad_input = grad_middle + norm_backward(grad_normed, unit_one, inverse_one, vec[0])

    small_own = small_own[:, :12].T
    up_bias_own = small_own[8:].reshape(48)
    return (
        result.reshape(tokens.shape),
        grad_input.astype(BF16).reshape(tokens.shape),
        small_own[0],
        small_own[1],
        in_own,
        small_own[2],
        small_own[3],
        out_own,
        small_own[4],
        small_own[5],
        small_own[6],
        up_own,
        up_bias_own,
        down_own,
        small_own[7],
    )


def solution(mesh):
    fine = Mesh(mesh.devices.reshape(2, 4, 4, 2, 2), ("xl", "z", "y", "xh", "c"))
    tok = P(SHARD, "xl", None, None)
    vec = P(SHARD)
    mat = P(SHARD, None)
    return jax.shard_map(
        local,
        mesh=fine,
        in_specs=(tok, tok, vec, vec, mat, vec, vec, mat, vec, vec, vec, mat, vec, mat, vec),
        out_specs=(tok, tok, vec, vec, mat, vec, vec, mat, vec, vec, vec, mat, vec, mat, vec),
        check_vma=False,
    )
```

```python
import jax
import jax.numpy as jnp
from jax import lax
from jax.experimental import pallas as pl
from jax.experimental.pallas import tpu as pltpu
from jax.sharding import Mesh, PartitionSpec as P

HEAD_DIM = 64
HEADS = 12
WIDTH = 768
HIDDEN = 3072
TOK = 128
RING = ("xl", "xh")
CHIPS = ("xl", "z", "y", "xh")
SHARD = ("z", "y", "xh", "c")
SWAP = [(0, 1), (1, 0)]
F32 = jnp.float32
BF16 = jnp.bfloat16


def ring_index(place):
    return (place % 2) * 2 + place // 2


def ring_shift(value, steps):
    pairs = [(ring_index(i), ring_index((i + steps) % 4)) for i in range(4)]
    return lax.ppermute(value, RING, pairs)


def mirror(value):
    pairs = [(ring_index(i), ring_index(3 - i)) for i in range(4)]
    return lax.ppermute(value, RING, pairs)


def core_swap(value):
    return lax.ppermute(value, "c", SWAP)


def ordered(flag, own, other, axis):
    return jnp.where(
        flag == 0,
        jnp.concatenate([own, other], axis=axis),
        jnp.concatenate([other, own], axis=axis),
    )


def half_of(value, which, axis):
    size = value.shape[axis] // 2
    return lax.dynamic_slice_in_dim(value, which * size, size, axis)


def normed_of(values):
    average = jnp.mean(values, axis=-1, keepdims=True)
    centered = values - average
    inverse = lax.rsqrt(jnp.mean(centered * centered, axis=-1, keepdims=True) + 1e-05)
    return centered * inverse, inverse


def norm_backward(upstream, normed, inverse, norm_gain):
    scaled = upstream * norm_gain
    return inverse * (
        scaled
        - jnp.mean(scaled, axis=-1, keepdims=True)
        - normed * jnp.mean(scaled * normed, axis=-1, keepdims=True)
    )


def gather_tokens(own):
    return [own] + [ring_shift(own, steps) for steps in (1, 2, 3)]


VMEM_LIMIT = 56 * 1024 * 1024


def dot(a, b, dims=((1,), (0,))):
    return lax.dot_general(a, b, (dims, ((), ())), preferred_element_type=F32)


ROWS = ((1,), (1,))


IN_VMEM = pl.BlockSpec(memory_space=pltpu.VMEM)
IN_SMEM = pl.BlockSpec(memory_space=pltpu.SMEM)
ANYWHERE = pl.BlockSpec(memory_space=pl.ANY)


def call(kernel, outs, scratch, specs, args, flops, size, by_hand=()):
    return pl.pallas_call(
        kernel,
        out_specs=[ANYWHERE if n in by_hand else IN_VMEM for n in range(len(outs))],
        out_shape=[jax.ShapeDtypeStruct(shape, kind) for shape, kind in outs],
        in_specs=specs,
        scratch_shapes=scratch,
        compiler_params=pltpu.CompilerParams(vmem_limit_bytes=VMEM_LIMIT),
        cost_estimate=pl.CostEstimate(flops=flops, bytes_accessed=size, transcendentals=0),
    )(*args)


def stacked_heads(pair):
    lane = lax.broadcasted_iota(jnp.int32, pair.shape, 1)
    zero = jnp.zeros_like(pair)
    return jnp.concatenate([jnp.where(lane < 64, pair, zero), jnp.where(lane < 64, zero, pair)])


def merged_heads(rows):
    lane = lax.broadcasted_iota(jnp.int32, (128, 128), 1)
    return jnp.where(lane < 64, rows[:128], rows[128:])


def unpacked_small(meta, packed):
    row_y, row_z = meta[9], meta[10]
    shard = lax.broadcasted_iota(jnp.int32, (64, WIDTH), 0)
    row = lax.broadcasted_iota(jnp.int32, (64, WIDTH), 1)
    far_z = (row_z - shard // 16) & 3
    far_y = (row_y - shard // 4) & 3
    start = (far_z * 4 + far_y) * 48 + 12 * (shard & 3)

    def picked(offset):
        return dot((row == start + offset).astype(BF16), packed).astype(BF16)

    def spread_out(part, size, first):
        count = 64 * size
        lane = lax.broadcasted_iota(jnp.int32, (128, count), 0)
        col = lax.broadcasted_iota(jnp.int32, (128, count), 1)
        wide = dot(part, (lane == first + lax.rem(col, size)).astype(BF16))
        row = lax.broadcasted_iota(jnp.int32, (64, count), 0)
        behind = lax.broadcasted_iota(jnp.int32, (64, count), 1) - size * row
        inside = jnp.logical_and(behind >= 0, behind < size)
        return jnp.sum(jnp.where(inside, wide, 0.0), axis=0, keepdims=True)

    values = picked(0)
    return [spread_out(values, 12, 12 * k) for k in range(8)], spread_out(picked(1), 48, 0)


def front_kernel(
    meta, tok, small, p0, p1, p2, p3, f0, f1, f2, f3,
    h1_out, q, k_out, v_out, p_out, o, mid, weights_out, vec, bias_up,
    h1, k, v, p, weights, bias, sems,
):
    core, place, row_y, row_z = meta[0], meta[8], meta[9], meta[10]
    for far, pieces in enumerate(((p0, p1, p2, p3), (f0, f1, f2, f3))):
        for s, piece in enumerate(pieces):
            block = lax.rem(core + far, 2) * 4 + lax.rem(place + 4 - s, 4)
            for sz in range(4):
                for sy in range(4):
                    zy = lax.rem(row_z + 4 - sz, 4) * 4 + lax.rem(row_y + 4 - sy, 4)
                    weights[block, zy] = piece[sz, sy]
    copies = [pltpu.make_async_copy(weights, weights_out, sems.at[0])]
    copies[0].start()
    rows, up_row = unpacked_small(meta, small[...])
    for index, row in enumerate(rows):
        vec[index : index + 1, :] = row
    bias_up[...] = up_row
    for j in range(8):
        unit, _ = normed_of(tok[j].astype(F32))
        h1[j * TOK : (j + 1) * TOK, :] = (unit * vec[0:1, :] + vec[1:2, :]).astype(BF16)
    copies.append(pltpu.make_async_copy(h1, h1_out, sems.at[1]))
    copies[-1].start()
    key_row = lax.broadcasted_iota(jnp.int32, (TOK, 2 * TOK), 0)
    query_col = lax.rem(lax.broadcasted_iota(jnp.int32, (TOK, 2 * TOK), 1), TOK)
    bias[0:TOK, :] = jnp.where(key_row <= query_col, 0.0, -1e30)
    for j in range(1, 8):
        shown = meta[j] > 0
        bias[j * TOK : (j + 1) * TOK, :] = jnp.full((TOK, 2 * TOK), jnp.where(shown, 0.0, -1e30), F32)
    for n in range(2):
        cols = slice(n * 384, (n + 1) * 384)
        q[:, cols] = (
            dot(h1[0:TOK, :], weights[n].reshape(WIDTH, 384)) + vec[2:3, cols]
        ).astype(BF16)
        weight_key = weights[2 + n].reshape(WIDTH, 384)
        weight_value = weights[4 + n].reshape(WIDTH, 384)
        for j in range(4):
            rows = slice(j * 256, (j + 1) * 256)
            k[rows, cols] = dot(h1[rows, :], weight_key).astype(BF16)
            v[rows, cols] = (dot(h1[rows, :], weight_value) + vec[3:4, cols]).astype(BF16)
    copies.append(pltpu.make_async_copy(k, k_out, sems.at[2]))
    copies.append(pltpu.make_async_copy(v, v_out, sems.at[3]))
    copies[-2].start()
    copies[-1].start()
    for pair in range(6):
        lanes = slice(pair * 128, (pair + 1) * 128)
        scores = dot(k[:, lanes], stacked_heads(q[:, lanes]), ROWS) * 0.125 + bias[...]
        exponent = jnp.exp(scores - jnp.max(scores, axis=0, keepdims=True))
        probs = exponent * (1.0 / jnp.sum(exponent, axis=0, keepdims=True))
        low = probs.astype(BF16)
        p[pair] = low
        copies.append(pltpu.make_async_copy(p.at[pair], p_out.at[pair], sems.at[4 + pair]))
        copies[-1].start()
        attended = dot(v[:, lanes].T, low)
        o[:, lanes] = merged_heads(attended.T).astype(BF16)
    for n in range(2):
        cols = slice(n * 384, (n + 1) * 384)
        mid[:, cols] = (
            tok[0, :, cols].astype(F32)
            + dot(o[...], weights[6 + n].reshape(WIDTH, 384))
            + vec[4:5, cols]
        )
    for copy in copies:
        copy.wait()


def middle_kernel(
    meta, mid, dy, vec, bias_up, mine, other, weights,
    result, act, du_keep, du_send, h2, dmid, da, dattended, small, up_bias_grad,
    up, down, weight_out, sems,
):
    core = meta[0]
    far = 1 - core
    copies = [
        pltpu.make_async_copy(mine.at[:, :, pl.ds(0, 1536)], up.at[core], sems.at[0]),
        pltpu.make_async_copy(other.at[:, :, pl.ds(0, 1536)], up.at[far], sems.at[1]),
        pltpu.make_async_copy(weights.at[pl.ds(6, 2)], weight_out, sems.at[10]),
    ]
    for g in range(4):
        cols = pl.ds(1536 + 384 * g, 384)
        copies.append(
            pltpu.make_async_copy(mine.at[:, :, cols], down.at[core, :, g], sems.at[2 + g])
        )
        copies.append(
            pltpu.make_async_copy(other.at[:, :, cols], down.at[far, :, g], sems.at[6 + g])
        )
    for copy in copies:
        copy.start()
    unit, inverse = normed_of(mid[...])
    h2[...] = (unit * vec[5:6, :] + vec[6:7, :]).astype(BF16)
    for copy in copies[:3]:
        copy.wait()
    low = dy[...]
    outcome = [mid[:, 384 * n : 384 * n + 384] + vec[7:8, 384 * n : 384 * n + 384] for n in range(2)]
    dh2 = None
    for half in range(2):
        cols = slice(half * 1536, (half + 1) * 1536)
        wide = up[half].reshape(WIDTH, 1536)
        u = dot(h2[...], wide) + bias_up[:, cols]
        cube = 0.7978845608028654 * (u + 0.044715 * u * u * u)
        tanh = jnp.tanh(cube)
        low_act = (0.5 * u * (1.0 + tanh)).astype(BF16)
        act[:, cols] = low_act
        slope_half = 0.5 * (1.0 + tanh) + 0.5 * u * (1.0 - tanh * tanh) * 0.7978845608028654 * (
            1.0 + 3.0 * 0.044715 * u * u
        )
        grad_act = None
        if half == 0:
            for copy in copies[3:]:
                copy.wait()
        for n in range(2):
            rows = down[n, half * 8 : half * 8 + 8].reshape(1536, 384)
            outcome[n] = outcome[n] + dot(low_act, rows)
            term = dot(low[:, 384 * n : 384 * n + 384], rows, ROWS)
            grad_act = term if grad_act is None else grad_act + term
        du = (grad_act * slope_half).astype(BF16)
        up_bias_grad[:, cols] = jnp.sum(du.astype(F32), axis=0, keepdims=True)

        @pl.when(core == half)
        def _():
            du_keep[...] = du

        @pl.when(core != half)
        def _():
            du_send[...] = du

        term = dot(du, wide, ROWS)
        dh2 = term if dh2 is None else dh2 + term
    for n in range(2):
        result[:, 384 * n : 384 * n + 384] = outcome[n].astype(BF16)
    upstream = low.astype(F32)
    dm = upstream + norm_backward(dh2, unit, inverse, vec[5:6, :])
    dmid[...] = dm
    branch = dm.astype(BF16)
    da[...] = branch
    small[0:1, :] = jnp.sum(branch.astype(F32), axis=0, keepdims=True)
    small[1:2, :] = jnp.sum(dh2 * unit, axis=0, keepdims=True)
    small[2:3, :] = jnp.sum(dh2, axis=0, keepdims=True)
    small[3:4, :] = jnp.sum(upstream, axis=0, keepdims=True)
    grad = dot(branch[:, :384], weight_out[0].reshape(WIDTH, 384), ROWS)
    grad = grad + dot(branch[:, 384:], weight_out[1].reshape(WIDTH, 384), ROWS)
    dattended[...] = grad.astype(BF16)


def attention_back_kernel(meta, q, k, v, p, do, dq, keep, send, biases):
    first = meta[0] == 0
    for pair in range(6):
        lanes = slice(pair * 128, (pair + 1) * 128)
        upstream = stacked_heads(do[:, lanes])
        keys = k[:, lanes]
        low = p[pair]
        probs = low.astype(F32)
        dprobs = dot(v[:, lanes], upstream, ROWS)
        inner = jnp.sum(probs * dprobs, axis=0, keepdims=True)
        dscores = (probs * (dprobs - inner)).astype(BF16)
        dk = dot(dscores, stacked_heads(q[:, lanes])) * 0.125
        dv = dot(low, upstream)
        low_dq = (merged_heads(dot(keys.T, dscores).T) * 0.125).astype(BF16)
        dq[:, lanes] = low_dq
        biases[0:1, lanes] = jnp.sum(low_dq.astype(F32), axis=0, keepdims=True)
        biases[1:2, lanes] = jnp.sum(dv, axis=0, keepdims=True)
        keep[:, lanes] = jnp.where(first, dk, dv).astype(BF16)
        send[:, lanes] = jnp.where(first, dv, dk).astype(BF16)


def relative(base, steps):
    return lax.rem(base + steps, 4)


def copies_by_y(meta, rows, out, sems):
    return [
        pltpu.make_async_copy(
            rows.at[relative(meta[10], t) * 4 + y], out.at[y, t], sems.at[4 * y + t]
        )
        for y in range(4)
        for t in range(4)
    ]


def copies_by_z(meta, rows, outs, sems):
    return [
        pltpu.make_async_copy(
            rows.at[relative(meta[10], s) * 4 + relative(meta[9], t)],
            outs[s].at[t],
            sems.at[16 + 4 * s + t],
        )
        for s in range(4)
        for t in range(4)
    ]


def feed_grads_kernel(meta, h2, h2_far, du, du_far, act, act_far, dy, dy_far, earlier, *refs):
    by_y, by_z, (up_grad, down_grad, sems) = refs[0], refs[1:5], refs[5:]
    lhs = jnp.concatenate([h2[...], h2_far[...]]).T
    for n in range(4):
        cols = slice(n * 384, (n + 1) * 384)
        grad = dot(lhs, jnp.concatenate([du[:, cols], du_far[:, cols]])).astype(BF16)
        up_grad[:, :, cols] = grad.reshape(16, 48, 384)
    copies = copies_by_y(meta, up_grad, by_y, sems)
    for copy in copies:
        copy.start()
    rhs = jnp.concatenate([dy[...], dy_far[...]])
    for n in range(4):
        cols = slice(n * 768, (n + 1) * 768)
        lhs = jnp.concatenate([act[:, cols], act_far[:, cols]]).T
        down_grad[4 * n : 4 * n + 4] = dot(lhs, rhs).astype(BF16).reshape(4, 192, 384)
    more = copies_by_z(meta, down_grad, by_z, sems)
    for copy in more:
        copy.start()
    for copy in copies + more:
        copy.wait()


def summed(pieces, index):
    total = pieces[0][index].astype(F32)
    for piece in pieces[1:]:
        total = total + piece[index].astype(F32)
    return total


def fold_kernel(meta, up, down0, down1, down2, down3, first, second0, second1, second2, second3, *outs):
    down, second = (down0, down1, down2, down3), (second0, second1, second2, second3)
    for s in range(4):
        sources = range(4)
        outs[s][:, 0:1536] = sum(up[n, s].astype(F32) for n in sources).astype(BF16)
        outs[s][:, 1536:2432] = sum(first[n, s].astype(F32) for n in sources).astype(BF16)
        y = relative(meta[9], s)
        outs[4][y, 0:192, :] = summed(down, s).astype(BF16)
        outs[4][y, 192:288, :] = summed(second, s).astype(BF16)


def second_fold_kernel(w0, w1, w2, w3, tall, out, wide_sum, tall_sum):
    wide_sum[...] = summed((w0, w1, w2, w3), ...)
    tall_sum[...] = sum(tall[n].astype(F32) for n in range(4))
    for place in range(4):
        half, index = place // 2, ring_index(place)
        rows = slice(24 * half, 24 * half + 24)
        out[index, :, 0:2304] = wide_sum[rows, 0:2304].astype(BF16)
        out[index, :, 4608:4736] = wide_sum[rows, 2304:2432].astype(BF16)
        for n in range(2):
            start = 192 + 48 * n + 24 * half
            out[index, :, 2304 + 384 * n : 2688 + 384 * n] = tall_sum[start : start + 24, :].astype(BF16)
        for n in range(4):
            start = 96 * half + 24 * n
            out[index, :, 3072 + 384 * n : 3456 + 384 * n] = tall_sum[start : start + 24, :].astype(BF16)


def third_fold_kernel(meta, parts, keep_wide, send_wide, keep_down, send_down):
    total = sum(parts[n].astype(F32) for n in range(4))

    def part(which):
        down = total[:, 3072 + 768 * which : 3840 + 768 * which]
        return (
            jnp.concatenate([total[12 * which : 12 * which + 12, 0:3072], total[12 * which : 12 * which + 12, 4608:4736]], axis=1),
            jnp.concatenate([down[:, :384], down[:, 384:]]),
        )

    for core in range(2):

        @pl.when(meta[0] == core)
        def _():
            keep_wide[...], keep_down[...] = part(core)
            wide, down = part(1 - core)
            send_wide[...] = wide.astype(BF16)
            send_down[...] = down.astype(BF16)


def finish_kernel(meta, keep_wide, got_wide, keep_down, got_down, up, in_grad, out_grad, down, small):
    small[...] = keep_wide[:, 3072:3200] + got_wide[:, 3072:3200].astype(F32)
    for core in range(2):

        @pl.when(meta[0] == core)
        def _():
            wide = [keep_wide[...], got_wide[...].astype(F32)]
            tall = [keep_down[...], got_down[...].astype(F32)]
            if core == 1:
                wide, tall = wide[::-1], tall[::-1]
            up[:, 0:1536] = wide[0][:, 0:1536]
            up[:, 1536:3072] = wide[1][:, 0:1536]
            in_grad[:, 0:1536] = wide[0][:, 1536:3072]
            in_grad[:, 1536:2304] = wide[1][:, 1536:2304]
            out_grad[...] = wide[1][:, 2304:3072]
            down[:, 0:384] = tall[0]
            down[:, 384:768] = tall[1]


def in_grads_kernel(
    meta, h1, total, o, o_far, da, da_far, dq, dq_far, columns, earlier0, earlier1, earlier2, *refs
):
    by_y, by_z, (grads_y, grads_z, sems) = refs[0], refs[1:5], refs[5:]
    first = meta[0] == 0
    grads_y[:, :, 768:896] = columns[...]
    lhs = h1[...].T
    lhs_own = jnp.where(
        first,
        jnp.concatenate([h1[0:TOK, :], h1[4 * TOK : 5 * TOK, :]]).astype(F32),
        jnp.concatenate([o[...], o_far[...]]).astype(F32),
    ).astype(BF16).T
    rhs_own = jnp.where(
        first,
        jnp.concatenate([dq[...], dq_far[...]]).astype(F32),
        jnp.concatenate([da[...], da_far[...]]).astype(F32),
    ).astype(BF16)
    for b in range(2):
        cols = slice(b * 384, (b + 1) * 384)
        grad = dot(lhs, total[:, cols])
        grad_own = dot(lhs_own, rhs_own[:, cols])
        low = jnp.where(first, grad, grad_own).astype(BF16)
        grads_z[:, 48 * b : 48 * b + 48, :] = low.reshape(16, 48, 384)
        low = jnp.where(first, grad_own, grad).astype(BF16)
        grads_y[:, :, cols] = low.reshape(16, 48, 384)
    copies = copies_by_y(meta, grads_y, by_y, sems) + copies_by_z(meta, grads_z, by_z, sems)
    for copy in copies:
        copy.start()
    for copy in copies:
        copy.wait()


def in_back_kernel(
    meta, keep, got, dq, small, tok, weights, total, ring, send, columns, sums, weight, weight_query, sems
):
    copies = [
        pltpu.make_async_copy(weights.at[pl.ds(0, 2)], weight_query, sems.at[0]),
        pltpu.make_async_copy(weights.at[pl.ds(2 + 2 * meta[0], 2)], weight, sems.at[1]),
    ]
    for copy in copies:
        copy.start()
    sums[...] = jnp.zeros_like(sums)
    sums[2:12, :] = small[...]
    for copy in copies:
        copy.wait()
    for j in range(8):
        there = (j + 4) % 8
        rows = (
            keep[j * TOK : (j + 1) * TOK, :].astype(F32)
            + got[there * TOK : (there + 1) * TOK, :].astype(F32)
        ).astype(BF16)
        total[j * TOK : (j + 1) * TOK, :] = rows
        grad = dot(rows[:, :384], weight[0].reshape(WIDTH, 384), ROWS)
        grad = grad + dot(rows[:, 384:], weight[1].reshape(WIDTH, 384), ROWS)
        if j == 0:
            grad = grad + dot(dq[:, :384], weight_query[0].reshape(WIDTH, 384), ROWS)
            grad = grad + dot(dq[:, 384:], weight_query[1].reshape(WIDTH, 384), ROWS)
        unit, _ = normed_of(tok[j].astype(F32))
        gain = jnp.sum(grad * unit, axis=0, keepdims=True)
        offset = jnp.sum(grad, axis=0, keepdims=True)
        sums[0:1, :] = gain if j == 0 else sums[0:1, :] + gain
        sums[1:2, :] = offset if j == 0 else sums[1:2, :] + offset
        if j < 4:
            ring[j] = grad
        else:
            send[j - 4] = grad.astype(BF16)
    columns[...] = sums[...].T.astype(BF16).reshape(16, 48, 128)


def pass_kernel(value, *others):
    pass


def after(value, *earlier):
    return pl.pallas_call(
        pass_kernel,
        out_shape=jax.ShapeDtypeStruct(value.shape, value.dtype),
        in_specs=[ANYWHERE] * (1 + len(earlier)),
        out_specs=ANYWHERE,
        input_output_aliases={0: 0},
    )(value, *earlier)


def shifted(value, axis, steps):
    return lax.ppermute(value, axis, [(i, (i + steps) % 4) for i in range(4)])


def along(value, axis):
    return jnp.stack([value] + [shifted(value, axis, steps) for steps in (1, 2, 3)])


def quad_small(core, xh, vectors, up_bias):
    own = jnp.concatenate(list(vectors) + [jnp.zeros((32,), BF16), up_bias, jnp.zeros((1360,), BF16)])
    own = own.reshape(12, 128)
    pair = ordered(core, own, core_swap(own), 0)
    return ordered(xh, pair, mirror(pair), 0)


def gather_weights(core, xh, place, pieces, small):
    in_weight, out_weight, up_weight, down_weight = pieces
    first = jnp.concatenate([in_weight, out_weight], axis=1)

    def part(which):
        return jnp.concatenate([half_of(first, which, 1), half_of(up_weight, which, 1)], axis=1)

    rows = ordered(core, part(core), core_swap(part(1 - core)), 0)

    def block(which):
        return lax.dynamic_slice_in_dim(rows[:, :1536], which * 384, 384, 1)

    got = mirror(jnp.concatenate([block(3 - place), rows[:, 1536:]], axis=1))
    chunk = ordered(xh, block(place), got[:, :384], 0)
    rest = ordered(xh, rows[:, 1536:], got[:, 384:], 0)
    down = ordered(core, half_of(down_weight, core, 1), core_swap(half_of(down_weight, 1 - core, 1)), 0)
    down = ordered(xh, down, mirror(down), 0)
    packed = jnp.concatenate([rest] + [down[48 * k : 48 * k + 48] for k in range(4)], axis=1)
    mine = lax.all_gather(packed, ("z", "y"), axis=0)
    chunk = along(along(jnp.concatenate([chunk, small], axis=1), "y"), "z")
    small = chunk[:, :, :, 384:].reshape(WIDTH, 128)
    chunk = chunk[:, :, :, :384]
    ring = [chunk] + [ring_shift(chunk, steps) for steps in (1, 2, 3)]
    return mine, small, ring + [core_swap(piece) for piece in ring]


def travel_z(parts):
    return [parts[0]] + [shifted(parts[steps], "z", steps) for steps in (1, 2, 3)]


def exchanged(value, axis):
    return lax.all_to_all(value, axis, 0, 0, tiled=True)


def local(
    tokens,
    cotangent,
    first_gain,
    first_offset,
    in_weight,
    query_bias,
    value_bias,
    out_weight,
    out_bias,
    second_gain,
    second_offset,
    up_weight,
    up_bias,
    down_weight,
    down_bias,
):
    core = lax.axis_index("c")
    xh = lax.axis_index("xh")
    xl = lax.axis_index("xl")
    place = 2 * xh + xl
    own_tokens = tokens.reshape(TOK, WIDTH)
    token_ring = gather_tokens(own_tokens)
    upstream = cotangent.reshape(TOK, WIDTH)
    upstream_half = half_of(upstream, core, 1)
    upstream_far = core_swap(half_of(upstream, 1 - core, 1))
    vectors = (
        first_gain,
        first_offset,
        query_bias,
        value_bias,
        out_bias,
        second_gain,
        second_offset,
        down_bias,
    )
    mine, small, pieces = gather_weights(
        core,
        xh,
        place,
        (in_weight, out_weight, up_weight, down_weight),
        quad_small(core, xh, vectors, up_bias),
    )
    group = jnp.stack(token_ring)
    group = jnp.concatenate([group, core_swap(group)])
    mine = after(mine, small, group, *pieces)
    other = core_swap(mine)

    blocks = []
    for apart in (0, 1):
        for steps in range(4):
            there = (place + 4 - steps) % 4
            blocks.append(((there // 2) * 2 + (core + apart) % 2) * 2 + there % 2)
    meta = jnp.stack(
        [core]
        + [(b < blocks[0]).astype(jnp.int32) for b in blocks[1:]]
        + [place, lax.axis_index("y"), lax.axis_index("z")]
    )

    h1, query, key, value, probs, attended, middle, weights, vec, bias_up = call(
        front_kernel,
        [
            ((8 * TOK, WIDTH), BF16),
            ((TOK, WIDTH), BF16),
            ((8 * TOK, WIDTH), BF16),
            ((8 * TOK, WIDTH), BF16),
            ((6, 8 * TOK, 2 * TOK), BF16),
            ((TOK, WIDTH), BF16),
            ((TOK, WIDTH), F32),
            ((8, 16, 48, 384), BF16),
            ((8, WIDTH), F32),
            ((1, HIDDEN), F32),
        ],
        [
            pltpu.VMEM((8 * TOK, WIDTH), BF16),
            pltpu.VMEM((8 * TOK, WIDTH), BF16),
            pltpu.VMEM((8 * TOK, WIDTH), BF16),
            pltpu.VMEM((6, 8 * TOK, 2 * TOK), BF16),
            pltpu.VMEM((8, 16, 48, 384), BF16),
            pltpu.VMEM((8 * TOK, 2 * TOK), F32),
            pltpu.SemaphoreType.DMA((10,)),
        ],
        [IN_SMEM] + [IN_VMEM] * 10,
        (meta, group, small) + tuple(pieces),
        1000,
        1000,
        (0, 2, 3, 4, 7),
    )
    (
        result,
        act,
        du_keep,
        du_send,
        h2,
        grad_middle,
        da,
        grad_attended,
        small_middle,
        grad_up_bias,
    ) = call(
        middle_kernel,
        [
            ((TOK, WIDTH), BF16),
            ((TOK, HIDDEN), BF16),
            ((TOK, HIDDEN // 2), BF16),
            ((TOK, HIDDEN // 2), BF16),
            ((TOK, WIDTH), BF16),
            ((TOK, WIDTH), F32),
            ((TOK, WIDTH), BF16),
            ((TOK, WIDTH), BF16),
            ((4, WIDTH), F32),
            ((1, HIDDEN), F32),
        ],
        [
            pltpu.VMEM((2, 16, 48, 1536), BF16),
            pltpu.VMEM((2, 16, 4, 48, 384), BF16),
            pltpu.VMEM((2, 16, 48, 384), BF16),
            pltpu.SemaphoreType.DMA((11,)),
        ],
        [IN_SMEM] + [IN_VMEM] * 4 + [ANYWHERE] * 3,
        (meta, middle, upstream, vec, bias_up, mine, other, weights),
        1000,
        1000,
    )
    act_far = core_swap(act)
    du_far = core_swap(du_send)
    rows_far = core_swap(jnp.concatenate([h2, attended, da]))
    grad_query, keep, send, small_attention = call(
        attention_back_kernel,
        [
            ((TOK, WIDTH), BF16),
            ((8 * TOK, WIDTH), BF16),
            ((8 * TOK, WIDTH), BF16),
            ((2, WIDTH), F32),
        ],
        [],
        [IN_SMEM] + [IN_VMEM] * 5,
        (meta, query, key, value, probs, grad_attended),
        10_000_000_000,
        20_000_000,
    )
    first_parts = call(
        feed_grads_kernel,
        [((4, 4, 48, 1536), BF16)] + [((4, 192, 384), BF16)] * 4,
        [
            pltpu.VMEM((16, 48, 1536), BF16),
            pltpu.VMEM((16, 192, 384), BF16),
            pltpu.SemaphoreType.DMA((32,)),
        ],
        [IN_SMEM] + [IN_VMEM] * 8 + [ANYWHERE],
        (
            meta,
            h2,
            rows_far[:TOK],
            du_keep,
            du_far,
            act,
            act_far,
            upstream_half,
            upstream_far,
            grad_query,
        ),
        1000,
        1000,
        range(5),
    )
    first_got = [exchanged(first_parts[0], "y")] + travel_z(first_parts[1:])

    small_rows = jnp.concatenate(
        [
            small_attention,
            small_middle,
            grad_up_bias.reshape(64, 4, 12).transpose(1, 0, 2).reshape(4, WIDTH),
        ]
    )
    got = core_swap(send)
    query_far = core_swap(grad_query)
    total, ring, ring_send, columns = call(
        in_back_kernel,
        [
            ((8 * TOK, WIDTH), BF16),
            ((4, TOK, WIDTH), F32),
            ((4, TOK, WIDTH), BF16),
            ((16, 48, 128), BF16),
        ],
        [
            pltpu.VMEM((TOK, WIDTH), F32),
            pltpu.VMEM((2, 16, 48, 384), BF16),
            pltpu.VMEM((2, 16, 48, 384), BF16),
            pltpu.SemaphoreType.DMA((2,)),
        ],
        [IN_SMEM] + [IN_VMEM] * 5 + [ANYWHERE],
        (meta, keep, got, grad_query, small_rows, group, weights),
        10_000_000_000,
        20_000_000,
    )
    second_parts = call(
        in_grads_kernel,
        [((4, 4, 48, 896), BF16)] + [((4, 96, 384), BF16)] * 4,
        [
            pltpu.VMEM((16, 48, 896), BF16),
            pltpu.VMEM((16, 96, 384), BF16),
            pltpu.SemaphoreType.DMA((32,)),
        ],
        [IN_SMEM] + [IN_VMEM] * 9 + [ANYWHERE] * 3,
        (
            meta,
            h1,
            total,
            attended,
            rows_far[TOK : 2 * TOK],
            da,
            rows_far[2 * TOK :],
            grad_query,
            query_far,
            columns,
            *first_got[2:],
        ),
        10_000_000_000,
        20_000_000,
        range(5),
    )
    second_got = [exchanged(second_parts[0], "y")] + travel_z(second_parts[1:])
    parts = call(
        fold_kernel,
        [((48, 2432), BF16)] * 4 + [((4, 288, 384), BF16)],
        [],
        [IN_SMEM] + [IN_VMEM] * 10,
        [meta] + first_got + second_got,
        1000,
        1000,
    )
    ring = ring + core_swap(ring_send).astype(F32)
    returned = [ring_shift(ring[steps].astype(BF16), -steps) for steps in (1, 2, 3)]
    grad_normed = ring[0] + sum(value.astype(F32) for value in returned)
    parts = [after(parts[0], *returned)] + list(parts[1:])
    (parts,) = call(
        second_fold_kernel,
        [((4, 24, 4736), BF16)],
        [pltpu.VMEM((48, 2432), F32), pltpu.VMEM((288, 384), F32)],
        [IN_VMEM] * 5,
        travel_z(parts) + [exchanged(parts[4], "y")],
        1000,
        1000,
    )
    keep_wide, send_wide, keep_down, send_down = call(
        third_fold_kernel,
        [((12, 3200), F32), ((12, 3200), BF16), ((48, 384), F32), ((48, 384), BF16)],
        [],
        [IN_SMEM, IN_VMEM],
        [meta, exchanged(parts, RING)],
        1000,
        1000,
    )
    up_own, in_own, out_own, down_own, small_own = call(
        finish_kernel,
        [((12, 3072), F32), ((12, 2304), F32), ((12, 768), F32), ((48, 768), F32), ((12, 128), F32)],
        [],
        [IN_SMEM] + [IN_VMEM] * 4,
        (meta, keep_wide, core_swap(send_wide), keep_down, core_swap(send_down)),
        1000,
        1000,
    )
    unit_one, inverse_one = normed_of(own_tokens.astype(F32))
    grad_input = grad_middle + norm_backward(grad_normed, unit_one, inverse_one, vec[0])

    small_own = small_own[:, :12].T
    up_bias_own = small_own[8:].reshape(48)
    return (
        result.reshape(tokens.shape),
        grad_input.astype(BF16).reshape(tokens.shape),
        small_own[0],
        small_own[1],
        in_own,
        small_own[2],
        small_own[3],
        out_own,
        small_own[4],
        small_own[5],
        small_own[6],
        up_own,
        up_bias_own,
        down_own,
        small_own[7],
    )


def solution(mesh):
    fine = Mesh(mesh.devices.reshape(2, 4, 4, 2, 2), ("xl", "z", "y", "xh", "c"))
    tok = P(SHARD, "xl", None, None)
    vec = P(SHARD)
    mat = P(SHARD, None)
    return jax.shard_map(
        local,
        mesh=fine,
        in_specs=(tok, tok, vec, vec, mat, vec, vec, mat, vec, vec, vec, mat, vec, mat, vec),
        out_specs=(tok, tok, vec, vec, mat, vec, vec, mat, vec, vec, vec, mat, vec, mat, vec),
        check_vma=False,
    )
```

```python
import jax
import jax.numpy as jnp
from jax import lax
from jax.experimental import pallas as pl
from jax.experimental.pallas import tpu as pltpu
from jax.sharding import Mesh, PartitionSpec as P

HEAD_DIM = 64
HEADS = 12
WIDTH = 768
HIDDEN = 3072
TOK = 128
RING = ("xl", "xh")
CHIPS = ("xl", "z", "y", "xh")
SHARD = ("z", "y", "xh", "c")
SWAP = [(0, 1), (1, 0)]
F32 = jnp.float32
BF16 = jnp.bfloat16


def ring_index(place):
    return (place % 2) * 2 + place // 2


def ring_shift(value, steps):
    pairs = [(ring_index(i), ring_index((i + steps) % 4)) for i in range(4)]
    return lax.ppermute(value, RING, pairs)


def mirror(value):
    pairs = [(ring_index(i), ring_index(3 - i)) for i in range(4)]
    return lax.ppermute(value, RING, pairs)


def core_swap(value):
    return lax.ppermute(value, "c", SWAP)


def ordered(flag, own, other, axis):
    return jnp.where(
        flag == 0,
        jnp.concatenate([own, other], axis=axis),
        jnp.concatenate([other, own], axis=axis),
    )


def half_of(value, which, axis):
    size = value.shape[axis] // 2
    return lax.dynamic_slice_in_dim(value, which * size, size, axis)


def normed_of(values):
    average = jnp.mean(values, axis=-1, keepdims=True)
    centered = values - average
    inverse = lax.rsqrt(jnp.mean(centered * centered, axis=-1, keepdims=True) + 1e-05)
    return centered * inverse, inverse


def norm_backward(upstream, normed, inverse, norm_gain):
    scaled = upstream * norm_gain
    return inverse * (
        scaled
        - jnp.mean(scaled, axis=-1, keepdims=True)
        - normed * jnp.mean(scaled * normed, axis=-1, keepdims=True)
    )


def gather_tokens(own):
    return [own] + [ring_shift(own, steps) for steps in (1, 2, 3)]


VMEM_LIMIT = 56 * 1024 * 1024


def dot(a, b, dims=((1,), (0,))):
    return lax.dot_general(a, b, (dims, ((), ())), preferred_element_type=F32)


ROWS = ((1,), (1,))


IN_VMEM = pl.BlockSpec(memory_space=pltpu.VMEM)
IN_SMEM = pl.BlockSpec(memory_space=pltpu.SMEM)
ANYWHERE = pl.BlockSpec(memory_space=pl.ANY)


def call(kernel, outs, scratch, specs, args, flops, size, by_hand=()):
    return pl.pallas_call(
        kernel,
        out_specs=[ANYWHERE if n in by_hand else IN_VMEM for n in range(len(outs))],
        out_shape=[jax.ShapeDtypeStruct(shape, kind) for shape, kind in outs],
        in_specs=specs,
        scratch_shapes=scratch,
        compiler_params=pltpu.CompilerParams(vmem_limit_bytes=VMEM_LIMIT),
        cost_estimate=pl.CostEstimate(flops=flops, bytes_accessed=size, transcendentals=0),
    )(*args)


def stacked_heads(pair):
    lane = lax.broadcasted_iota(jnp.int32, pair.shape, 1)
    zero = jnp.zeros_like(pair)
    return jnp.concatenate([jnp.where(lane < 64, pair, zero), jnp.where(lane < 64, zero, pair)])


def merged_heads(rows):
    lane = lax.broadcasted_iota(jnp.int32, (128, 128), 1)
    return jnp.where(lane < 64, rows[:128], rows[128:])


def unpacked_small(meta, packed):
    row_y, row_z = meta[9], meta[10]
    shard = lax.broadcasted_iota(jnp.int32, (64, WIDTH), 0)
    row = lax.broadcasted_iota(jnp.int32, (64, WIDTH), 1)
    far_z = (row_z - shard // 16) & 3
    far_y = (row_y - shard // 4) & 3
    start = (far_z * 4 + far_y) * 48 + 12 * (shard & 3)

    def picked(offset):
        return dot((row == start + offset).astype(BF16), packed).astype(BF16)

    def spread_out(part, size, first):
        count = 64 * size
        lane = lax.broadcasted_iota(jnp.int32, (128, count), 0)
        col = lax.broadcasted_iota(jnp.int32, (128, count), 1)
        wide = dot(part, (lane == first + lax.rem(col, size)).astype(BF16))
        row = lax.broadcasted_iota(jnp.int32, (64, count), 0)
        behind = lax.broadcasted_iota(jnp.int32, (64, count), 1) - size * row
        inside = jnp.logical_and(behind >= 0, behind < size)
        return jnp.sum(jnp.where(inside, wide, 0.0), axis=0, keepdims=True)

    values = picked(0)
    return [spread_out(values, 12, 12 * k) for k in range(8)], spread_out(picked(1), 48, 0)


def front_kernel(
    meta, tok, small, p0, p1, p2, p3, f0, f1, f2, f3,
    h1_out, q, k_out, v_out, p_out, o, mid, weights_out, vec, bias_up,
    h1, k, v, p, weights, bias, sems,
):
    core, place, row_y, row_z = meta[0], meta[8], meta[9], meta[10]
    for far, pieces in enumerate(((p0, p1, p2, p3), (f0, f1, f2, f3))):
        for s, piece in enumerate(pieces):
            block = lax.rem(core + far, 2) * 4 + lax.rem(place + 4 - s, 4)
            for sz in range(4):
                for sy in range(4):
                    zy = lax.rem(row_z + 4 - sz, 4) * 4 + lax.rem(row_y + 4 - sy, 4)
                    weights[block, zy] = piece[sz, sy]
    copies = [pltpu.make_async_copy(weights, weights_out, sems.at[0])]
    copies[0].start()
    rows, up_row = unpacked_small(meta, small[...])
    for index, row in enumerate(rows):
        vec[index : index + 1, :] = row
    bias_up[...] = up_row
    for j in range(8):
        unit, _ = normed_of(tok[j].astype(F32))
        h1[j * TOK : (j + 1) * TOK, :] = (unit * vec[0:1, :] + vec[1:2, :]).astype(BF16)
    copies.append(pltpu.make_async_copy(h1, h1_out, sems.at[1]))
    copies[-1].start()
    key_row = lax.broadcasted_iota(jnp.int32, (TOK, 2 * TOK), 0)
    query_col = lax.rem(lax.broadcasted_iota(jnp.int32, (TOK, 2 * TOK), 1), TOK)
    bias[0:TOK, :] = jnp.where(key_row <= query_col, 0.0, -1e30)
    for j in range(1, 8):
        shown = meta[j] > 0
        bias[j * TOK : (j + 1) * TOK, :] = jnp.full((TOK, 2 * TOK), jnp.where(shown, 0.0, -1e30), F32)
    for n in range(2):
        cols = slice(n * 384, (n + 1) * 384)
        q[:, cols] = (
            dot(h1[0:TOK, :], weights[n].reshape(WIDTH, 384)) + vec[2:3, cols]
        ).astype(BF16)
        weight_key = weights[2 + n].reshape(WIDTH, 384)
        weight_value = weights[4 + n].reshape(WIDTH, 384)
        for j in range(4):
            rows = slice(j * 256, (j + 1) * 256)
            k[rows, cols] = dot(h1[rows, :], weight_key).astype(BF16)
            v[rows, cols] = (dot(h1[rows, :], weight_value) + vec[3:4, cols]).astype(BF16)
    copies.append(pltpu.make_async_copy(k, k_out, sems.at[2]))
    copies.append(pltpu.make_async_copy(v, v_out, sems.at[3]))
    copies[-2].start()
    copies[-1].start()
    for pair in range(6):
        lanes = slice(pair * 128, (pair + 1) * 128)
        scores = dot(k[:, lanes], stacked_heads(q[:, lanes]), ROWS) * 0.125 + bias[...]
        exponent = jnp.exp(scores - jnp.max(scores, axis=0, keepdims=True))
        probs = exponent * (1.0 / jnp.sum(exponent, axis=0, keepdims=True))
        low = probs.astype(BF16)
        p[pair] = low
        copies.append(pltpu.make_async_copy(p.at[pair], p_out.at[pair], sems.at[4 + pair]))
        copies[-1].start()
        attended = dot(v[:, lanes].T, low)
        o[:, lanes] = merged_heads(attended.T).astype(BF16)
    for n in range(2):
        cols = slice(n * 384, (n + 1) * 384)
        mid[:, cols] = (
            tok[0, :, cols].astype(F32)
            + dot(o[...], weights[6 + n].reshape(WIDTH, 384))
            + vec[4:5, cols]
        )
    for copy in copies:
        copy.wait()


def middle_kernel(
    meta, mid, dy, vec, bias_up, mine, other, weights,
    result, act, du_keep, du_send, h2, dmid, da, dattended, small, up_bias_grad,
    up, down, weight_out, sems,
):
    core = meta[0]
    far = 1 - core
    copies = [
        pltpu.make_async_copy(mine.at[:, :, pl.ds(0, 1536)], up.at[core], sems.at[0]),
        pltpu.make_async_copy(other.at[:, :, pl.ds(0, 1536)], up.at[far], sems.at[1]),
        pltpu.make_async_copy(weights.at[pl.ds(6, 2)], weight_out, sems.at[10]),
    ]
    for g in range(4):
        cols = pl.ds(1536 + 384 * g, 384)
        copies.append(
            pltpu.make_async_copy(mine.at[:, :, cols], down.at[core, :, g], sems.at[2 + g])
        )
        copies.append(
            pltpu.make_async_copy(other.at[:, :, cols], down.at[far, :, g], sems.at[6 + g])
        )
    for copy in copies:
        copy.start()
    unit, inverse = normed_of(mid[...])
    h2[...] = (unit * vec[5:6, :] + vec[6:7, :]).astype(BF16)
    for copy in copies[:3]:
        copy.wait()
    low = dy[...]
    outcome = [mid[:, 384 * n : 384 * n + 384] + vec[7:8, 384 * n : 384 * n + 384] for n in range(2)]
    dh2 = None
    for half in range(2):
        cols = slice(half * 1536, (half + 1) * 1536)
        wide = up[half].reshape(WIDTH, 1536)
        u = dot(h2[...], wide) + bias_up[:, cols]
        cube = 0.7978845608028654 * (u + 0.044715 * u * u * u)
        tanh = jnp.tanh(cube)
        low_act = (0.5 * u * (1.0 + tanh)).astype(BF16)
        act[:, cols] = low_act
        slope_half = 0.5 * (1.0 + tanh) + 0.5 * u * (1.0 - tanh * tanh) * 0.7978845608028654 * (
            1.0 + 3.0 * 0.044715 * u * u
        )
        grad_act = None
        if half == 0:
            for copy in copies[3:]:
                copy.wait()
        for n in range(2):
            rows = down[n, half * 8 : half * 8 + 8].reshape(1536, 384)
            outcome[n] = outcome[n] + dot(low_act, rows)
            term = dot(low[:, 384 * n : 384 * n + 384], rows, ROWS)
            grad_act = term if grad_act is None else grad_act + term
        du = (grad_act * slope_half).astype(BF16)
        up_bias_grad[:, cols] = jnp.sum(du.astype(F32), axis=0, keepdims=True)

        @pl.when(core == half)
        def _():
            du_keep[...] = du

        @pl.when(core != half)
        def _():
            du_send[...] = du

        term = dot(du, wide, ROWS)
        dh2 = term if dh2 is None else dh2 + term
    for n in range(2):
        result[:, 384 * n : 384 * n + 384] = outcome[n].astype(BF16)
    upstream = low.astype(F32)
    dm = upstream + norm_backward(dh2, unit, inverse, vec[5:6, :])
    dmid[...] = dm
    branch = dm.astype(BF16)
    da[...] = branch
    small[0:1, :] = jnp.sum(branch.astype(F32), axis=0, keepdims=True)
    small[1:2, :] = jnp.sum(dh2 * unit, axis=0, keepdims=True)
    small[2:3, :] = jnp.sum(dh2, axis=0, keepdims=True)
    small[3:4, :] = jnp.sum(upstream, axis=0, keepdims=True)
    grad = dot(branch[:, :384], weight_out[0].reshape(WIDTH, 384), ROWS)
    grad = grad + dot(branch[:, 384:], weight_out[1].reshape(WIDTH, 384), ROWS)
    dattended[...] = grad.astype(BF16)


def attention_back_kernel(meta, q, k, v, p, do, dq, keep, send, biases):
    first = meta[0] == 0
    for pair in range(6):
        lanes = slice(pair * 128, (pair + 1) * 128)
        upstream = stacked_heads(do[:, lanes])
        keys = k[:, lanes]
        low = p[pair]
        probs = low.astype(F32)
        dprobs = dot(v[:, lanes], upstream, ROWS)
        inner = jnp.sum(probs * dprobs, axis=0, keepdims=True)
        dscores = (probs * (dprobs - inner)).astype(BF16)
        dk = dot(dscores, stacked_heads(q[:, lanes])) * 0.125
        dv = dot(low, upstream)
        low_dq = (merged_heads(dot(keys.T, dscores).T) * 0.125).astype(BF16)
        dq[:, lanes] = low_dq
        biases[0:1, lanes] = jnp.sum(low_dq.astype(F32), axis=0, keepdims=True)
        biases[1:2, lanes] = jnp.sum(dv, axis=0, keepdims=True)
        keep[:, lanes] = jnp.where(first, dk, dv).astype(BF16)
        send[:, lanes] = jnp.where(first, dv, dk).astype(BF16)


def relative(base, steps):
    return lax.rem(base + steps, 4)


def copies_by_y(meta, rows, out, sems):
    return [
        pltpu.make_async_copy(
            rows.at[relative(meta[10], t) * 4 + y], out.at[y, t], sems.at[4 * y + t]
        )
        for y in range(4)
        for t in range(4)
    ]


def copies_by_z(meta, rows, outs, sems):
    return [
        pltpu.make_async_copy(
            rows.at[relative(meta[10], s) * 4 + relative(meta[9], t)],
            outs[s].at[t],
            sems.at[16 + 4 * s + t],
        )
        for s in range(4)
        for t in range(4)
    ]


def feed_grads_kernel(
    meta, h2, h2_far, du, du_far, act, act_far, dy, dy_far, h1, o, o_far, da, da_far, dq, dq_far, *refs
):
    by_y, by_z, (up_grad, down_grad, sems) = refs[0], refs[1:5], refs[5:]
    lhs = jnp.concatenate([h2[...], h2_far[...]]).T
    for n in range(4):
        cols = slice(n * 384, (n + 1) * 384)
        grad = dot(lhs, jnp.concatenate([du[:, cols], du_far[:, cols]])).astype(BF16)
        up_grad[:, :, cols] = grad.reshape(16, 48, 384)
    first = meta[0] == 0
    lhs = jnp.where(
        first,
        jnp.concatenate([h1[0:TOK, :], h1[4 * TOK : 5 * TOK, :]]).astype(F32),
        jnp.concatenate([o[...], o_far[...]]).astype(F32),
    ).astype(BF16).T
    rhs = jnp.where(
        first,
        jnp.concatenate([dq[...], dq_far[...]]).astype(F32),
        jnp.concatenate([da[...], da_far[...]]).astype(F32),
    ).astype(BF16)
    up_grad[:, :, 1536:1920] = dot(lhs, rhs[:, :384]).astype(BF16).reshape(16, 48, 384)
    copies = copies_by_y(meta, up_grad, by_y, sems)
    for copy in copies:
        copy.start()
    down_grad[:, 192:240, :] = dot(lhs, rhs[:, 384:]).astype(BF16).reshape(16, 48, 384)
    rhs = jnp.concatenate([dy[...], dy_far[...]])
    for n in range(4):
        cols = slice(n * 768, (n + 1) * 768)
        lhs = jnp.concatenate([act[:, cols], act_far[:, cols]]).T
        down_grad[4 * n : 4 * n + 4, 0:192, :] = dot(lhs, rhs).astype(BF16).reshape(4, 192, 384)
    more = copies_by_z(meta, down_grad, by_z, sems)
    for copy in more:
        copy.start()
    for copy in copies + more:
        copy.wait()


def summed(pieces, index):
    total = pieces[0][index].astype(F32)
    for piece in pieces[1:]:
        total = total + piece[index].astype(F32)
    return total


def fold_kernel(meta, up, down0, down1, down2, down3, first, second0, second1, second2, second3, *outs):
    down, second = (down0, down1, down2, down3), (second0, second1, second2, second3)
    for s in range(4):
        sources = range(4)
        outs[s][:, 0:1920] = sum(up[n, s].astype(F32) for n in sources).astype(BF16)
        outs[s][:, 1920:2432] = sum(first[n, s].astype(F32) for n in sources).astype(BF16)
        y = relative(meta[9], s)
        outs[4][y, 0:240, :] = summed(down, s).astype(BF16)
        outs[4][y, 240:288, :] = summed(second, s).astype(BF16)


def second_fold_kernel(w0, w1, w2, w3, tall, out, wide_sum, tall_sum):
    wide_sum[...] = summed((w0, w1, w2, w3), ...)
    tall_sum[...] = sum(tall[n].astype(F32) for n in range(4))
    for place in range(4):
        half, index = place // 2, ring_index(place)
        rows = slice(24 * half, 24 * half + 24)
        out[index, :, 0:2304] = wide_sum[rows, 0:2304].astype(BF16)
        out[index, :, 4608:4736] = wide_sum[rows, 2304:2432].astype(BF16)
        for n in range(2):
            start = 192 + 48 * n + 24 * half
            out[index, :, 2304 + 384 * n : 2688 + 384 * n] = tall_sum[start : start + 24, :].astype(BF16)
        for n in range(4):
            start = 96 * half + 24 * n
            out[index, :, 3072 + 384 * n : 3456 + 384 * n] = tall_sum[start : start + 24, :].astype(BF16)


def third_fold_kernel(meta, parts, keep_wide, send_wide, keep_down, send_down):
    total = sum(parts[n].astype(F32) for n in range(4))

    def part(which):
        down = total[:, 3072 + 768 * which : 3840 + 768 * which]
        return (
            jnp.concatenate([total[12 * which : 12 * which + 12, 0:3072], total[12 * which : 12 * which + 12, 4608:4736]], axis=1),
            jnp.concatenate([down[:, :384], down[:, 384:]]),
        )

    for core in range(2):

        @pl.when(meta[0] == core)
        def _():
            keep_wide[...], keep_down[...] = part(core)
            wide, down = part(1 - core)
            send_wide[...] = wide.astype(BF16)
            send_down[...] = down.astype(BF16)


def finish_kernel(meta, keep_wide, got_wide, keep_down, got_down, up, in_grad, out_grad, down, small):
    small[...] = keep_wide[:, 3072:3200] + got_wide[:, 3072:3200].astype(F32)
    for core in range(2):

        @pl.when(meta[0] == core)
        def _():
            wide = [keep_wide[...], got_wide[...].astype(F32)]
            tall = [keep_down[...], got_down[...].astype(F32)]
            if core == 1:
                wide, tall = wide[::-1], tall[::-1]
            up[:, 0:1536] = wide[0][:, 0:1536]
            up[:, 1536:3072] = wide[1][:, 0:1536]
            in_grad[:, 0:384] = wide[0][:, 1536:1920]
            in_grad[:, 384:768] = wide[0][:, 2304:2688]
            in_grad[:, 768:1152] = wide[0][:, 1920:2304]
            in_grad[:, 1152:1536] = wide[0][:, 2688:3072]
            in_grad[:, 1536:1920] = wide[1][:, 1920:2304]
            in_grad[:, 1920:2304] = wide[1][:, 2688:3072]
            out_grad[:, 0:384] = wide[1][:, 1536:1920]
            out_grad[:, 384:768] = wide[1][:, 2304:2688]
            down[:, 0:384] = tall[0]
            down[:, 384:768] = tall[1]


def in_grads_kernel(meta, h1, total, columns, *refs):
    by_y, by_z, (grads_y, grads_z, sems) = refs[-8], refs[-7:-3], refs[-3:]
    lhs = h1[...].T
    grads_y[:, :, 0:384] = dot(lhs, total[:, 0:384]).astype(BF16).reshape(16, 48, 384)
    grads_y[:, :, 384:512] = columns[...]
    copies = copies_by_y(meta, grads_y, by_y, sems)
    for copy in copies:
        copy.start()
    grads_z[...] = dot(lhs, total[:, 384:768]).astype(BF16).reshape(16, 48, 384)
    more = copies_by_z(meta, grads_z, by_z, sems)
    for copy in more:
        copy.start()
    for copy in copies + more:
        copy.wait()


def in_back_kernel(
    meta, keep, got, dq, small, tok, weights, total, ring, send, columns, sums, weight, weight_query, sems
):
    copies = [
        pltpu.make_async_copy(weights.at[pl.ds(0, 2)], weight_query, sems.at[0]),
        pltpu.make_async_copy(weights.at[pl.ds(2 + 2 * meta[0], 2)], weight, sems.at[1]),
    ]
    for copy in copies:
        copy.start()
    sums[...] = jnp.zeros_like(sums)
    sums[2:12, :] = small[...]
    for copy in copies:
        copy.wait()
    for j in range(8):
        there = (j + 4) % 8
        rows = (
            keep[j * TOK : (j + 1) * TOK, :].astype(F32)
            + got[there * TOK : (there + 1) * TOK, :].astype(F32)
        ).astype(BF16)
        total[j * TOK : (j + 1) * TOK, :] = rows
        grad = dot(rows[:, :384], weight[0].reshape(WIDTH, 384), ROWS)
        grad = grad + dot(rows[:, 384:], weight[1].reshape(WIDTH, 384), ROWS)
        if j == 0:
            grad = grad + dot(dq[:, :384], weight_query[0].reshape(WIDTH, 384), ROWS)
            grad = grad + dot(dq[:, 384:], weight_query[1].reshape(WIDTH, 384), ROWS)
        unit, _ = normed_of(tok[j].astype(F32))
        gain = jnp.sum(grad * unit, axis=0, keepdims=True)
        offset = jnp.sum(grad, axis=0, keepdims=True)
        sums[0:1, :] = gain if j == 0 else sums[0:1, :] + gain
        sums[1:2, :] = offset if j == 0 else sums[1:2, :] + offset
        if j < 4:
            ring[j] = grad
        else:
            send[j - 4] = grad.astype(BF16)
    columns[...] = sums[...].T.astype(BF16).reshape(16, 48, 128)


def pass_kernel(value, *others):
    pass


def after(value, *earlier):
    return pl.pallas_call(
        pass_kernel,
        out_shape=jax.ShapeDtypeStruct(value.shape, value.dtype),
        in_specs=[ANYWHERE] * (1 + len(earlier)),
        out_specs=ANYWHERE,
        input_output_aliases={0: 0},
    )(value, *earlier)


def shifted(value, axis, steps):
    return lax.ppermute(value, axis, [(i, (i + steps) % 4) for i in range(4)])


def along(value, axis):
    return jnp.stack([value] + [shifted(value, axis, steps) for steps in (1, 2, 3)])


def quad_small(core, xh, vectors, up_bias):
    own = jnp.concatenate(list(vectors) + [jnp.zeros((32,), BF16), up_bias, jnp.zeros((1360,), BF16)])
    own = own.reshape(12, 128)
    pair = ordered(core, own, core_swap(own), 0)
    return ordered(xh, pair, mirror(pair), 0)


def gather_weights(core, xh, place, pieces, small):
    in_weight, out_weight, up_weight, down_weight = pieces
    first = jnp.concatenate([in_weight, out_weight], axis=1)

    def part(which):
        return jnp.concatenate([half_of(first, which, 1), half_of(up_weight, which, 1)], axis=1)

    rows = ordered(core, part(core), core_swap(part(1 - core)), 0)

    def block(which):
        return lax.dynamic_slice_in_dim(rows[:, :1536], which * 384, 384, 1)

    got = mirror(jnp.concatenate([block(3 - place), rows[:, 1536:]], axis=1))
    chunk = ordered(xh, block(place), got[:, :384], 0)
    rest = ordered(xh, rows[:, 1536:], got[:, 384:], 0)
    down = ordered(core, half_of(down_weight, core, 1), core_swap(half_of(down_weight, 1 - core, 1)), 0)
    down = ordered(xh, down, mirror(down), 0)
    packed = jnp.concatenate([rest] + [down[48 * k : 48 * k + 48] for k in range(4)], axis=1)
    mine = lax.all_gather(packed, ("z", "y"), axis=0)
    chunk = along(along(jnp.concatenate([chunk, small], axis=1), "y"), "z")
    small = chunk[:, :, :, 384:].reshape(WIDTH, 128)
    chunk = chunk[:, :, :, :384]
    ring = [chunk] + [ring_shift(chunk, steps) for steps in (1, 2, 3)]
    return mine, small, ring + [core_swap(piece) for piece in ring]


def travel_z(parts):
    return [parts[0]] + [shifted(parts[steps], "z", steps) for steps in (1, 2, 3)]


def exchanged(value, axis):
    return lax.all_to_all(value, axis, 0, 0, tiled=True)


def local(
    tokens,
    cotangent,
    first_gain,
    first_offset,
    in_weight,
    query_bias,
    value_bias,
    out_weight,
    out_bias,
    second_gain,
    second_offset,
    up_weight,
    up_bias,
    down_weight,
    down_bias,
):
    core = lax.axis_index("c")
    xh = lax.axis_index("xh")
    xl = lax.axis_index("xl")
    place = 2 * xh + xl
    own_tokens = tokens.reshape(TOK, WIDTH)
    token_ring = gather_tokens(own_tokens)
    upstream = cotangent.reshape(TOK, WIDTH)
    upstream_half = half_of(upstream, core, 1)
    upstream_far = core_swap(half_of(upstream, 1 - core, 1))
    vectors = (
        first_gain,
        first_offset,
        query_bias,
        value_bias,
        out_bias,
        second_gain,
        second_offset,
        down_bias,
    )
    mine, small, pieces = gather_weights(
        core,
        xh,
        place,
        (in_weight, out_weight, up_weight, down_weight),
        quad_small(core, xh, vectors, up_bias),
    )
    group = jnp.stack(token_ring)
    group = jnp.concatenate([group, core_swap(group)])
    mine = after(mine, small, group, *pieces)
    other = core_swap(mine)

    blocks = []
    for apart in (0, 1):
        for steps in range(4):
            there = (place + 4 - steps) % 4
            blocks.append(((there // 2) * 2 + (core + apart) % 2) * 2 + there % 2)
    meta = jnp.stack(
        [core]
        + [(b < blocks[0]).astype(jnp.int32) for b in blocks[1:]]
        + [place, lax.axis_index("y"), lax.axis_index("z")]
    )

    h1, query, key, value, probs, attended, middle, weights, vec, bias_up = call(
        front_kernel,
        [
            ((8 * TOK, WIDTH), BF16),
            ((TOK, WIDTH), BF16),
            ((8 * TOK, WIDTH), BF16),
            ((8 * TOK, WIDTH), BF16),
            ((6, 8 * TOK, 2 * TOK), BF16),
            ((TOK, WIDTH), BF16),
            ((TOK, WIDTH), F32),
            ((8, 16, 48, 384), BF16),
            ((8, WIDTH), F32),
            ((1, HIDDEN), F32),
        ],
        [
            pltpu.VMEM((8 * TOK, WIDTH), BF16),
            pltpu.VMEM((8 * TOK, WIDTH), BF16),
            pltpu.VMEM((8 * TOK, WIDTH), BF16),
            pltpu.VMEM((6, 8 * TOK, 2 * TOK), BF16),
            pltpu.VMEM((8, 16, 48, 384), BF16),
            pltpu.VMEM((8 * TOK, 2 * TOK), F32),
            pltpu.SemaphoreType.DMA((10,)),
        ],
        [IN_SMEM] + [IN_VMEM] * 10,
        (meta, group, small) + tuple(pieces),
        1000,
        1000,
        (0, 2, 3, 4, 7),
    )
    (
        result,
        act,
        du_keep,
        du_send,
        h2,
        grad_middle,
        da,
        grad_attended,
        small_middle,
        grad_up_bias,
    ) = call(
        middle_kernel,
        [
            ((TOK, WIDTH), BF16),
            ((TOK, HIDDEN), BF16),
            ((TOK, HIDDEN // 2), BF16),
            ((TOK, HIDDEN // 2), BF16),
            ((TOK, WIDTH), BF16),
            ((TOK, WIDTH), F32),
            ((TOK, WIDTH), BF16),
            ((TOK, WIDTH), BF16),
            ((4, WIDTH), F32),
            ((1, HIDDEN), F32),
        ],
        [
            pltpu.VMEM((2, 16, 48, 1536), BF16),
            pltpu.VMEM((2, 16, 4, 48, 384), BF16),
            pltpu.VMEM((2, 16, 48, 384), BF16),
            pltpu.SemaphoreType.DMA((11,)),
        ],
        [IN_SMEM] + [IN_VMEM] * 4 + [ANYWHERE] * 3,
        (meta, middle, upstream, vec, bias_up, mine, other, weights),
        1000,
        1000,
    )
    act_far = core_swap(act)
    du_far = core_swap(du_send)
    rows_far = core_swap(jnp.concatenate([h2, attended, da]))
    grad_query, keep, send, small_attention = call(
        attention_back_kernel,
        [
            ((TOK, WIDTH), BF16),
            ((8 * TOK, WIDTH), BF16),
            ((8 * TOK, WIDTH), BF16),
            ((2, WIDTH), F32),
        ],
        [],
        [IN_SMEM] + [IN_VMEM] * 5,
        (meta, query, key, value, probs, grad_attended),
        10_000_000_000,
        20_000_000,
    )
    query_far = core_swap(grad_query)
    first_parts = call(
        feed_grads_kernel,
        [((4, 4, 48, 1920), BF16)] + [((4, 240, 384), BF16)] * 4,
        [
            pltpu.VMEM((16, 48, 1920), BF16),
            pltpu.VMEM((16, 240, 384), BF16),
            pltpu.SemaphoreType.DMA((32,)),
        ],
        [IN_SMEM] + [IN_VMEM] * 15,
        (
            meta,
            h2,
            rows_far[:TOK],
            du_keep,
            du_far,
            act,
            act_far,
            upstream_half,
            upstream_far,
            h1,
            attended,
            rows_far[TOK : 2 * TOK],
            da,
            rows_far[2 * TOK :],
            grad_query,
            query_far,
        ),
        1000,
        1000,
        range(5),
    )
    first_got = [exchanged(first_parts[0], "y")] + travel_z(first_parts[1:])

    small_rows = jnp.concatenate(
        [
            small_attention,
            small_middle,
            grad_up_bias.reshape(64, 4, 12).transpose(1, 0, 2).reshape(4, WIDTH),
        ]
    )
    got = core_swap(send)
    total, ring, ring_send, columns = call(
        in_back_kernel,
        [
            ((8 * TOK, WIDTH), BF16),
            ((4, TOK, WIDTH), F32),
            ((4, TOK, WIDTH), BF16),
            ((16, 48, 128), BF16),
        ],
        [
            pltpu.VMEM((TOK, WIDTH), F32),
            pltpu.VMEM((2, 16, 48, 384), BF16),
            pltpu.VMEM((2, 16, 48, 384), BF16),
            pltpu.SemaphoreType.DMA((2,)),
        ],
        [IN_SMEM] + [IN_VMEM] * 5 + [ANYWHERE],
        (meta, keep, got, grad_query, small_rows, group, weights),
        10_000_000_000,
        20_000_000,
    )
    second_parts = call(
        in_grads_kernel,
        [((4, 4, 48, 512), BF16)] + [((4, 48, 384), BF16)] * 4,
        [
            pltpu.VMEM((16, 48, 512), BF16),
            pltpu.VMEM((16, 48, 384), BF16),
            pltpu.SemaphoreType.DMA((32,)),
        ],
        [IN_SMEM] + [IN_VMEM] * 3 + [ANYWHERE] * 4,
        (meta, h1, total, columns, first_got[0], *first_got[2:]),
        10_000_000_000,
        20_000_000,
        range(5),
    )
    second_got = [exchanged(second_parts[0], "y")] + travel_z(second_parts[1:])
    parts = call(
        fold_kernel,
        [((48, 2432), BF16)] * 4 + [((4, 288, 384), BF16)],
        [],
        [IN_SMEM] + [IN_VMEM] * 10,
        [meta] + first_got + second_got,
        1000,
        1000,
    )
    ring = ring + core_swap(ring_send).astype(F32)
    returned = [ring_shift(ring[steps].astype(BF16), -steps) for steps in (1, 2, 3)]
    grad_normed = ring[0] + sum(value.astype(F32) for value in returned)
    parts = [after(parts[0], *returned)] + list(parts[1:])
    (parts,) = call(
        second_fold_kernel,
        [((4, 24, 4736), BF16)],
        [pltpu.VMEM((48, 2432), F32), pltpu.VMEM((288, 384), F32)],
        [IN_VMEM] * 5,
        travel_z(parts) + [exchanged(parts[4], "y")],
        1000,
        1000,
    )
    keep_wide, send_wide, keep_down, send_down = call(
        third_fold_kernel,
        [((12, 3200), F32), ((12, 3200), BF16), ((48, 384), F32), ((48, 384), BF16)],
        [],
        [IN_SMEM, IN_VMEM],
        [meta, exchanged(parts, RING)],
        1000,
        1000,
    )
    up_own, in_own, out_own, down_own, small_own = call(
        finish_kernel,
        [((12, 3072), F32), ((12, 2304), F32), ((12, 768), F32), ((48, 768), F32), ((12, 128), F32)],
        [],
        [IN_SMEM] + [IN_VMEM] * 4,
        (meta, keep_wide, core_swap(send_wide), keep_down, core_swap(send_down)),
        1000,
        1000,
    )
    unit_one, inverse_one = normed_of(own_tokens.astype(F32))
    grad_input = grad_middle + norm_backward(grad_normed, unit_one, inverse_one, vec[0])

    small_own = small_own[:, :12].T
    up_bias_own = small_own[8:].reshape(48)
    return (
        result.reshape(tokens.shape),
        grad_input.astype(BF16).reshape(tokens.shape),
        small_own[0],
        small_own[1],
        in_own,
        small_own[2],
        small_own[3],
        out_own,
        small_own[4],
        small_own[5],
        small_own[6],
        up_own,
        up_bias_own,
        down_own,
        small_own[7],
    )


def solution(mesh):
    fine = Mesh(mesh.devices.reshape(2, 4, 4, 2, 2), ("xl", "z", "y", "xh", "c"))
    tok = P(SHARD, "xl", None, None)
    vec = P(SHARD)
    mat = P(SHARD, None)
    return jax.shard_map(
        local,
        mesh=fine,
        in_specs=(tok, tok, vec, vec, mat, vec, vec, mat, vec, vec, vec, mat, vec, mat, vec),
        out_specs=(tok, tok, vec, vec, mat, vec, vec, mat, vec, vec, vec, mat, vec, mat, vec),
        check_vma=False,
    )
```

```python
import jax
import jax.numpy as jnp
from jax import lax
from jax.experimental import pallas as pl
from jax.experimental.pallas import tpu as pltpu
from jax.sharding import Mesh, PartitionSpec as P

HEAD_DIM = 64
HEADS = 12
WIDTH = 768
HIDDEN = 3072
TOK = 128
RING = ("xl", "xh")
CHIPS = ("xl", "z", "y", "xh")
SHARD = ("z", "y", "xh", "c")
SWAP = [(0, 1), (1, 0)]
F32 = jnp.float32
BF16 = jnp.bfloat16


def ring_index(place):
    return (place % 2) * 2 + place // 2


def ring_shift(value, steps):
    pairs = [(ring_index(i), ring_index((i + steps) % 4)) for i in range(4)]
    return lax.ppermute(value, RING, pairs)


def mirror(value):
    pairs = [(ring_index(i), ring_index(3 - i)) for i in range(4)]
    return lax.ppermute(value, RING, pairs)


def core_swap(value):
    return lax.ppermute(value, "c", SWAP)


def ordered(flag, own, other, axis):
    return jnp.where(
        flag == 0,
        jnp.concatenate([own, other], axis=axis),
        jnp.concatenate([other, own], axis=axis),
    )


def half_of(value, which, axis):
    size = value.shape[axis] // 2
    return lax.dynamic_slice_in_dim(value, which * size, size, axis)


def normed_of(values):
    average = jnp.mean(values, axis=-1, keepdims=True)
    centered = values - average
    inverse = lax.rsqrt(jnp.mean(centered * centered, axis=-1, keepdims=True) + 1e-05)
    return centered * inverse, inverse


def norm_backward(upstream, normed, inverse, norm_gain):
    scaled = upstream * norm_gain
    return inverse * (
        scaled
        - jnp.mean(scaled, axis=-1, keepdims=True)
        - normed * jnp.mean(scaled * normed, axis=-1, keepdims=True)
    )


def gather_tokens(own):
    return [own] + [ring_shift(own, steps) for steps in (1, 2, 3)]


VMEM_LIMIT = 56 * 1024 * 1024


def dot(a, b, dims=((1,), (0,))):
    return lax.dot_general(a, b, (dims, ((), ())), preferred_element_type=F32)


ROWS = ((1,), (1,))


IN_VMEM = pl.BlockSpec(memory_space=pltpu.VMEM)
IN_SMEM = pl.BlockSpec(memory_space=pltpu.SMEM)
ANYWHERE = pl.BlockSpec(memory_space=pl.ANY)


def call(kernel, outs, scratch, specs, args, flops, size, by_hand=()):
    return pl.pallas_call(
        kernel,
        out_specs=[ANYWHERE if n in by_hand else IN_VMEM for n in range(len(outs))],
        out_shape=[jax.ShapeDtypeStruct(shape, kind) for shape, kind in outs],
        in_specs=specs,
        scratch_shapes=scratch,
        compiler_params=pltpu.CompilerParams(vmem_limit_bytes=VMEM_LIMIT),
        cost_estimate=pl.CostEstimate(flops=flops, bytes_accessed=size, transcendentals=0),
    )(*args)


def stacked_heads(pair):
    lane = lax.broadcasted_iota(jnp.int32, pair.shape, 1)
    zero = jnp.zeros_like(pair)
    return jnp.concatenate([jnp.where(lane < 64, pair, zero), jnp.where(lane < 64, zero, pair)])


def merged_heads(rows):
    lane = lax.broadcasted_iota(jnp.int32, (128, 128), 1)
    return jnp.where(lane < 64, rows[:128], rows[128:])


def unpacked_small(meta, packed):
    row_y, row_z = meta[9], meta[10]
    shard = lax.broadcasted_iota(jnp.int32, (64, WIDTH), 0)
    row = lax.broadcasted_iota(jnp.int32, (64, WIDTH), 1)
    far_z = (row_z - shard // 16) & 3
    far_y = (row_y - shard // 4) & 3
    start = (far_z * 4 + far_y) * 48 + 12 * (shard & 3)

    def picked(offset):
        return dot((row == start + offset).astype(BF16), packed).astype(BF16)

    def spread_out(part, size, first):
        count = 64 * size
        lane = lax.broadcasted_iota(jnp.int32, (128, count), 0)
        col = lax.broadcasted_iota(jnp.int32, (128, count), 1)
        wide = dot(part, (lane == first + lax.rem(col, size)).astype(BF16))
        row = lax.broadcasted_iota(jnp.int32, (64, count), 0)
        behind = lax.broadcasted_iota(jnp.int32, (64, count), 1) - size * row
        inside = jnp.logical_and(behind >= 0, behind < size)
        return jnp.sum(jnp.where(inside, wide, 0.0), axis=0, keepdims=True)

    values = picked(0)
    return [spread_out(values, 12, 12 * k) for k in range(8)], spread_out(picked(1), 48, 0)


def front_kernel(
    meta, tok, small, p0, p1, p2, p3, f0, f1, f2, f3,
    h1_out, q, k_out, v_out, p_out, o, mid, weights_out, vec, bias_up,
    h1, k, v, p, weights, bias, sems,
):
    core, place, row_y, row_z = meta[0], meta[8], meta[9], meta[10]
    for far, pieces in enumerate(((p0, p1, p2, p3), (f0, f1, f2, f3))):
        for s, piece in enumerate(pieces):
            block = lax.rem(core + far, 2) * 4 + lax.rem(place + 4 - s, 4)
            for sz in range(4):
                for sy in range(4):
                    zy = lax.rem(row_z + 4 - sz, 4) * 4 + lax.rem(row_y + 4 - sy, 4)
                    weights[block, zy] = piece[sz, sy]
    copies = [pltpu.make_async_copy(weights, weights_out, sems.at[0])]
    copies[0].start()
    rows, up_row = unpacked_small(meta, small[...])
    for index, row in enumerate(rows):
        vec[index : index + 1, :] = row
    bias_up[...] = up_row
    for j in range(8):
        unit, _ = normed_of(tok[j].astype(F32))
        h1[j * TOK : (j + 1) * TOK, :] = (unit * vec[0:1, :] + vec[1:2, :]).astype(BF16)
    copies.append(pltpu.make_async_copy(h1, h1_out, sems.at[1]))
    copies[-1].start()
    key_row = lax.broadcasted_iota(jnp.int32, (TOK, 2 * TOK), 0)
    query_col = lax.rem(lax.broadcasted_iota(jnp.int32, (TOK, 2 * TOK), 1), TOK)
    bias[0:TOK, :] = jnp.where(key_row <= query_col, 0.0, -1e30)
    for j in range(1, 8):
        shown = meta[j] > 0
        bias[j * TOK : (j + 1) * TOK, :] = jnp.full((TOK, 2 * TOK), jnp.where(shown, 0.0, -1e30), F32)
    for n in range(2):
        cols = slice(n * 384, (n + 1) * 384)
        q[:, cols] = (
            dot(h1[0:TOK, :], weights[n].reshape(WIDTH, 384)) + vec[2:3, cols]
        ).astype(BF16)
        weight_key = weights[2 + n].reshape(WIDTH, 384)
        weight_value = weights[4 + n].reshape(WIDTH, 384)
        for j in range(4):
            rows = slice(j * 256, (j + 1) * 256)
            k[rows, cols] = dot(h1[rows, :], weight_key).astype(BF16)
            v[rows, cols] = (dot(h1[rows, :], weight_value) + vec[3:4, cols]).astype(BF16)
    copies.append(pltpu.make_async_copy(k, k_out, sems.at[2]))
    copies.append(pltpu.make_async_copy(v, v_out, sems.at[3]))
    copies[-2].start()
    copies[-1].start()
    for pair in range(6):
        lanes = slice(pair * 128, (pair + 1) * 128)
        scores = dot(k[:, lanes], stacked_heads(q[:, lanes]), ROWS) * 0.125 + bias[...]
        exponent = jnp.exp(scores - jnp.max(scores, axis=0, keepdims=True))
        probs = exponent * (1.0 / jnp.sum(exponent, axis=0, keepdims=True))
        low = probs.astype(BF16)
        p[pair] = low
        copies.append(pltpu.make_async_copy(p.at[pair], p_out.at[pair], sems.at[4 + pair]))
        copies[-1].start()
        attended = dot(v[:, lanes].T, low)
        o[:, lanes] = merged_heads(attended.T).astype(BF16)
    for n in range(2):
        cols = slice(n * 384, (n + 1) * 384)
        mid[:, cols] = (
            tok[0, :, cols].astype(F32)
            + dot(o[...], weights[6 + n].reshape(WIDTH, 384))
            + vec[4:5, cols]
        )
    for copy in copies:
        copy.wait()


def middle_kernel(
    meta, mid, dy, vec, bias_up, mine, other, weights,
    result, act, du_keep, du_send, h2, dmid, da, dattended, small, up_bias_grad,
    up, down, weight_out, sems,
):
    core = meta[0]
    far = 1 - core
    copies = [
        pltpu.make_async_copy(mine.at[:, :, pl.ds(0, 1536)], up.at[core], sems.at[0]),
        pltpu.make_async_copy(other.at[:, :, pl.ds(0, 1536)], up.at[far], sems.at[1]),
        pltpu.make_async_copy(weights.at[pl.ds(6, 2)], weight_out, sems.at[10]),
    ]
    for g in range(4):
        cols = pl.ds(1536 + 384 * g, 384)
        copies.append(
            pltpu.make_async_copy(mine.at[:, :, cols], down.at[core, :, g], sems.at[2 + g])
        )
        copies.append(
            pltpu.make_async_copy(other.at[:, :, cols], down.at[far, :, g], sems.at[6 + g])
        )
    for copy in copies:
        copy.start()
    unit, inverse = normed_of(mid[...])
    h2[...] = (unit * vec[5:6, :] + vec[6:7, :]).astype(BF16)
    for copy in copies[:3]:
        copy.wait()
    low = dy[...]
    outcome = [mid[:, 384 * n : 384 * n + 384] + vec[7:8, 384 * n : 384 * n + 384] for n in range(2)]
    dh2 = None
    for half in range(2):
        cols = slice(half * 1536, (half + 1) * 1536)
        wide = up[half].reshape(WIDTH, 1536)
        u = dot(h2[...], wide) + bias_up[:, cols]
        cube = 0.7978845608028654 * (u + 0.044715 * u * u * u)
        tanh = jnp.tanh(cube)
        low_act = (0.5 * u * (1.0 + tanh)).astype(BF16)
        act[:, cols] = low_act
        slope_half = 0.5 * (1.0 + tanh) + 0.5 * u * (1.0 - tanh * tanh) * 0.7978845608028654 * (
            1.0 + 3.0 * 0.044715 * u * u
        )
        grad_act = None
        if half == 0:
            for copy in copies[3:]:
                copy.wait()
        for n in range(2):
            rows = down[n, half * 8 : half * 8 + 8].reshape(1536, 384)
            outcome[n] = outcome[n] + dot(low_act, rows)
            term = dot(low[:, 384 * n : 384 * n + 384], rows, ROWS)
            grad_act = term if grad_act is None else grad_act + term
        du = (grad_act * slope_half).astype(BF16)
        up_bias_grad[:, cols] = jnp.sum(du.astype(F32), axis=0, keepdims=True)

        @pl.when(core == half)
        def _():
            du_keep[...] = du

        @pl.when(core != half)
        def _():
            du_send[...] = du

        term = dot(du, wide, ROWS)
        dh2 = term if dh2 is None else dh2 + term
    for n in range(2):
        result[:, 384 * n : 384 * n + 384] = outcome[n].astype(BF16)
    upstream = low.astype(F32)
    dm = upstream + norm_backward(dh2, unit, inverse, vec[5:6, :])
    dmid[...] = dm
    branch = dm.astype(BF16)
    da[...] = branch
    small[0:1, :] = jnp.sum(branch.astype(F32), axis=0, keepdims=True)
    small[1:2, :] = jnp.sum(dh2 * unit, axis=0, keepdims=True)
    small[2:3, :] = jnp.sum(dh2, axis=0, keepdims=True)
    small[3:4, :] = jnp.sum(upstream, axis=0, keepdims=True)
    grad = dot(branch[:, :384], weight_out[0].reshape(WIDTH, 384), ROWS)
    grad = grad + dot(branch[:, 384:], weight_out[1].reshape(WIDTH, 384), ROWS)
    dattended[...] = grad.astype(BF16)


def attention_back_kernel(meta, q, k, v, p, do, dq, keep, send, biases):
    first = meta[0] == 0
    for pair in range(6):
        lanes = slice(pair * 128, (pair + 1) * 128)
        upstream = stacked_heads(do[:, lanes])
        keys = k[:, lanes]
        low = p[pair]
        probs = low.astype(F32)
        dprobs = dot(v[:, lanes], upstream, ROWS)
        inner = jnp.sum(probs * dprobs, axis=0, keepdims=True)
        dscores = (probs * (dprobs - inner)).astype(BF16)
        dk = dot(dscores, stacked_heads(q[:, lanes])) * 0.125
        dv = dot(low, upstream)
        low_dq = (merged_heads(dot(keys.T, dscores).T) * 0.125).astype(BF16)
        dq[:, lanes] = low_dq
        biases[0:1, lanes] = jnp.sum(low_dq.astype(F32), axis=0, keepdims=True)
        biases[1:2, lanes] = jnp.sum(dv, axis=0, keepdims=True)
        keep[:, lanes] = jnp.where(first, dk, dv).astype(BF16)
        send[:, lanes] = jnp.where(first, dv, dk).astype(BF16)


def relative(base, steps):
    return lax.rem(base + steps, 4)


def copies_by_y(meta, rows, out, sems):
    return [
        pltpu.make_async_copy(
            rows.at[relative(meta[10], t) * 4 + y], out.at[y, t], sems.at[4 * y + t]
        )
        for y in range(4)
        for t in range(4)
    ]


def copies_by_z(meta, rows, outs, sems):
    return [
        pltpu.make_async_copy(
            rows.at[relative(meta[10], s) * 4 + relative(meta[9], t)],
            outs[s].at[t],
            sems.at[16 + 4 * s + t],
        )
        for s in range(4)
        for t in range(4)
    ]


def feed_grads_kernel(meta, h2, h2_far, du, du_far, act, act_far, dy, dy_far, earlier, *refs):
    by_y, by_z, (up_grad, down_grad, sems) = refs[0], refs[1:5], refs[5:]
    lhs = jnp.concatenate([h2[...], h2_far[...]]).T
    for n in range(4):
        cols = slice(n * 384, (n + 1) * 384)
        grad = dot(lhs, jnp.concatenate([du[:, cols], du_far[:, cols]])).astype(BF16)
        up_grad[:, :, cols] = grad.reshape(16, 48, 384)
    copies = copies_by_y(meta, up_grad, by_y, sems)
    for copy in copies:
        copy.start()
    rhs = jnp.concatenate([dy[...], dy_far[...]])
    for n in range(4):
        cols = slice(n * 768, (n + 1) * 768)
        lhs = jnp.concatenate([act[:, cols], act_far[:, cols]]).T
        down_grad[4 * n : 4 * n + 4] = dot(lhs, rhs).astype(BF16).reshape(4, 192, 384)
    more = copies_by_z(meta, down_grad, by_z, sems)
    for copy in more:
        copy.start()
    for copy in copies + more:
        copy.wait()


def summed(pieces, index):
    total = pieces[0][index].astype(F32)
    for piece in pieces[1:]:
        total = total + piece[index].astype(F32)
    return total


def fold_kernel(meta, up, down0, down1, down2, down3, first, second0, second1, second2, second3, *outs):
    down, second = (down0, down1, down2, down3), (second0, second1, second2, second3)
    for s in range(4):
        sources = range(4)
        outs[s][:, 0:1536] = sum(up[n, s].astype(F32) for n in sources).astype(BF16)
        outs[s][:, 1536:2432] = sum(first[n, s].astype(F32) for n in sources).astype(BF16)
        y = relative(meta[9], s)
        outs[4][y, 0:192, :] = summed(down, s).astype(BF16)
        outs[4][y, 192:288, :] = summed(second, s).astype(BF16)


def second_fold_kernel(w0, w1, w2, w3, tall, out, wide_sum, tall_sum):
    wide_sum[...] = summed((w0, w1, w2, w3), ...)
    tall_sum[...] = sum(tall[n].astype(F32) for n in range(4))
    for place in range(4):
        half, index = place // 2, ring_index(place)
        rows = slice(24 * half, 24 * half + 24)
        out[index, :, 0:2304] = wide_sum[rows, 0:2304].astype(BF16)
        out[index, :, 4608:4736] = wide_sum[rows, 2304:2432].astype(BF16)
        for n in range(2):
            start = 192 + 48 * n + 24 * half
            out[index, :, 2304 + 384 * n : 2688 + 384 * n] = tall_sum[start : start + 24, :].astype(BF16)
        for n in range(4):
            start = 96 * half + 24 * n
            out[index, :, 3072 + 384 * n : 3456 + 384 * n] = tall_sum[start : start + 24, :].astype(BF16)


def third_fold_kernel(meta, parts, keep_wide, send_wide, keep_down, send_down):
    total = sum(parts[n].astype(F32) for n in range(4))

    def part(which):
        down = total[:, 3072 + 768 * which : 3840 + 768 * which]
        return (
            jnp.concatenate([total[12 * which : 12 * which + 12, 0:3072], total[12 * which : 12 * which + 12, 4608:4736]], axis=1),
            jnp.concatenate([down[:, :384], down[:, 384:]]),
        )

    for core in range(2):

        @pl.when(meta[0] == core)
        def _():
            keep_wide[...], keep_down[...] = part(core)
            wide, down = part(1 - core)
            send_wide[...] = wide.astype(BF16)
            send_down[...] = down.astype(BF16)


def finish_kernel(meta, keep_wide, got_wide, keep_down, got_down, up, in_grad, out_grad, down, small):
    small[...] = keep_wide[:, 3072:3200] + got_wide[:, 3072:3200].astype(F32)
    for core in range(2):

        @pl.when(meta[0] == core)
        def _():
            wide = [keep_wide[...], got_wide[...].astype(F32)]
            tall = [keep_down[...], got_down[...].astype(F32)]
            if core == 1:
                wide, tall = wide[::-1], tall[::-1]
            up[:, 0:1536] = wide[0][:, 0:1536]
            up[:, 1536:3072] = wide[1][:, 0:1536]
            in_grad[:, 0:1536] = wide[0][:, 1536:3072]
            in_grad[:, 1536:2304] = wide[1][:, 1536:2304]
            out_grad[...] = wide[1][:, 2304:3072]
            down[:, 0:384] = tall[0]
            down[:, 384:768] = tall[1]


def in_grads_kernel(
    meta, h1, total, o, o_far, da, da_far, dq, dq_far, columns, *refs
):
    by_y, by_z, (grads_y, grads_z, sems) = refs[-8], refs[-7:-3], refs[-3:]
    first = meta[0] == 0
    grads_y[:, :, 768:896] = columns[...]
    lhs = h1[...].T
    lhs_own = jnp.where(
        first,
        jnp.concatenate([h1[0:TOK, :], h1[4 * TOK : 5 * TOK, :]]).astype(F32),
        jnp.concatenate([o[...], o_far[...]]).astype(F32),
    ).astype(BF16).T
    rhs_own = jnp.where(
        first,
        jnp.concatenate([dq[...], dq_far[...]]).astype(F32),
        jnp.concatenate([da[...], da_far[...]]).astype(F32),
    ).astype(BF16)
    for b in range(2):
        cols = slice(b * 384, (b + 1) * 384)
        grad = dot(lhs, total[:, cols])
        grad_own = dot(lhs_own, rhs_own[:, cols])
        low = jnp.where(first, grad, grad_own).astype(BF16)
        grads_z[:, 48 * b : 48 * b + 48, :] = low.reshape(16, 48, 384)
        low = jnp.where(first, grad_own, grad).astype(BF16)
        grads_y[:, :, cols] = low.reshape(16, 48, 384)
    copies = copies_by_y(meta, grads_y, by_y, sems) + copies_by_z(meta, grads_z, by_z, sems)
    for copy in copies:
        copy.start()
    for copy in copies:
        copy.wait()


def in_back_kernel(
    meta, keep, got, dq, small, tok, weights, total, ring, send, columns, sums, weight, weight_query, sems
):
    copies = [
        pltpu.make_async_copy(weights.at[pl.ds(0, 2)], weight_query, sems.at[0]),
        pltpu.make_async_copy(weights.at[pl.ds(2 + 2 * meta[0], 2)], weight, sems.at[1]),
    ]
    for copy in copies:
        copy.start()
    sums[...] = jnp.zeros_like(sums)
    sums[2:12, :] = small[...]
    for copy in copies:
        copy.wait()
    for j in range(8):
        there = (j + 4) % 8
        rows = (
            keep[j * TOK : (j + 1) * TOK, :].astype(F32)
            + got[there * TOK : (there + 1) * TOK, :].astype(F32)
        ).astype(BF16)
        total[j * TOK : (j + 1) * TOK, :] = rows
        grad = dot(rows[:, :384], weight[0].reshape(WIDTH, 384), ROWS)
        grad = grad + dot(rows[:, 384:], weight[1].reshape(WIDTH, 384), ROWS)
        if j == 0:
            grad = grad + dot(dq[:, :384], weight_query[0].reshape(WIDTH, 384), ROWS)
            grad = grad + dot(dq[:, 384:], weight_query[1].reshape(WIDTH, 384), ROWS)
        unit, _ = normed_of(tok[j].astype(F32))
        gain = jnp.sum(grad * unit, axis=0, keepdims=True)
        offset = jnp.sum(grad, axis=0, keepdims=True)
        sums[0:1, :] = gain if j == 0 else sums[0:1, :] + gain
        sums[1:2, :] = offset if j == 0 else sums[1:2, :] + offset
        if j < 4:
            ring[j] = grad
        else:
            send[j - 4] = grad.astype(BF16)
    columns[...] = sums[...].T.astype(BF16).reshape(16, 48, 128)


def pass_kernel(value, *others):
    pass


def after(value, *earlier):
    return pl.pallas_call(
        pass_kernel,
        out_shape=jax.ShapeDtypeStruct(value.shape, value.dtype),
        in_specs=[ANYWHERE] * (1 + len(earlier)),
        out_specs=ANYWHERE,
        input_output_aliases={0: 0},
    )(value, *earlier)


def shifted(value, axis, steps):
    return lax.ppermute(value, axis, [(i, (i + steps) % 4) for i in range(4)])


def along(value, axis):
    return jnp.stack([value] + [shifted(value, axis, steps) for steps in (1, 2, 3)])


def quad_small(core, xh, vectors, up_bias):
    own = jnp.concatenate(list(vectors) + [jnp.zeros((32,), BF16), up_bias, jnp.zeros((1360,), BF16)])
    own = own.reshape(12, 128)
    pair = ordered(core, own, core_swap(own), 0)
    return ordered(xh, pair, mirror(pair), 0)


def gather_weights(core, xh, place, pieces, small):
    in_weight, out_weight, up_weight, down_weight = pieces
    first = jnp.concatenate([in_weight, out_weight], axis=1)

    def part(which):
        return jnp.concatenate([half_of(first, which, 1), half_of(up_weight, which, 1)], axis=1)

    rows = ordered(core, part(core), core_swap(part(1 - core)), 0)

    def block(which):
        return lax.dynamic_slice_in_dim(rows[:, :1536], which * 384, 384, 1)

    got = mirror(jnp.concatenate([block(3 - place), rows[:, 1536:]], axis=1))
    chunk = ordered(xh, block(place), got[:, :384], 0)
    rest = ordered(xh, rows[:, 1536:], got[:, 384:], 0)
    down = ordered(core, half_of(down_weight, core, 1), core_swap(half_of(down_weight, 1 - core, 1)), 0)
    down = ordered(xh, down, mirror(down), 0)
    packed = jnp.concatenate([rest] + [down[48 * k : 48 * k + 48] for k in range(4)], axis=1)
    mine = lax.all_gather(packed, ("z", "y"), axis=0)
    chunk = along(along(jnp.concatenate([chunk, small], axis=1), "y"), "z")
    small = chunk[:, :, :, 384:].reshape(WIDTH, 128)
    chunk = chunk[:, :, :, :384]
    ring = [chunk] + [ring_shift(chunk, steps) for steps in (1, 2, 3)]
    return mine, small, ring + [core_swap(piece) for piece in ring]


def travel_z(parts):
    return [parts[0]] + [shifted(parts[steps], "z", steps) for steps in (1, 2, 3)]


def exchanged(value, axis):
    return lax.all_to_all(value, axis, 0, 0, tiled=True)


def local(
    tokens,
    cotangent,
    first_gain,
    first_offset,
    in_weight,
    query_bias,
    value_bias,
    out_weight,
    out_bias,
    second_gain,
    second_offset,
    up_weight,
    up_bias,
    down_weight,
    down_bias,
):
    core = lax.axis_index("c")
    xh = lax.axis_index("xh")
    xl = lax.axis_index("xl")
    place = 2 * xh + xl
    own_tokens = tokens.reshape(TOK, WIDTH)
    token_ring = gather_tokens(own_tokens)
    upstream = cotangent.reshape(TOK, WIDTH)
    upstream_half = half_of(upstream, core, 1)
    upstream_far = core_swap(half_of(upstream, 1 - core, 1))
    vectors = (
        first_gain,
        first_offset,
        query_bias,
        value_bias,
        out_bias,
        second_gain,
        second_offset,
        down_bias,
    )
    mine, small, pieces = gather_weights(
        core,
        xh,
        place,
        (in_weight, out_weight, up_weight, down_weight),
        quad_small(core, xh, vectors, up_bias),
    )
    group = jnp.stack(token_ring)
    group = jnp.concatenate([group, core_swap(group)])
    mine = after(mine, small, group, *pieces)
    other = core_swap(mine)

    blocks = []
    for apart in (0, 1):
        for steps in range(4):
            there = (place + 4 - steps) % 4
            blocks.append(((there // 2) * 2 + (core + apart) % 2) * 2 + there % 2)
    meta = jnp.stack(
        [core]
        + [(b < blocks[0]).astype(jnp.int32) for b in blocks[1:]]
        + [place, lax.axis_index("y"), lax.axis_index("z")]
    )

    h1, query, key, value, probs, attended, middle, weights, vec, bias_up = call(
        front_kernel,
        [
            ((8 * TOK, WIDTH), BF16),
            ((TOK, WIDTH), BF16),
            ((8 * TOK, WIDTH), BF16),
            ((8 * TOK, WIDTH), BF16),
            ((6, 8 * TOK, 2 * TOK), BF16),
            ((TOK, WIDTH), BF16),
            ((TOK, WIDTH), F32),
            ((8, 16, 48, 384), BF16),
            ((8, WIDTH), F32),
            ((1, HIDDEN), F32),
        ],
        [
            pltpu.VMEM((8 * TOK, WIDTH), BF16),
            pltpu.VMEM((8 * TOK, WIDTH), BF16),
            pltpu.VMEM((8 * TOK, WIDTH), BF16),
            pltpu.VMEM((6, 8 * TOK, 2 * TOK), BF16),
            pltpu.VMEM((8, 16, 48, 384), BF16),
            pltpu.VMEM((8 * TOK, 2 * TOK), F32),
            pltpu.SemaphoreType.DMA((10,)),
        ],
        [IN_SMEM] + [IN_VMEM] * 10,
        (meta, group, small) + tuple(pieces),
        1000,
        1000,
        (0, 2, 3, 4, 7),
    )
    (
        result,
        act,
        du_keep,
        du_send,
        h2,
        grad_middle,
        da,
        grad_attended,
        small_middle,
        grad_up_bias,
    ) = call(
        middle_kernel,
        [
            ((TOK, WIDTH), BF16),
            ((TOK, HIDDEN), BF16),
            ((TOK, HIDDEN // 2), BF16),
            ((TOK, HIDDEN // 2), BF16),
            ((TOK, WIDTH), BF16),
            ((TOK, WIDTH), F32),
            ((TOK, WIDTH), BF16),
            ((TOK, WIDTH), BF16),
            ((4, WIDTH), F32),
            ((1, HIDDEN), F32),
        ],
        [
            pltpu.VMEM((2, 16, 48, 1536), BF16),
            pltpu.VMEM((2, 16, 4, 48, 384), BF16),
            pltpu.VMEM((2, 16, 48, 384), BF16),
            pltpu.SemaphoreType.DMA((11,)),
        ],
        [IN_SMEM] + [IN_VMEM] * 4 + [ANYWHERE] * 3,
        (meta, middle, upstream, vec, bias_up, mine, other, weights),
        1000,
        1000,
    )
    act_far = core_swap(act)
    du_far = core_swap(du_send)
    rows_far = core_swap(jnp.concatenate([h2, attended, da]))
    grad_query, keep, send, small_attention = call(
        attention_back_kernel,
        [
            ((TOK, WIDTH), BF16),
            ((8 * TOK, WIDTH), BF16),
            ((8 * TOK, WIDTH), BF16),
            ((2, WIDTH), F32),
        ],
        [],
        [IN_SMEM] + [IN_VMEM] * 5,
        (meta, query, key, value, probs, grad_attended),
        10_000_000_000,
        20_000_000,
    )
    first_parts = call(
        feed_grads_kernel,
        [((4, 4, 48, 1536), BF16)] + [((4, 192, 384), BF16)] * 4,
        [
            pltpu.VMEM((16, 48, 1536), BF16),
            pltpu.VMEM((16, 192, 384), BF16),
            pltpu.SemaphoreType.DMA((32,)),
        ],
        [IN_SMEM] + [IN_VMEM] * 8 + [ANYWHERE],
        (
            meta,
            h2,
            rows_far[:TOK],
            du_keep,
            du_far,
            act,
            act_far,
            upstream_half,
            upstream_far,
            grad_query,
        ),
        1000,
        1000,
        range(5),
    )
    first_got = [exchanged(first_parts[0], "y")] + travel_z(first_parts[1:])

    small_rows = jnp.concatenate(
        [
            small_attention,
            small_middle,
            grad_up_bias.reshape(64, 4, 12).transpose(1, 0, 2).reshape(4, WIDTH),
        ]
    )
    got = core_swap(send)
    query_far = core_swap(grad_query)
    total, ring, ring_send, columns = call(
        in_back_kernel,
        [
            ((8 * TOK, WIDTH), BF16),
            ((4, TOK, WIDTH), F32),
            ((4, TOK, WIDTH), BF16),
            ((16, 48, 128), BF16),
        ],
        [
            pltpu.VMEM((TOK, WIDTH), F32),
            pltpu.VMEM((2, 16, 48, 384), BF16),
            pltpu.VMEM((2, 16, 48, 384), BF16),
            pltpu.SemaphoreType.DMA((2,)),
        ],
        [IN_SMEM] + [IN_VMEM] * 5 + [ANYWHERE],
        (meta, keep, got, grad_query, small_rows, group, weights),
        10_000_000_000,
        20_000_000,
    )
    ring = ring + core_swap(ring_send).astype(F32)
    leaving = [ring[steps].astype(BF16) for steps in (1, 2, 3)]
    second_parts = call(
        in_grads_kernel,
        [((4, 4, 48, 896), BF16)] + [((4, 96, 384), BF16)] * 4,
        [
            pltpu.VMEM((16, 48, 896), BF16),
            pltpu.VMEM((16, 96, 384), BF16),
            pltpu.SemaphoreType.DMA((32,)),
        ],
        [IN_SMEM] + [IN_VMEM] * 9 + [ANYWHERE] * 6,
        (
            meta,
            h1,
            total,
            attended,
            rows_far[TOK : 2 * TOK],
            da,
            rows_far[2 * TOK :],
            grad_query,
            query_far,
            columns,
            *first_got[2:],
            *leaving,
        ),
        10_000_000_000,
        20_000_000,
        range(5),
    )
    second_got = [exchanged(second_parts[0], "y")] + travel_z(second_parts[1:])
    parts = call(
        fold_kernel,
        [((48, 2432), BF16)] * 4 + [((4, 288, 384), BF16)],
        [],
        [IN_SMEM] + [IN_VMEM] * 10,
        [meta] + first_got + second_got,
        1000,
        1000,
    )
    returned = [ring_shift(leaving[steps - 1], -steps) for steps in (1, 2, 3)]
    grad_normed = ring[0] + sum(value.astype(F32) for value in returned)
    parts = [after(parts[0], *returned)] + list(parts[1:])
    (parts,) = call(
        second_fold_kernel,
        [((4, 24, 4736), BF16)],
        [pltpu.VMEM((48, 2432), F32), pltpu.VMEM((288, 384), F32)],
        [IN_VMEM] * 5,
        travel_z(parts) + [exchanged(parts[4], "y")],
        1000,
        1000,
    )
    keep_wide, send_wide, keep_down, send_down = call(
        third_fold_kernel,
        [((12, 3200), F32), ((12, 3200), BF16), ((48, 384), F32), ((48, 384), BF16)],
        [],
        [IN_SMEM, IN_VMEM],
        [meta, exchanged(parts, RING)],
        1000,
        1000,
    )
    up_own, in_own, out_own, down_own, small_own = call(
        finish_kernel,
        [((12, 3072), F32), ((12, 2304), F32), ((12, 768), F32), ((48, 768), F32), ((12, 128), F32)],
        [],
        [IN_SMEM] + [IN_VMEM] * 4,
        (meta, keep_wide, core_swap(send_wide), keep_down, core_swap(send_down)),
        1000,
        1000,
    )
    unit_one, inverse_one = normed_of(own_tokens.astype(F32))
    grad_input = grad_middle + norm_backward(grad_normed, unit_one, inverse_one, vec[0])

    small_own = small_own[:, :12].T
    up_bias_own = small_own[8:].reshape(48)
    return (
        result.reshape(tokens.shape),
        grad_input.astype(BF16).reshape(tokens.shape),
        small_own[0],
        small_own[1],
        in_own,
        small_own[2],
        small_own[3],
        out_own,
        small_own[4],
        small_own[5],
        small_own[6],
        up_own,
        up_bias_own,
        down_own,
        small_own[7],
    )


def solution(mesh):
    fine = Mesh(mesh.devices.reshape(2, 4, 4, 2, 2), ("xl", "z", "y", "xh", "c"))
    tok = P(SHARD, "xl", None, None)
    vec = P(SHARD)
    mat = P(SHARD, None)
    return jax.shard_map(
        local,
        mesh=fine,
        in_specs=(tok, tok, vec, vec, mat, vec, vec, mat, vec, vec, vec, mat, vec, mat, vec),
        out_specs=(tok, tok, vec, vec, mat, vec, vec, mat, vec, vec, vec, mat, vec, mat, vec),
        check_vma=False,
    )
```

```python
import jax
import jax.numpy as jnp
from jax import lax
from jax.experimental import pallas as pl
from jax.experimental.pallas import tpu as pltpu
from jax.sharding import Mesh, PartitionSpec as P

HEAD_DIM = 64
HEADS = 12
WIDTH = 768
HIDDEN = 3072
TOK = 128
RING = ("xl", "xh")
CHIPS = ("xl", "z", "y", "xh")
SHARD = ("z", "y", "xh", "c")
SWAP = [(0, 1), (1, 0)]
F32 = jnp.float32
BF16 = jnp.bfloat16


def ring_index(place):
    return (place % 2) * 2 + place // 2


def ring_shift(value, steps):
    pairs = [(ring_index(i), ring_index((i + steps) % 4)) for i in range(4)]
    return lax.ppermute(value, RING, pairs)


def mirror(value):
    pairs = [(ring_index(i), ring_index(3 - i)) for i in range(4)]
    return lax.ppermute(value, RING, pairs)


def core_swap(value):
    return lax.ppermute(value, "c", SWAP)


def ordered(flag, own, other, axis):
    return jnp.where(
        flag == 0,
        jnp.concatenate([own, other], axis=axis),
        jnp.concatenate([other, own], axis=axis),
    )


def half_of(value, which, axis):
    size = value.shape[axis] // 2
    return lax.dynamic_slice_in_dim(value, which * size, size, axis)


def normed_of(values):
    average = jnp.mean(values, axis=-1, keepdims=True)
    centered = values - average
    inverse = lax.rsqrt(jnp.mean(centered * centered, axis=-1, keepdims=True) + 1e-05)
    return centered * inverse, inverse


def norm_backward(upstream, normed, inverse, norm_gain):
    scaled = upstream * norm_gain
    return inverse * (
        scaled
        - jnp.mean(scaled, axis=-1, keepdims=True)
        - normed * jnp.mean(scaled * normed, axis=-1, keepdims=True)
    )


def gather_tokens(own):
    return [own] + [ring_shift(own, steps) for steps in (1, 2, 3)]


VMEM_LIMIT = 56 * 1024 * 1024


def dot(a, b, dims=((1,), (0,))):
    return lax.dot_general(a, b, (dims, ((), ())), preferred_element_type=F32)


ROWS = ((1,), (1,))


IN_VMEM = pl.BlockSpec(memory_space=pltpu.VMEM)
IN_SMEM = pl.BlockSpec(memory_space=pltpu.SMEM)
ANYWHERE = pl.BlockSpec(memory_space=pl.ANY)


def call(kernel, outs, scratch, specs, args, flops, size, by_hand=()):
    return pl.pallas_call(
        kernel,
        out_specs=[ANYWHERE if n in by_hand else IN_VMEM for n in range(len(outs))],
        out_shape=[jax.ShapeDtypeStruct(shape, kind) for shape, kind in outs],
        in_specs=specs,
        scratch_shapes=scratch,
        compiler_params=pltpu.CompilerParams(vmem_limit_bytes=VMEM_LIMIT),
        cost_estimate=pl.CostEstimate(flops=flops, bytes_accessed=size, transcendentals=0),
    )(*args)


def stacked_heads(pair):
    lane = lax.broadcasted_iota(jnp.int32, pair.shape, 1)
    zero = jnp.zeros_like(pair)
    return jnp.concatenate([jnp.where(lane < 64, pair, zero), jnp.where(lane < 64, zero, pair)])


def merged_heads(rows):
    lane = lax.broadcasted_iota(jnp.int32, (128, 128), 1)
    return jnp.where(lane < 64, rows[:128], rows[128:])


def unpacked_small(meta, packed):
    row_y, row_z = meta[9], meta[10]
    shard = lax.broadcasted_iota(jnp.int32, (64, WIDTH), 0)
    row = lax.broadcasted_iota(jnp.int32, (64, WIDTH), 1)
    far_z = (row_z - shard // 16) & 3
    far_y = (row_y - shard // 4) & 3
    start = (far_z * 4 + far_y) * 48 + 12 * (shard & 3)

    def picked(offset):
        return dot((row == start + offset).astype(BF16), packed).astype(BF16)

    def spread_out(part, size, first):
        count = 64 * size
        lane = lax.broadcasted_iota(jnp.int32, (128, count), 0)
        col = lax.broadcasted_iota(jnp.int32, (128, count), 1)
        wide = dot(part, (lane == first + lax.rem(col, size)).astype(BF16))
        row = lax.broadcasted_iota(jnp.int32, (64, count), 0)
        behind = lax.broadcasted_iota(jnp.int32, (64, count), 1) - size * row
        inside = jnp.logical_and(behind >= 0, behind < size)
        return jnp.sum(jnp.where(inside, wide, 0.0), axis=0, keepdims=True)

    values = picked(0)
    return [spread_out(values, 12, 12 * k) for k in range(8)], spread_out(picked(1), 48, 0)


def front_kernel(
    meta, tok, small, p0, p1, p2, p3, f0, f1, f2, f3,
    h1_out, q, k_out, v_out, p_out, o, mid, weights_out, vec, bias_up,
    h1, k, v, p, weights, bias, sems,
):
    core, place, row_y, row_z = meta[0], meta[8], meta[9], meta[10]
    for far, pieces in enumerate(((p0, p1, p2, p3), (f0, f1, f2, f3))):
        for s, piece in enumerate(pieces):
            block = lax.rem(core + far, 2) * 4 + lax.rem(place + 4 - s, 4)
            for sz in range(4):
                for sy in range(4):
                    zy = lax.rem(row_z + 4 - sz, 4) * 4 + lax.rem(row_y + 4 - sy, 4)
                    weights[block, zy] = piece[sz, sy]
    copies = [pltpu.make_async_copy(weights, weights_out, sems.at[0])]
    copies[0].start()
    rows, up_row = unpacked_small(meta, small[...])
    for index, row in enumerate(rows):
        vec[index : index + 1, :] = row
    bias_up[...] = up_row
    for j in range(8):
        unit, _ = normed_of(tok[j].astype(F32))
        h1[j * TOK : (j + 1) * TOK, :] = (unit * vec[0:1, :] + vec[1:2, :]).astype(BF16)
    copies.append(pltpu.make_async_copy(h1, h1_out, sems.at[1]))
    copies[-1].start()
    key_row = lax.broadcasted_iota(jnp.int32, (TOK, 2 * TOK), 0)
    query_col = lax.rem(lax.broadcasted_iota(jnp.int32, (TOK, 2 * TOK), 1), TOK)
    bias[0:TOK, :] = jnp.where(key_row <= query_col, 0.0, -1e30)
    for j in range(1, 8):
        shown = meta[j] > 0
        bias[j * TOK : (j + 1) * TOK, :] = jnp.full((TOK, 2 * TOK), jnp.where(shown, 0.0, -1e30), F32)
    for n in range(2):
        cols = slice(n * 384, (n + 1) * 384)
        q[:, cols] = (
            dot(h1[0:TOK, :], weights[n].reshape(WIDTH, 384)) + vec[2:3, cols]
        ).astype(BF16)
        weight_key = weights[2 + n].reshape(WIDTH, 384)
        weight_value = weights[4 + n].reshape(WIDTH, 384)
        for j in range(4):
            rows = slice(j * 256, (j + 1) * 256)
            k[rows, cols] = dot(h1[rows, :], weight_key).astype(BF16)
            v[rows, cols] = (dot(h1[rows, :], weight_value) + vec[3:4, cols]).astype(BF16)
    copies.append(pltpu.make_async_copy(k, k_out, sems.at[2]))
    copies.append(pltpu.make_async_copy(v, v_out, sems.at[3]))
    copies[-2].start()
    copies[-1].start()
    for pair in range(6):
        lanes = slice(pair * 128, (pair + 1) * 128)
        scores = dot(k[:, lanes], stacked_heads(q[:, lanes] * 0.125), ROWS) + bias[...]
        exponent = jnp.exp(scores - jnp.max(scores, axis=0, keepdims=True))
        probs = exponent * (1.0 / jnp.sum(exponent, axis=0, keepdims=True))
        low = probs.astype(BF16)
        p[pair] = low
        copies.append(pltpu.make_async_copy(p.at[pair], p_out.at[pair], sems.at[4 + pair]))
        copies[-1].start()
        attended = dot(v[:, lanes].T, low)
        o[:, lanes] = merged_heads(attended.T).astype(BF16)
    for n in range(2):
        cols = slice(n * 384, (n + 1) * 384)
        mid[:, cols] = (
            tok[0, :, cols].astype(F32)
            + dot(o[...], weights[6 + n].reshape(WIDTH, 384))
            + vec[4:5, cols]
        )
    for copy in copies:
        copy.wait()


def middle_kernel(
    meta, mid, dy, vec, bias_up, mine, other, weights,
    result, act, du_keep, du_send, h2, dmid, da, dattended, small, up_bias_grad,
    up, down, weight_out, sems,
):
    core = meta[0]
    far = 1 - core
    copies = [
        pltpu.make_async_copy(mine.at[:, :, pl.ds(0, 1536)], up.at[core], sems.at[0]),
        pltpu.make_async_copy(other.at[:, :, pl.ds(0, 1536)], up.at[far], sems.at[1]),
        pltpu.make_async_copy(weights.at[pl.ds(6, 2)], weight_out, sems.at[10]),
    ]
    for g in range(4):
        cols = pl.ds(1536 + 384 * g, 384)
        copies.append(
            pltpu.make_async_copy(mine.at[:, :, cols], down.at[core, :, g], sems.at[2 + g])
        )
        copies.append(
            pltpu.make_async_copy(other.at[:, :, cols], down.at[far, :, g], sems.at[6 + g])
        )
    for copy in copies:
        copy.start()
    unit, inverse = normed_of(mid[...])
    h2[...] = (unit * vec[5:6, :] + vec[6:7, :]).astype(BF16)
    for copy in copies[:2]:
        copy.wait()
    low = dy[...]
    outcome = [mid[:, 384 * n : 384 * n + 384] + vec[7:8, 384 * n : 384 * n + 384] for n in range(2)]
    dh2 = None
    for half in range(2):
        cols = slice(half * 1536, (half + 1) * 1536)
        wide = up[half].reshape(WIDTH, 1536)
        u = dot(h2[...], wide) + bias_up[:, cols]
        cube = 0.7978845608028654 * (u + 0.044715 * u * u * u)
        tanh = jnp.tanh(cube)
        low_act = (0.5 * u * (1.0 + tanh)).astype(BF16)
        act[:, cols] = low_act
        slope_half = 0.5 * (1.0 + tanh) + 0.5 * u * (1.0 - tanh * tanh) * 0.7978845608028654 * (
            1.0 + 3.0 * 0.044715 * u * u
        )
        grad_act = None
        if half == 0:
            for copy in copies[2:]:
                copy.wait()
        for n in range(2):
            rows = down[n, half * 8 : half * 8 + 8].reshape(1536, 384)
            outcome[n] = outcome[n] + dot(low_act, rows)
            term = dot(low[:, 384 * n : 384 * n + 384], rows, ROWS)
            grad_act = term if grad_act is None else grad_act + term
        du = (grad_act * slope_half).astype(BF16)
        up_bias_grad[:, cols] = jnp.sum(du.astype(F32), axis=0, keepdims=True)

        @pl.when(core == half)
        def _():
            du_keep[...] = du

        @pl.when(core != half)
        def _():
            du_send[...] = du

        term = dot(du, wide, ROWS)
        dh2 = term if dh2 is None else dh2 + term
    for n in range(2):
        result[:, 384 * n : 384 * n + 384] = outcome[n].astype(BF16)
    upstream = low.astype(F32)
    dm = upstream + norm_backward(dh2, unit, inverse, vec[5:6, :])
    dmid[...] = dm
    branch = dm.astype(BF16)
    da[...] = branch
    small[0:1, :] = jnp.sum(branch.astype(F32), axis=0, keepdims=True)
    small[1:2, :] = jnp.sum(dh2 * unit, axis=0, keepdims=True)
    small[2:3, :] = jnp.sum(dh2, axis=0, keepdims=True)
    small[3:4, :] = jnp.sum(upstream, axis=0, keepdims=True)
    grad = dot(branch[:, :384], weight_out[0].reshape(WIDTH, 384), ROWS)
    grad = grad + dot(branch[:, 384:], weight_out[1].reshape(WIDTH, 384), ROWS)
    dattended[...] = grad.astype(BF16)


def attention_back_kernel(meta, q, k, v, p, do, dq, keep, send, biases):
    first = meta[0] == 0
    for pair in range(6):
        lanes = slice(pair * 128, (pair + 1) * 128)
        upstream = stacked_heads(do[:, lanes])
        keys = k[:, lanes]
        low = p[pair]
        probs = low.astype(F32)
        dprobs = dot(v[:, lanes], upstream, ROWS)
        inner = jnp.sum(probs * dprobs, axis=0, keepdims=True)
        dscores = (probs * (dprobs - inner)).astype(BF16)
        dk = dot(dscores, stacked_heads(q[:, lanes])) * 0.125
        dv = dot(low, upstream)
        low_dq = (merged_heads(dot(keys.T, dscores).T) * 0.125).astype(BF16)
        dq[:, lanes] = low_dq
        biases[0:1, lanes] = jnp.sum(low_dq.astype(F32), axis=0, keepdims=True)
        biases[1:2, lanes] = jnp.sum(dv, axis=0, keepdims=True)
        keep[:, lanes] = jnp.where(first, dk, dv).astype(BF16)
        send[:, lanes] = jnp.where(first, dv, dk).astype(BF16)


def relative(base, steps):
    return lax.rem(base + steps, 4)


def copies_by_y(meta, rows, out, sems):
    return [
        pltpu.make_async_copy(
            rows.at[relative(meta[10], t) * 4 + y], out.at[y, t], sems.at[4 * y + t]
        )
        for y in range(4)
        for t in range(4)
    ]


def copies_by_z(meta, rows, outs, sems):
    return [
        pltpu.make_async_copy(
            rows.at[relative(meta[10], s) * 4 + relative(meta[9], t)],
            outs[s].at[t],
            sems.at[16 + 4 * s + t],
        )
        for s in range(4)
        for t in range(4)
    ]


def feed_grads_kernel(meta, h2, h2_far, du, du_far, act, act_far, dy, dy_far, earlier, *refs):
    by_y, by_z, (up_grad, down_grad, sems) = refs[0], refs[1:5], refs[5:]
    lhs = jnp.concatenate([h2[...], h2_far[...]]).T
    for n in range(4):
        cols = slice(n * 384, (n + 1) * 384)
        grad = dot(lhs, jnp.concatenate([du[:, cols], du_far[:, cols]])).astype(BF16)
        up_grad[:, :, cols] = grad.reshape(16, 48, 384)
    copies = copies_by_y(meta, up_grad, by_y, sems)
    for copy in copies:
        copy.start()
    rhs = jnp.concatenate([dy[...], dy_far[...]])
    for n in range(4):
        cols = slice(n * 768, (n + 1) * 768)
        lhs = jnp.concatenate([act[:, cols], act_far[:, cols]]).T
        down_grad[4 * n : 4 * n + 4] = dot(lhs, rhs).astype(BF16).reshape(4, 192, 384)
    more = copies_by_z(meta, down_grad, by_z, sems)
    for copy in more:
        copy.start()
    for copy in copies + more:
        copy.wait()


def summed(pieces, index):
    total = pieces[0][index].astype(F32)
    for piece in pieces[1:]:
        total = total + piece[index].astype(F32)
    return total


def fold_kernel(meta, up, down0, down1, down2, down3, first, second0, second1, second2, second3, *outs):
    down, second = (down0, down1, down2, down3), (second0, second1, second2, second3)
    for s in range(4):
        sources = range(4)
        outs[s][:, 0:1536] = sum(up[n, s].astype(F32) for n in sources).astype(BF16)
        outs[s][:, 1536:2432] = sum(first[n, s].astype(F32) for n in sources).astype(BF16)
        y = relative(meta[9], s)
        outs[4][y, 0:192, :] = summed(down, s).astype(BF16)
        outs[4][y, 192:288, :] = summed(second, s).astype(BF16)


def second_fold_kernel(w0, w1, w2, w3, tall, out, wide_sum, tall_sum):
    wide_sum[...] = summed((w0, w1, w2, w3), ...)
    tall_sum[...] = sum(tall[n].astype(F32) for n in range(4))
    for place in range(4):
        half, index = place // 2, ring_index(place)
        rows = slice(24 * half, 24 * half + 24)
        out[index, :, 0:2304] = wide_sum[rows, 0:2304].astype(BF16)
        out[index, :, 4608:4736] = wide_sum[rows, 2304:2432].astype(BF16)
        for n in range(2):
            start = 192 + 48 * n + 24 * half
            out[index, :, 2304 + 384 * n : 2688 + 384 * n] = tall_sum[start : start + 24, :].astype(BF16)
        for n in range(4):
            start = 96 * half + 24 * n
            out[index, :, 3072 + 384 * n : 3456 + 384 * n] = tall_sum[start : start + 24, :].astype(BF16)


def third_fold_kernel(meta, parts, keep_wide, send_wide, keep_down, send_down):
    total = sum(parts[n].astype(F32) for n in range(4))

    def part(which):
        down = total[:, 3072 + 768 * which : 3840 + 768 * which]
        return (
            jnp.concatenate([total[12 * which : 12 * which + 12, 0:3072], total[12 * which : 12 * which + 12, 4608:4736]], axis=1),
            jnp.concatenate([down[:, :384], down[:, 384:]]),
        )

    for core in range(2):

        @pl.when(meta[0] == core)
        def _():
            keep_wide[...], keep_down[...] = part(core)
            wide, down = part(1 - core)
            send_wide[...] = wide.astype(BF16)
            send_down[...] = down.astype(BF16)


def finish_kernel(meta, keep_wide, got_wide, keep_down, got_down, up, in_grad, out_grad, down, small):
    small[...] = keep_wide[:, 3072:3200] + got_wide[:, 3072:3200].astype(F32)
    for core in range(2):

        @pl.when(meta[0] == core)
        def _():
            wide = [keep_wide[...], got_wide[...].astype(F32)]
            tall = [keep_down[...], got_down[...].astype(F32)]
            if core == 1:
                wide, tall = wide[::-1], tall[::-1]
            up[:, 0:1536] = wide[0][:, 0:1536]
            up[:, 1536:3072] = wide[1][:, 0:1536]
            in_grad[:, 0:1536] = wide[0][:, 1536:3072]
            in_grad[:, 1536:2304] = wide[1][:, 1536:2304]
            out_grad[...] = wide[1][:, 2304:3072]
            down[:, 0:384] = tall[0]
            down[:, 384:768] = tall[1]


def in_grads_kernel(
    meta, h1, total, o, o_far, da, da_far, dq, dq_far, columns, earlier0, earlier1, earlier2, *refs
):
    by_y, by_z, (grads_y, grads_z, sems) = refs[0], refs[1:5], refs[5:]
    first = meta[0] == 0
    grads_y[:, :, 768:896] = columns[...]
    lhs = h1[...].T
    lhs_own = jnp.where(
        first,
        jnp.concatenate([h1[0:TOK, :], h1[4 * TOK : 5 * TOK, :]]).astype(F32),
        jnp.concatenate([o[...], o_far[...]]).astype(F32),
    ).astype(BF16).T
    rhs_own = jnp.where(
        first,
        jnp.concatenate([dq[...], dq_far[...]]).astype(F32),
        jnp.concatenate([da[...], da_far[...]]).astype(F32),
    ).astype(BF16)
    for b in range(2):
        cols = slice(b * 384, (b + 1) * 384)
        grad = dot(lhs, total[:, cols])
        grad_own = dot(lhs_own, rhs_own[:, cols])
        low = jnp.where(first, grad, grad_own).astype(BF16)
        grads_z[:, 48 * b : 48 * b + 48, :] = low.reshape(16, 48, 384)
        low = jnp.where(first, grad_own, grad).astype(BF16)
        grads_y[:, :, cols] = low.reshape(16, 48, 384)
    copies = copies_by_y(meta, grads_y, by_y, sems) + copies_by_z(meta, grads_z, by_z, sems)
    for copy in copies:
        copy.start()
    for copy in copies:
        copy.wait()


def in_back_kernel(
    meta, keep, got, dq, small, tok, weights, total, ring, send, columns, sums, weight, weight_query, sems
):
    copies = [
        pltpu.make_async_copy(weights.at[pl.ds(0, 2)], weight_query, sems.at[0]),
        pltpu.make_async_copy(weights.at[pl.ds(2 + 2 * meta[0], 2)], weight, sems.at[1]),
    ]
    for copy in copies:
        copy.start()
    sums[...] = jnp.zeros_like(sums)
    sums[2:12, :] = small[...]
    for copy in copies:
        copy.wait()
    for j in range(8):
        there = (j + 4) % 8
        rows = (
            keep[j * TOK : (j + 1) * TOK, :].astype(F32)
            + got[there * TOK : (there + 1) * TOK, :].astype(F32)
        ).astype(BF16)
        total[j * TOK : (j + 1) * TOK, :] = rows
        grad = dot(rows[:, :384], weight[0].reshape(WIDTH, 384), ROWS)
        grad = grad + dot(rows[:, 384:], weight[1].reshape(WIDTH, 384), ROWS)
        if j == 0:
            grad = grad + dot(dq[:, :384], weight_query[0].reshape(WIDTH, 384), ROWS)
            grad = grad + dot(dq[:, 384:], weight_query[1].reshape(WIDTH, 384), ROWS)
        unit, _ = normed_of(tok[j].astype(F32))
        gain = jnp.sum(grad * unit, axis=0, keepdims=True)
        offset = jnp.sum(grad, axis=0, keepdims=True)
        sums[0:1, :] = gain if j == 0 else sums[0:1, :] + gain
        sums[1:2, :] = offset if j == 0 else sums[1:2, :] + offset
        if j < 4:
            ring[j] = grad
        else:
            send[j - 4] = grad.astype(BF16)
    columns[...] = sums[...].T.astype(BF16).reshape(16, 48, 128)


def pass_kernel(value, *others):
    pass


def after(value, *earlier):
    return pl.pallas_call(
        pass_kernel,
        out_shape=jax.ShapeDtypeStruct(value.shape, value.dtype),
        in_specs=[ANYWHERE] * (1 + len(earlier)),
        out_specs=ANYWHERE,
        input_output_aliases={0: 0},
    )(value, *earlier)


def shifted(value, axis, steps):
    return lax.ppermute(value, axis, [(i, (i + steps) % 4) for i in range(4)])


def along(value, axis):
    return jnp.stack([value] + [shifted(value, axis, steps) for steps in (1, 2, 3)])


def quad_small(core, xh, vectors, up_bias):
    own = jnp.concatenate(list(vectors) + [jnp.zeros((32,), BF16), up_bias, jnp.zeros((1360,), BF16)])
    own = own.reshape(12, 128)
    pair = ordered(core, own, core_swap(own), 0)
    return ordered(xh, pair, mirror(pair), 0)


def gather_weights(core, xh, place, pieces, small):
    in_weight, out_weight, up_weight, down_weight = pieces
    first = jnp.concatenate([in_weight, out_weight], axis=1)

    def part(which):
        return jnp.concatenate([half_of(first, which, 1), half_of(up_weight, which, 1)], axis=1)

    rows = ordered(core, part(core), core_swap(part(1 - core)), 0)

    def block(which):
        return lax.dynamic_slice_in_dim(rows[:, :1536], which * 384, 384, 1)

    got = mirror(jnp.concatenate([block(3 - place), rows[:, 1536:]], axis=1))
    chunk = ordered(xh, block(place), got[:, :384], 0)
    rest = ordered(xh, rows[:, 1536:], got[:, 384:], 0)
    down = ordered(core, half_of(down_weight, core, 1), core_swap(half_of(down_weight, 1 - core, 1)), 0)
    down = ordered(xh, down, mirror(down), 0)
    packed = jnp.concatenate([rest] + [down[48 * k : 48 * k + 48] for k in range(4)], axis=1)
    mine = lax.all_gather(packed, ("z", "y"), axis=0)
    chunk = along(along(jnp.concatenate([chunk, small], axis=1), "y"), "z")
    small = chunk[:, :, :, 384:].reshape(WIDTH, 128)
    chunk = chunk[:, :, :, :384]
    ring = [chunk] + [ring_shift(chunk, steps) for steps in (1, 2, 3)]
    return mine, small, ring + [core_swap(piece) for piece in ring]


def travel_z(parts):
    return [parts[0]] + [shifted(parts[steps], "z", steps) for steps in (1, 2, 3)]


def exchanged(value, axis):
    return lax.all_to_all(value, axis, 0, 0, tiled=True)


def local(
    tokens,
    cotangent,
    first_gain,
    first_offset,
    in_weight,
    query_bias,
    value_bias,
    out_weight,
    out_bias,
    second_gain,
    second_offset,
    up_weight,
    up_bias,
    down_weight,
    down_bias,
):
    core = lax.axis_index("c")
    xh = lax.axis_index("xh")
    xl = lax.axis_index("xl")
    place = 2 * xh + xl
    own_tokens = tokens.reshape(TOK, WIDTH)
    token_ring = gather_tokens(own_tokens)
    upstream = cotangent.reshape(TOK, WIDTH)
    upstream_half = half_of(upstream, core, 1)
    upstream_far = core_swap(half_of(upstream, 1 - core, 1))
    vectors = (
        first_gain,
        first_offset,
        query_bias,
        value_bias,
        out_bias,
        second_gain,
        second_offset,
        down_bias,
    )
    mine, small, pieces = gather_weights(
        core,
        xh,
        place,
        (in_weight, out_weight, up_weight, down_weight),
        quad_small(core, xh, vectors, up_bias),
    )
    group = jnp.stack(token_ring)
    group = jnp.concatenate([group, core_swap(group)])
    mine = after(mine, small, group, *pieces)
    other = core_swap(mine)

    blocks = []
    for apart in (0, 1):
        for steps in range(4):
            there = (place + 4 - steps) % 4
            blocks.append(((there // 2) * 2 + (core + apart) % 2) * 2 + there % 2)
    meta = jnp.stack(
        [core]
        + [(b < blocks[0]).astype(jnp.int32) for b in blocks[1:]]
        + [place, lax.axis_index("y"), lax.axis_index("z")]
    )

    h1, query, key, value, probs, attended, middle, weights, vec, bias_up = call(
        front_kernel,
        [
            ((8 * TOK, WIDTH), BF16),
            ((TOK, WIDTH), BF16),
            ((8 * TOK, WIDTH), BF16),
            ((8 * TOK, WIDTH), BF16),
            ((6, 8 * TOK, 2 * TOK), BF16),
            ((TOK, WIDTH), BF16),
            ((TOK, WIDTH), F32),
            ((8, 16, 48, 384), BF16),
            ((8, WIDTH), F32),
            ((1, HIDDEN), F32),
        ],
        [
            pltpu.VMEM((8 * TOK, WIDTH), BF16),
            pltpu.VMEM((8 * TOK, WIDTH), BF16),
            pltpu.VMEM((8 * TOK, WIDTH), BF16),
            pltpu.VMEM((6, 8 * TOK, 2 * TOK), BF16),
            pltpu.VMEM((8, 16, 48, 384), BF16),
            pltpu.VMEM((8 * TOK, 2 * TOK), F32),
            pltpu.SemaphoreType.DMA((10,)),
        ],
        [IN_SMEM] + [IN_VMEM] * 10,
        (meta, group, small) + tuple(pieces),
        1000,
        1000,
        (0, 2, 3, 4, 7),
    )
    (
        result,
        act,
        du_keep,
        du_send,
        h2,
        grad_middle,
        da,
        grad_attended,
        small_middle,
        grad_up_bias,
    ) = call(
        middle_kernel,
        [
            ((TOK, WIDTH), BF16),
            ((TOK, HIDDEN), BF16),
            ((TOK, HIDDEN // 2), BF16),
            ((TOK, HIDDEN // 2), BF16),
            ((TOK, WIDTH), BF16),
            ((TOK, WIDTH), F32),
            ((TOK, WIDTH), BF16),
            ((TOK, WIDTH), BF16),
            ((4, WIDTH), F32),
            ((1, HIDDEN), F32),
        ],
        [
            pltpu.VMEM((2, 16, 48, 1536), BF16),
            pltpu.VMEM((2, 16, 4, 48, 384), BF16),
            pltpu.VMEM((2, 16, 48, 384), BF16),
            pltpu.SemaphoreType.DMA((11,)),
        ],
        [IN_SMEM] + [IN_VMEM] * 4 + [ANYWHERE] * 3,
        (meta, middle, upstream, vec, bias_up, mine, other, weights),
        1000,
        1000,
    )
    act_far = core_swap(act)
    du_far = core_swap(du_send)
    rows_far = core_swap(jnp.concatenate([h2, attended, da]))
    grad_query, keep, send, small_attention = call(
        attention_back_kernel,
        [
            ((TOK, WIDTH), BF16),
            ((8 * TOK, WIDTH), BF16),
            ((8 * TOK, WIDTH), BF16),
            ((2, WIDTH), F32),
        ],
        [],
        [IN_SMEM] + [IN_VMEM] * 5,
        (meta, query, key, value, probs, grad_attended),
        10_000_000_000,
        20_000_000,
    )
    first_parts = call(
        feed_grads_kernel,
        [((4, 4, 48, 1536), BF16)] + [((4, 192, 384), BF16)] * 4,
        [
            pltpu.VMEM((16, 48, 1536), BF16),
            pltpu.VMEM((16, 192, 384), BF16),
            pltpu.SemaphoreType.DMA((32,)),
        ],
        [IN_SMEM] + [IN_VMEM] * 8 + [ANYWHERE],
        (
            meta,
            h2,
            rows_far[:TOK],
            du_keep,
            du_far,
            act,
            act_far,
            upstream_half,
            upstream_far,
            grad_query,
        ),
        1000,
        1000,
        range(5),
    )
    first_got = [exchanged(first_parts[0], "y")] + travel_z(first_parts[1:])

    small_rows = jnp.concatenate(
        [
            small_attention,
            small_middle,
            grad_up_bias.reshape(64, 4, 12).transpose(1, 0, 2).reshape(4, WIDTH),
        ]
    )
    got = core_swap(send)
    query_far = core_swap(grad_query)
    total, ring, ring_send, columns = call(
        in_back_kernel,
        [
            ((8 * TOK, WIDTH), BF16),
            ((4, TOK, WIDTH), F32),
            ((4, TOK, WIDTH), BF16),
            ((16, 48, 128), BF16),
        ],
        [
            pltpu.VMEM((TOK, WIDTH), F32),
            pltpu.VMEM((2, 16, 48, 384), BF16),
            pltpu.VMEM((2, 16, 48, 384), BF16),
            pltpu.SemaphoreType.DMA((2,)),
        ],
        [IN_SMEM] + [IN_VMEM] * 5 + [ANYWHERE],
        (meta, keep, got, grad_query, small_rows, group, weights),
        10_000_000_000,
        20_000_000,
    )
    second_parts = call(
        in_grads_kernel,
        [((4, 4, 48, 896), BF16)] + [((4, 96, 384), BF16)] * 4,
        [
            pltpu.VMEM((16, 48, 896), BF16),
            pltpu.VMEM((16, 96, 384), BF16),
            pltpu.SemaphoreType.DMA((32,)),
        ],
        [IN_SMEM] + [IN_VMEM] * 9 + [ANYWHERE] * 3,
        (
            meta,
            h1,
            total,
            attended,
            rows_far[TOK : 2 * TOK],
            da,
            rows_far[2 * TOK :],
            grad_query,
            query_far,
            columns,
            *first_got[2:],
        ),
        10_000_000_000,
        20_000_000,
        range(5),
    )
    second_got = [exchanged(second_parts[0], "y")] + travel_z(second_parts[1:])
    parts = call(
        fold_kernel,
        [((48, 2432), BF16)] * 4 + [((4, 288, 384), BF16)],
        [],
        [IN_SMEM] + [IN_VMEM] * 10,
        [meta] + first_got + second_got,
        1000,
        1000,
    )
    ring = ring + core_swap(ring_send).astype(F32)
    returned = [ring_shift(ring[steps].astype(BF16), -steps) for steps in (1, 2, 3)]
    grad_normed = ring[0] + sum(value.astype(F32) for value in returned)
    parts = [after(parts[0], *returned)] + list(parts[1:])
    (parts,) = call(
        second_fold_kernel,
        [((4, 24, 4736), BF16)],
        [pltpu.VMEM((48, 2432), F32), pltpu.VMEM((288, 384), F32)],
        [IN_VMEM] * 5,
        travel_z(parts) + [exchanged(parts[4], "y")],
        1000,
        1000,
    )
    keep_wide, send_wide, keep_down, send_down = call(
        third_fold_kernel,
        [((12, 3200), F32), ((12, 3200), BF16), ((48, 384), F32), ((48, 384), BF16)],
        [],
        [IN_SMEM, IN_VMEM],
        [meta, exchanged(parts, RING)],
        1000,
        1000,
    )
    up_own, in_own, out_own, down_own, small_own = call(
        finish_kernel,
        [((12, 3072), F32), ((12, 2304), F32), ((12, 768), F32), ((48, 768), F32), ((12, 128), F32)],
        [],
        [IN_SMEM] + [IN_VMEM] * 4,
        (meta, keep_wide, core_swap(send_wide), keep_down, core_swap(send_down)),
        1000,
        1000,
    )
    unit_one, inverse_one = normed_of(own_tokens.astype(F32))
    grad_input = grad_middle + norm_backward(grad_normed, unit_one, inverse_one, vec[0])

    small_own = small_own[:, :12].T
    up_bias_own = small_own[8:].reshape(48)
    return (
        result.reshape(tokens.shape),
        grad_input.astype(BF16).reshape(tokens.shape),
        small_own[0],
        small_own[1],
        in_own,
        small_own[2],
        small_own[3],
        out_own,
        small_own[4],
        small_own[5],
        small_own[6],
        up_own,
        up_bias_own,
        down_own,
        small_own[7],
    )


def solution(mesh):
    fine = Mesh(mesh.devices.reshape(2, 4, 4, 2, 2), ("xl", "z", "y", "xh", "c"))
    tok = P(SHARD, "xl", None, None)
    vec = P(SHARD)
    mat = P(SHARD, None)
    return jax.shard_map(
        local,
        mesh=fine,
        in_specs=(tok, tok, vec, vec, mat, vec, vec, mat, vec, vec, vec, mat, vec, mat, vec),
        out_specs=(tok, tok, vec, vec, mat, vec, vec, mat, vec, vec, vec, mat, vec, mat, vec),
        check_vma=False,
    )
```
